32 devices in a mesh: parts: 2 (over y), gz: 4 (over x, core), ty: 4 (over z).
Axes of the slice: x: 2, y: 2, z: 4, core: 2. Of those that a mesh axis runs over, the one named last changes fastest.
Arguments:
- sections: bfloat16 [8, 1024, 2048], P(('parts', 'gz'), 'ty'), parts along dimension 0, may hold values from -6 to 6
- boundary: bfloat16 [2048, 2048], P(('parts', 'ty')), parts along dimension 0, may hold values from -5 to 5
- row_shift: int32 [8, 1024], P(('parts', 'gz'), 'ty'), parts along dimension 0, may hold values from -64 to 63
- row_frac: int32 [8, 1024], P(('parts', 'gz'), 'ty'), parts along dimension 0, may hold values from 0 to 255
- col_shift: int32 [8, 2048], P(('parts', 'gz')), parts along dimension 0, may hold values from -64 to 63
- col_frac: int32 [8, 2048], P(('parts', 'gz')), parts along dimension 0, may hold values from 0 to 255
- peak_shift: int32 [2, 8, 8, 16], P(None, ('parts', 'gz'), 'ty'), parts along dimension 1, may hold values from -8 to 8
Outputs:
- rendered: bfloat16 [8, 1024, 2048], P(('parts', 'gz'), 'ty'), parts along dimension 0
- flow: float32 [2, 8, 8, 16], P(None, ('parts', 'gz'), 'ty'), parts along dimension 1
The draws below stay inside these ranges and needn't reach their ends.
There are 2 independent parts, one for each index of `parts`. The reference program is written for one: setup_inputs(seed, part) draws one part's arguments, and reference() takes and returns one part's arrays. A program takes and returns all parts, laid end to end along the dimension named above; each array names one. Nothing has to cross between parts.
All inputs are finite; a program needn't handle non-finite values.
Results may differ from the reference program's by a relative error of at most 0.0049.
Values may be sent and summed in bfloat16 or wider, within the bound.
No kernel may reach another device: no remote copies, remote signals or barrier semaphores. Data moves between devices by JAX's collectives and lax.ppermute only.
A program may use at most 64 MiB of HBM per device.

```python
import jax
import jax.numpy as jnp
from jax import lax

PATCH = 128
NX = 2048
MARGIN = 64
COL_REACH = 64
MAX_PEAK = 8
SMOOTH_PASSES = 2
NZ = 4
NY = 1024
PY = 8
PX = 16


def set_ends(entries, own_key, least, high):
    shape = entries.shape
    place = [jax.random.randint(jax.random.fold_in(own_key, axis), (), 0, shape[axis]) for axis in range(len(shape))]
    entries = entries.at[tuple(place)].set(least)
    longest = shape.index(max(shape))
    place[longest] = (place[longest] + 1) % shape[longest]
    return entries.at[tuple(place)].set(high)


def shard_levels(rng, dims, split, smallest, high):
    gain = 1.0
    for position, blocks in split:
        heights = jax.random.uniform(jax.random.fold_in(jax.random.fold_in(rng, 6), position), (blocks,), jnp.float32, smallest / len(split), high / len(split))
        gain = gain * jnp.repeat(jnp.exp(heights), dims[position] // blocks).reshape((-1,) + (1,) * (len(dims) - 1 - position))
    return gain


def noise(stream_key, extent, deviation, reach, pieces=(), kind=jnp.bfloat16):
    values = jax.random.normal(stream_key, extent, jnp.float32) * deviation
    if len(pieces) > 0:
        values = shard_levels(stream_key, extent, pieces, -0.22, 0.18) * values
    return jnp.clip(values, min=-reach, max=reach).astype(kind)


def setup_inputs(seed: int = 0, part: int = 0) -> dict:
    seeds = jax.random.split(jax.random.key(seed), 8)
    own_keys = jax.random.split(jax.random.fold_in(seeds[7], part), 8)
    return {
        "sections": noise(own_keys[0], (NZ, NY, NX), 1.0, 6.0, ((0, 4), (1, 4))),
        "boundary": noise(own_keys[1], (NY, NX), 0.7, 5.0, ((0, 4),)),
        "row_shift": set_ends(jax.random.randint(own_keys[2], (NZ, NY), -MARGIN, MARGIN), jax.random.fold_in(own_keys[2], 1), -MARGIN, MARGIN - 1).astype(jnp.int32),
        "row_frac": set_ends(jax.random.randint(own_keys[3], (NZ, NY), 0, 256), jax.random.fold_in(own_keys[3], 1), 0, 255).astype(jnp.int32),
        "col_shift": set_ends(jax.random.randint(own_keys[4], (NZ, NX), -COL_REACH, COL_REACH), jax.random.fold_in(own_keys[4], 1), -COL_REACH, COL_REACH - 1).astype(jnp.int32),
        "col_frac": set_ends(jax.random.randint(own_keys[5], (NZ, NX), 0, 256), jax.random.fold_in(own_keys[5], 1), 0, 255).astype(jnp.int32),
        "peak_shift": set_ends(jax.random.randint(own_keys[6], (2, NZ, PY, PX), -MAX_PEAK, MAX_PEAK + 1), jax.random.fold_in(own_keys[6], 1), -MAX_PEAK, MAX_PEAK).astype(jnp.int32),
    }


blur_taps = (0.0625, 0.25, 0.375, 0.25, 0.0625)


def render_section(section, shift_rows, frac_rows, shift_cols, frac_cols):
    sec_height = section.shape[0]
    sec_width = section.shape[1]
    row_ids = jnp.arange(sec_height, dtype=jnp.int32)
    source_row = jnp.clip(row_ids + shift_rows, 0, sec_height - 2).astype(jnp.int32)
    row_weight = (frac_rows.astype(jnp.float32) / 256.0)[:, None]
    upper_rows = jnp.take(section, source_row, axis=0).astype(jnp.float32)
    lower_rows = jnp.take(section, source_row + 1, axis=0).astype(jnp.float32)
    row_mix = ((1.0 - row_weight) * upper_rows + row_weight * lower_rows).astype(jnp.bfloat16)
    col_ids = jnp.arange(sec_width, dtype=jnp.int32)
    source_col = jnp.clip(col_ids + shift_cols, 0, sec_width - 2).astype(jnp.int32)
    col_weight = (frac_cols.astype(jnp.float32) / 256.0)[None, :]
    first_cols = jnp.take(row_mix, source_col, axis=1).astype(jnp.float32)
    second_cols = jnp.take(row_mix, source_col + 1, axis=1).astype(jnp.float32)
    return ((1.0 - col_weight) * first_cols + col_weight * second_cols).astype(jnp.bfloat16)


def to_patches(section):
    return section.reshape(PY, PATCH, PX, PATCH).transpose(0, 2, 1, 3).astype(jnp.float32)


def window_of(current, earlier, peak_row, peak_col):
    cur_patches = to_patches(current)
    old_patches = to_patches(earlier)
    spectrum = jnp.conj(jnp.fft.fft2(cur_patches)) * jnp.fft.fft2(old_patches)
    correlation = jnp.real(jnp.fft.ifft2(spectrum)) / PATCH
    offsets = jnp.arange(3, dtype=jnp.int32) - 1
    patch_ids = jnp.arange(PATCH, dtype=jnp.int32)
    select_row = (((peak_row[..., None] + offsets) % PATCH)[..., None] == patch_ids).astype(correlation.dtype)
    select_col = (((peak_col[..., None] + offsets) % PATCH)[..., None] == patch_ids).astype(correlation.dtype)
    return jnp.einsum("abip,abpq,abjq->abij", select_row, correlation, select_col, precision=lax.Precision.HIGHEST)


def centroid_flow(window, peak_row, peak_col):
    offsets = jnp.arange(3, dtype=jnp.int32).astype(jnp.float32) - 1.0
    weights = jnp.maximum(window, 0.0)
    weight_sum = jnp.maximum(jnp.sum(weights, axis=(-2, -1)), 1.0)
    flow_row = peak_row.astype(jnp.float32) + jnp.sum(weights * offsets[:, None], axis=(-2, -1)) / weight_sum
    flow_col = peak_col.astype(jnp.float32) + jnp.sum(weights * offsets[None, :], axis=(-2, -1)) / weight_sum
    return flow_row, flow_col


def blur_rows(padded, n_rows):
    result = blur_taps[0] * padded[..., 0:n_rows, :]
    for offset in range(1, 5):
        result = result + blur_taps[offset] * padded[..., offset:offset + n_rows, :]
    return result


def blur_cols(grid_values):
    n_cols = grid_values.shape[-1]
    padded = jnp.pad(grid_values, [(0, 0)] * (grid_values.ndim - 1) + [(2, 2)])
    result = blur_taps[0] * padded[..., 0:n_cols]
    for offset in range(1, 5):
        result = result + blur_taps[offset] * padded[..., offset:offset + n_cols]
    return result


def reference(sections, boundary, row_shift, row_frac, col_shift, col_frac, peak_shift):
    rendered = jnp.stack([render_section(sections[section_id], row_shift[section_id], row_frac[section_id], col_shift[section_id], col_frac[section_id]) for section_id in range(NZ)])
    previous = jnp.concatenate([boundary[None], rendered[:-1]], axis=0)
    rows_out = []
    cols_out = []
    for section_id in range(NZ):
        window = window_of(rendered[section_id], previous[section_id], peak_shift[0, section_id], peak_shift[1, section_id])
        flow_row, flow_col = centroid_flow(window, peak_shift[0, section_id], peak_shift[1, section_id])
        rows_out.append(flow_row)
        cols_out.append(flow_col)
    flow_now = jnp.stack([jnp.stack(rows_out), jnp.stack(cols_out)])
    unit_field = jnp.ones_like(flow_now[0:1])
    padding = [(0, 0), (0, 0), (2, 2), (0, 0)]
    for repeat in range(SMOOTH_PASSES):
        stacked = jnp.concatenate([flow_now, unit_field], axis=0)
        blurred = blur_cols(blur_rows(jnp.pad(stacked, padding), PY))
        flow_now = blurred[0:2] / blurred[2:3]
    return rendered, flow_now
```

```python
import functools

import jax
import jax.numpy as jnp
import numpy as np
from jax import lax
from jax.experimental import pallas as pl
from jax.experimental.pallas import tpu as pltpu
from jax.sharding import PartitionSpec as P

PATCH = 128
MARGIN = 64
SMOOTH_PASSES = 2
BLOCK = 256
LANES = 128
TAPS = (0.0625, 0.25, 0.375, 0.25, 0.0625)
FAR = 1 << 20
VMEM_LIMIT = 40 * 1024 * 1024

f32 = jnp.float32
bf16 = jnp.bfloat16


def swap_pairs(n, d, second):
    pairs = []
    for i in range(n):
        if (i // d) % 2 == int(second):
            j = i + d
            if j >= n:
                if not second or n % (2 * d):
                    continue
                j -= n
            pairs.append((i, j))
    return frozenset(frozenset(p) for p in pairs)


def both_ways(pairs):
    return sorted([tuple(sorted(p)) for p in pairs] + [tuple(sorted(p))[::-1] for p in pairs])


def halo_pairs(n_gz, n_ty, second):
    table = []
    for z in range(n_gz):
        for t in range(n_ty):
            partner = t + 1 if (t % 2 == 0) != second else t - 1
            if 0 <= partner < n_ty:
                table.append((z * n_ty + t, z * n_ty + partner))
            elif (z ^ 1) < n_gz:
                table.append((z * n_ty + t, (z ^ 1) * n_ty + t))
    return table


def hat(coord, position):
    return jnp.maximum(1.0 - jnp.abs(coord - position), 0.0)


def source_positions(ids, shift, frac, limit, base):
    source = jnp.clip(ids + shift, 0, limit) - base
    return source.astype(f32) + frac.astype(f32) * (1.0 / 256.0)


def columns_from(mix, table_ref, out_ref, rows):
    n_cols = mix.shape[1]
    for j in range(n_cols // BLOCK):
        first, last = j * BLOCK - LANES, (j + 1) * BLOCK + LANES
        low, high = max(first, 0), min(last, n_cols)
        out_ref[rows, j * BLOCK : (j + 1) * BLOCK] = jnp.dot(
            mix[:, low:high], table_ref[j, low - first : high - first, :], preferred_element_type=f32
        ).astype(bf16)


def contract_rows(table, source):
    return lax.dot_general(
        table, source, (((0,), (0,)), ((), ())), preferred_element_type=f32
    ).astype(bf16)


def middle_kernel(all_rows, place, sec, row_shift, row_frac, col_shift, col_frac, mid_ref, table_ref):
    n_rows, n_cols = sec.shape
    tile = place[1]
    base = tile * n_rows
    ids = lax.broadcasted_iota(jnp.int32, (1, n_rows), 1) + base
    pos = source_positions(ids, row_shift[...], row_frac[...], all_rows - 2, base)
    pos = pos[:, MARGIN : n_rows - MARGIN]
    coord = lax.broadcasted_iota(jnp.int32, (n_rows, pos.shape[1]), 0).astype(f32)
    mix = contract_rows(hat(coord, pos).astype(bf16), sec[...])
    window = BLOCK + 2 * LANES
    reach = window - LANES
    coord = lax.broadcasted_iota(jnp.int32, (reach, BLOCK), 0).astype(f32)
    ids = lax.broadcasted_iota(jnp.int32, (1, BLOCK), 1)
    edge = jnp.zeros((LANES // 2, BLOCK), bf16)
    for j in range(n_cols // BLOCK):
        cols = slice(j * BLOCK, (j + 1) * BLOCK)
        pos = source_positions(
            ids + j * BLOCK, col_shift[:, cols], col_frac[:, cols], n_cols - 2, j * BLOCK - LANES // 2
        )
        table_ref[j, 0 : LANES // 2, :] = edge
        table_ref[j, LANES // 2 : LANES // 2 + reach, :] = hat(coord, pos).astype(bf16)
        table_ref[j, LANES // 2 + reach :, :] = edge
    columns_from(mix, table_ref, mid_ref, slice(None))


def edges_kernel(all_rows, place, first, second, sec, row_shift, row_frac, table_ref, edge_ref):
    n_rows = sec.shape[0]
    tile = place[1]
    base = tile * n_rows
    even = tile % 2 == 0
    half = n_rows // 2
    ids = lax.broadcasted_iota(jnp.int32, (1, n_rows), 1) + base
    pos = source_positions(ids, row_shift[...], row_frac[...], all_rows - 2, base)
    slot = lax.broadcasted_iota(jnp.int32, (MARGIN, MARGIN), 0)
    own = lax.broadcasted_iota(jnp.int32, (half, MARGIN), 0)
    mixes = []
    for top in (True, False):
        near = slot - MARGIN if top else slot + n_rows
        in_first = even != top
        coord = jnp.concatenate(
            [
                jnp.where(in_first, near, FAR),
                jnp.where(in_first, FAR, near),
                own if top else own + half,
            ],
            axis=0,
        ).astype(f32)
        here = pos[:, :MARGIN] if top else pos[:, n_rows - MARGIN :]
        stack = jnp.concatenate(
            [first[...], second[...], sec[0:half, :] if top else sec[half:, :]], axis=0
        )
        mixes.append(contract_rows(hat(coord, here).astype(bf16), stack))
    columns_from(jnp.concatenate(mixes, axis=0), table_ref, edge_ref, slice(None))


def window_kernel(place, peaks, mid, edge, old_mid, old_edge, boundary, smooth, out_ref, ext, acc, peak, whole, sem):
    n_mid, n_cols = mid.shape
    n_rows = n_mid + edge.shape[0]
    patch_rows, patch_cols = n_rows // PATCH, n_cols // PATCH
    n_patches = patch_rows * patch_cols
    pad = 16

    def parts_of(i):
        start, stop = i * PATCH, (i + 1) * PATCH
        pieces = []
        for is_edge, low, high, shift in (
            (True, 0, MARGIN, 0),
            (False, MARGIN, n_rows - MARGIN, MARGIN),
            (True, n_rows - MARGIN, n_rows, n_mid),
        ):
            a, b = max(start, low), min(stop, high)
            if a < b:
                pieces.append((is_edge, a - shift, b - a))
        return pieces

    def fill(p, block):
        ext[p, pad : pad + PATCH, :] = block
        ext[p, 0:pad, :] = block[PATCH - pad :, :]
        ext[p, pad + PATCH :, :] = block[:pad, :]

    def block_of(i, lanes, mid_source, edge_source):
        return jnp.concatenate(
            [(edge_source if is_edge else mid_source)[a : a + n, lanes] for is_edge, a, n in parts_of(i)], axis=0
        ).astype(f32)

    @pl.when(place[0] == 0)
    def _():
        copy = pltpu.make_async_copy(boundary, whole, sem)
        copy.start()
        copy.wait()
        for i in range(patch_rows):

            @pl.loop(0, patch_cols)
            def _(j):
                lanes = pl.ds(pl.multiple_of(j * PATCH, PATCH), PATCH)
                fill(i * patch_cols + j, whole[i * PATCH : (i + 1) * PATCH, lanes].astype(f32))

    @pl.when(place[0] != 0)
    def _():
        for i in range(patch_rows):

            @pl.loop(0, patch_cols)
            def _(j):
                lanes = pl.ds(pl.multiple_of(j * PATCH, PATCH), PATCH)
                fill(i * patch_cols + j, block_of(i, lanes, old_mid, old_edge))

    for i in range(patch_rows):

        @pl.loop(0, patch_cols)
        def _(j):
            p = i * patch_cols + j
            lanes = pl.ds(pl.multiple_of(j * PATCH, PATCH), PATCH)
            peak_row, peak_col = peaks[0, p], peaks[1, p]
            peak[0, pl.ds(p, 1), :] = jnp.full((1, LANES), peak_row, jnp.int32).astype(f32)
            peak[1, pl.ds(p, 1), :] = jnp.full((1, LANES), peak_col, jnp.int32).astype(f32)
            sums = [None] * 9
            current = block_of(i, lanes, mid, edge)
            for r in range(PATCH // 8):
                rows = current[8 * r : 8 * r + 8, :]
                turned = [pltpu.roll(rows, (peak_col + dx) % PATCH, 1) for dx in (-1, 0, 1)]
                for dy in (-1, 0, 1):
                    old = ext[p, pl.ds(peak_row + (pad + dy + 8 * r), 8), :]
                    for dx in range(3):
                        k = (dy + 1) * 3 + dx
                        term = turned[dx] * old
                        sums[k] = term if sums[k] is None else sums[k] + term
            for k in range(9):
                acc[pl.ds(pl.multiple_of((k * n_patches + p) * 8, 8), 8), :] = sums[k]

    total = acc[pl.ds(0, 9 * n_patches, stride=8), :]
    for s in range(1, 8):
        total = total + acc[pl.ds(s, 9 * n_patches, stride=8), :]
    weights = jnp.maximum(jnp.sum(total, axis=1, keepdims=True) * (1.0 / PATCH), 0.0)
    w = [weights[k * n_patches : (k + 1) * n_patches] for k in range(9)]
    scale = 1.0 / jnp.maximum(sum(w), 1.0)
    moves = (
        (w[6] + w[7] + w[8] - w[0] - w[1] - w[2]) * scale,
        (w[2] + w[5] + w[8] - w[0] - w[3] - w[6]) * scale,
    )
    out_ref[...] = jnp.zeros_like(out_ref)
    for c in range(2):
        flow = moves[c] + peak[c]
        for i in range(patch_rows):
            row = flow[i * patch_cols : (i + 1) * patch_cols, :] * smooth[...]
            out_ref[c * patch_rows + i : c * patch_rows + i + 1, :] = jnp.sum(row, axis=0, keepdims=True)


def partner_of(tile, n, d, second):
    up = (tile // d) % 2 == int(second)
    return (tile + jnp.where(up, d, -d) + n) % n


def rows_kernel(n_ty, swaps, place, *refs):
    blocks, out_ref = refs[:-1], refs[-1]
    patch_rows, patch_cols = out_ref.shape[2], out_ref.shape[3]
    all_rows = n_ty * patch_rows
    tile = place[1]
    depth = 8 * len(blocks)
    at = lax.broadcasted_iota(jnp.int32, (8, depth), 0)
    slot = lax.broadcasted_iota(jnp.int32, (8, depth), 1)
    holder = jnp.full((8, depth), tile, jnp.int32)
    for k, (d, second) in enumerate(swaps):
        holder = jnp.where((slot >> 3) == k + 1, partner_of(tile, n_ty, d, second), holder)
    slot = slot & 7
    c_out = (at >= patch_rows).astype(jnp.int32)
    c_in = (slot >= patch_rows).astype(jnp.int32)
    row = tile * patch_rows + at - c_out * patch_rows
    source = holder * patch_rows + slot - c_in * patch_rows

    def inside(r):
        return (r >= 0) & (r < all_rows)

    def tap(delta):
        size = jnp.abs(delta)
        return jnp.where(
            size == 0, TAPS[2], jnp.where(size == 1, TAPS[1], jnp.where(size == 2, TAPS[0], 0.0))
        )

    def norm(r):
        return sum(jnp.where(inside(r + o), TAPS[o + 2], 0.0) for o in range(-2, 3))

    weight = jnp.zeros((8, depth), f32)
    for o in range(-2, 3):
        weight = weight + jnp.where(inside(row + o), TAPS[o + 2] * tap(source - row - o) / norm(row + o), 0.0)
    used = (slot < 2 * patch_rows) & (at < 2 * patch_rows) & (c_in == c_out) & inside(source)
    weight = jnp.where(used, weight / norm(row), 0.0)
    stack = jnp.concatenate([b[...] for b in blocks], axis=0)
    result = jnp.dot(weight, stack, precision=lax.Precision.HIGHEST, preferred_element_type=f32)
    for c in range(2):
        out_ref[c, 0] = result[c * patch_rows : (c + 1) * patch_rows, :patch_cols]


def column_smoother(n):
    kernel = np.zeros((n, n))
    for i in range(n):
        for o in range(-2, 3):
            if 0 <= i + o < n:
                kernel[i, i + o] = TAPS[o + 2]
    kernel = kernel / kernel.sum(1, keepdims=True)
    table = np.zeros((n, LANES), np.float32)
    table[:, :n] = np.linalg.matrix_power(kernel, SMOOTH_PASSES).T
    return table


def call(body, out_shape, in_specs, out_specs, scratch=(), flops=0, moved=0):
    return pl.pallas_call(
        body,
        out_shape=out_shape,
        in_specs=in_specs,
        out_specs=out_specs,
        scratch_shapes=scratch,
        compiler_params=pltpu.CompilerParams(vmem_limit_bytes=VMEM_LIMIT),
        cost_estimate=pl.CostEstimate(flops=flops, bytes_accessed=moved, transcendentals=0),
    )


def local(sections, boundary, row_shift, row_frac, col_shift, col_frac, peak_shift):
    section = sections[0]
    n_rows, n_cols = section.shape
    n_ty, n_gz = lax.axis_size("ty"), lax.axis_size("gz")
    patch_rows, patch_cols = n_rows // PATCH, n_cols // PATCH
    n_patches = patch_rows * patch_cols
    gz, ty = lax.axis_index("gz"), lax.axis_index("ty")
    all_rows = n_rows * n_ty
    place = jnp.stack([gz, ty]).astype(jnp.int32)
    vmem = pl.BlockSpec(memory_space=pltpu.VMEM)
    smem = pl.BlockSpec(memory_space=pltpu.SMEM)

    even = ty % 2 == 0
    tops, bottoms = section[:MARGIN], section[n_rows - MARGIN :]
    first = lax.ppermute(jnp.where(even, bottoms, tops), ("gz", "ty"), halo_pairs(n_gz, n_ty, False))
    second = lax.ppermute(jnp.where(even, tops, bottoms), ("gz", "ty"), halo_pairs(n_gz, n_ty, True))

    n_mid = n_rows - 2 * MARGIN
    table_shape = (n_cols // BLOCK, BLOCK + 2 * LANES, BLOCK)
    mid, table = call(
        functools.partial(middle_kernel, all_rows),
        (jax.ShapeDtypeStruct((n_mid, n_cols), bf16), jax.ShapeDtypeStruct(table_shape, bf16)),
        [smem] + [vmem] * 5,
        (vmem, vmem),
    )(place, section, row_shift, row_frac, col_shift, col_frac)

    to_next = [(i, (i + 1) % n_gz) for i in range(n_gz)]
    old_mid = lax.ppermute(mid, "gz", to_next)
    edge = call(
        functools.partial(edges_kernel, all_rows),
        jax.ShapeDtypeStruct((2 * MARGIN, n_cols), bf16),
        [smem] + [vmem] * 6,
        vmem,
    )(place, first, second, section, row_shift, row_frac, table)
    old_edge = lax.ppermute(edge, "gz", to_next)
    rendered = jnp.concatenate([edge[:MARGIN], mid, edge[MARGIN:]], axis=0)[None]

    payload = call(
        window_kernel,
        jax.ShapeDtypeStruct((8, LANES), f32),
        [smem, smem] + [vmem] * 4 + [pl.BlockSpec(memory_space=pl.ANY), vmem],
        vmem,
        [
            pltpu.VMEM((n_patches, PATCH + 32, LANES), f32),
            pltpu.VMEM((9 * n_patches * 8, LANES), f32),
            pltpu.VMEM((2, n_patches, LANES), f32),
            pltpu.VMEM((n_rows, n_cols), bf16),
            pltpu.SemaphoreType.DMA,
        ],
    )(
        place,
        peak_shift.reshape(2, n_patches),
        mid,
        edge,
        old_mid,
        old_edge,
        boundary,
        jnp.asarray(column_smoother(patch_cols)),
    )

    swaps, seen, blocks = [], set(), [payload]
    for d in range(1, -(-2 * SMOOTH_PASSES // patch_rows) + 1):
        for other in (False, True):
            pairs = swap_pairs(n_ty, d, other)
            if pairs and pairs not in seen:
                seen.add(pairs)
                swaps.append((d, other))
                blocks.append(lax.ppermute(payload, "ty", both_ways(pairs)))
    flow = call(
        functools.partial(rows_kernel, n_ty, tuple(swaps)),
        jax.ShapeDtypeStruct((2, 1, patch_rows, patch_cols), f32),
        [smem] + [vmem] * len(blocks),
        vmem,
    )(place, *blocks)
    return rendered, flow


def solution(mesh):
    in_specs = (
        P(("parts", "gz"), "ty", None),
        P(("parts", "ty"), None),
        P(("parts", "gz"), "ty"),
        P(("parts", "gz"), "ty"),
        P(("parts", "gz"), None),
        P(("parts", "gz"), None),
        P(None, ("parts", "gz"), "ty", None),
    )
    out_specs = (P(("parts", "gz"), "ty", None), P(None, ("parts", "gz"), "ty", None))
    return jax.shard_map(local, mesh=mesh, in_specs=in_specs, out_specs=out_specs, check_vma=False)
```

```python
import functools

import jax
import jax.numpy as jnp
import numpy as np
from jax import lax
from jax.experimental import pallas as pl
from jax.experimental.pallas import tpu as pltpu
from jax.sharding import PartitionSpec as P

PATCH = 128
MARGIN = 64
SMOOTH_PASSES = 2
BLOCK = 256
LANES = 128
TAPS = (0.0625, 0.25, 0.375, 0.25, 0.0625)
FAR = 1 << 20
VMEM_LIMIT = 40 * 1024 * 1024

f32 = jnp.float32
bf16 = jnp.bfloat16


def swap_pairs(n, d, second):
    pairs = []
    for i in range(n):
        if (i // d) % 2 == int(second):
            j = i + d
            if j >= n:
                if not second or n % (2 * d):
                    continue
                j -= n
            pairs.append((i, j))
    return frozenset(frozenset(p) for p in pairs)


def both_ways(pairs):
    return sorted([tuple(sorted(p)) for p in pairs] + [tuple(sorted(p))[::-1] for p in pairs])


def halo_pairs(n_gz, n_ty, second):
    table = []
    for z in range(n_gz):
        for t in range(n_ty):
            partner = t + 1 if (t % 2 == 0) != second else t - 1
            if 0 <= partner < n_ty:
                table.append((z * n_ty + t, z * n_ty + partner))
            elif (z ^ 1) < n_gz:
                table.append((z * n_ty + t, (z ^ 1) * n_ty + t))
    return table


def hat(coord, position):
    return jnp.maximum(1.0 - jnp.abs(coord - position), 0.0)


def source_positions(ids, shift, frac, limit, base):
    source = jnp.clip(ids + shift, 0, limit) - base
    return source.astype(f32) + frac.astype(f32) * (1.0 / 256.0)


def contract_rows(table, source):
    return lax.dot_general(
        table, source, (((0,), (0,)), ((), ())), preferred_element_type=f32
    ).astype(bf16)


def columns_from(mix, start, table_ref, blocks, out_ref):
    for at, j in enumerate(blocks):
        first = j * BLOCK - LANES
        low, high = max(first, start), min(first + BLOCK + 2 * LANES, start + mix.shape[1])
        out_ref[:, at * BLOCK : (at + 1) * BLOCK] = jnp.dot(
            mix[:, low - start : high - start],
            table_ref[j, low - first : high - first, :],
            preferred_element_type=f32,
        ).astype(bf16)


def fetch_kernel(all_rows, section, row_shift, row_frac, col_shift, col_frac, *rest):
    held, send_first, send_second, mid_table, top_table, bottom_table, col_table = rest[:7]
    row_shift_v, row_frac_v, col_shift_v, col_frac_v, sems = rest[7:]
    n_rows, n_cols = section.shape
    tile = lax.axis_index("ty")
    base = tile * n_rows
    even = tile % 2 == 0
    low, high = 0, n_rows - MARGIN
    first_at = pl.multiple_of(jnp.where(even, high, low), MARGIN)
    second_at = pl.multiple_of(jnp.where(even, low, high), MARGIN)
    copies = [
        pltpu.make_async_copy(source, target, sems.at[k])
        for k, (source, target) in enumerate(
            (
                (col_shift, col_shift_v),
                (col_frac, col_frac_v),
                (row_shift, row_shift_v),
                (row_frac, row_frac_v),
                (section.at[pl.ds(first_at, MARGIN), :], send_first),
                (section.at[pl.ds(second_at, MARGIN), :], send_second),
                (section, held),
            )
        )
    ]
    for copy in copies:
        copy.start()
    for copy in copies[:4]:
        copy.wait()

    window = BLOCK + 2 * LANES
    reach = window - LANES
    coord = lax.broadcasted_iota(jnp.int32, (reach, BLOCK), 0).astype(f32)
    ids = lax.broadcasted_iota(jnp.int32, (1, BLOCK), 1)
    edge = jnp.zeros((LANES // 2, BLOCK), bf16)
    for j in range(n_cols // BLOCK):
        cols = slice(j * BLOCK, (j + 1) * BLOCK)
        pos = source_positions(
            ids + j * BLOCK, col_shift_v[:, cols], col_frac_v[:, cols], n_cols - 2, j * BLOCK - LANES // 2
        )
        col_table[j, 0 : LANES // 2, :] = edge
        col_table[j, LANES // 2 : LANES // 2 + reach, :] = hat(coord, pos).astype(bf16)
        col_table[j, LANES // 2 + reach :, :] = edge

    ids = lax.broadcasted_iota(jnp.int32, (1, n_rows), 1) + base
    pos = source_positions(ids, row_shift_v[...], row_frac_v[...], all_rows - 2, base)
    coord = lax.broadcasted_iota(jnp.int32, (n_rows, n_rows - 2 * MARGIN), 0).astype(f32)
    mid_table[...] = hat(coord, pos[:, MARGIN : n_rows - MARGIN]).astype(bf16)
    half = n_rows // 2
    slot = lax.broadcasted_iota(jnp.int32, (MARGIN, MARGIN), 0)
    own = lax.broadcasted_iota(jnp.int32, (half, MARGIN), 0)
    for top, table in ((True, top_table), (False, bottom_table)):
        near = slot - MARGIN if top else slot + n_rows
        in_first = even != top
        coord = jnp.concatenate(
            [
                jnp.where(in_first, near, FAR),
                jnp.where(in_first, FAR, near),
                own if top else own + half,
            ],
            axis=0,
        ).astype(f32)
        here = pos[:, :MARGIN] if top else pos[:, n_rows - MARGIN :]
        table[...] = hat(coord, here).astype(bf16)
    for copy in copies[4:]:
        copy.wait()


def middle_kernel(held, mid_table, col_table, mid_ref):
    mix = contract_rows(mid_table[...], held[...])
    columns_from(mix, 0, col_table, range(held.shape[1] // BLOCK), mid_ref)


def edges_kernel(blocks, first, second, held, top_table, bottom_table, col_table, *rest):
    edge_ref = rest[-1]
    n_rows, n_cols = held.shape
    half = n_rows // 2
    low = max(blocks[0] * BLOCK - LANES, 0)
    high = min((blocks[-1] + 1) * BLOCK + LANES, n_cols)
    mixes = []
    for table, own in ((top_table, slice(0, half)), (bottom_table, slice(half, n_rows))):
        stack = jnp.concatenate([first[:, low:high], second[:, low:high], held[own, low:high]], axis=0)
        mixes.append(contract_rows(table[...], stack))
    columns_from(jnp.concatenate(mixes, axis=0), low, col_table, blocks, edge_ref)


def pieces_of(i, n_rows):
    start, stop = i * PATCH, (i + 1) * PATCH
    pieces = []
    for is_edge, low, high, shift in (
        (True, 0, MARGIN, 0),
        (False, MARGIN, n_rows - MARGIN, MARGIN),
        (True, n_rows - MARGIN, n_rows, n_rows - 2 * MARGIN),
    ):
        a, b = max(start, low), min(stop, high)
        if a < b:
            pieces.append((is_edge, a - shift, b - a))
    return pieces


PAD = 16


def turned_kernel(n_ty, swaps, peaks, mid, *rest):
    edges, (rendered, turned, row_weights, sems) = rest[:-4], rest[-4:]
    n_mid, n_cols = mid.shape
    n_rows = n_mid + 2 * MARGIN
    patch_rows, patch_cols = n_rows // PATCH, n_cols // PATCH
    n_patches = patch_rows * patch_cols
    wide = n_cols // len(edges)
    moves = [(mid, rendered.at[pl.ds(MARGIN, n_mid), :])]
    for h, edge in enumerate(edges):
        cols = pl.ds(h * wide, wide)
        moves.append((edge.at[pl.ds(0, MARGIN), :], rendered.at[pl.ds(0, MARGIN), cols]))
        moves.append((edge.at[pl.ds(MARGIN, MARGIN), :], rendered.at[pl.ds(n_rows - MARGIN, MARGIN), cols]))
    copies = [pltpu.make_async_copy(a, b, sems.at[k]) for k, (a, b) in enumerate(moves)]
    for copy in copies:
        copy.start()
    fill_row_weights(n_ty, swaps, patch_rows, row_weights)
    for i in range(patch_rows):
        for h, edge in enumerate(edges):

            @pl.loop(0, wide // PATCH)
            def _(j):
                p = i * patch_cols + h * (wide // PATCH) + j
                here = pl.ds(pl.multiple_of(j * PATCH, PATCH), PATCH)
                there = pl.ds(pl.multiple_of(h * wide + j * PATCH, PATCH), PATCH)
                block = jnp.concatenate(
                    [edge[a : a + n, here] if is_edge else mid[a : a + n, there] for is_edge, a, n in pieces_of(i, n_rows)],
                    axis=0,
                ).astype(f32)
                for dx in range(3):
                    moved = pltpu.roll(block, (peaks[1, p] + (dx - 1)) % PATCH, 1)
                    q = dx * n_patches + p
                    turned[q, PAD : PAD + PATCH, :] = moved
                    turned[q, 0:PAD, :] = moved[PATCH - PAD :, :]
                    turned[q, PAD + PATCH :, :] = moved[:PAD, :]

    for copy in copies:
        copy.wait()


def window_kernel(h, n_halves, peaks, turned, old_mid, old_edge, boundary, smooth, *rest):
    before, (out_ref, acc, peak, whole, sem) = rest[:-5], rest[-5:]
    n_rows = boundary.shape[0]
    wide = old_edge.shape[1]
    patch_rows, here_cols = n_rows // PATCH, wide // PATCH
    patch_cols = here_cols * n_halves
    n_patches = patch_rows * patch_cols
    n_here = patch_rows * here_cols

    def sum_windows(block_of):
        for i in range(patch_rows):

            @pl.loop(0, here_cols)
            def _(j):
                p = i * patch_cols + h * here_cols + j
                at = i * here_cols + j
                peak_row, peak_col = peaks[0, p], peaks[1, p]
                peak[0, pl.ds(at, 1), :] = jnp.full((1, LANES), peak_row, jnp.int32).astype(f32)
                peak[1, pl.ds(at, 1), :] = jnp.full((1, LANES), peak_col, jnp.int32).astype(f32)
                sums = [None] * 9
                old = block_of(i, j)
                for r in range(PATCH // 8):
                    rows = old[8 * r : 8 * r + 8, :]
                    for dx in range(3):
                        for dy in range(3):
                            k = dy * 3 + dx
                            start = (PAD + 8 * r - (dy - 1)) - peak_row
                            term = turned[dx * n_patches + p, pl.ds(start, 8), :] * rows
                            sums[k] = term if sums[k] is None else sums[k] + term
                for k in range(9):
                    acc[pl.ds(pl.multiple_of((k * n_here + at) * 8, 8), 8), :] = sums[k]

    @pl.when(lax.axis_index("gz") == 0)
    def _():
        copy = pltpu.make_async_copy(boundary.at[:, pl.ds(h * wide, wide)], whole, sem)
        copy.start()
        copy.wait()
        sum_windows(
            lambda i, j: whole[
                i * PATCH : (i + 1) * PATCH, pl.ds(pl.multiple_of(j * PATCH, PATCH), PATCH)
            ].astype(f32)
        )

    @pl.when(lax.axis_index("gz") != 0)
    def _():
        def block_of(i, j):
            here = pl.ds(pl.multiple_of(j * PATCH, PATCH), PATCH)
            there = pl.ds(pl.multiple_of(h * wide + j * PATCH, PATCH), PATCH)
            return jnp.concatenate(
                [
                    old_edge[a : a + n, here] if is_edge else old_mid[a : a + n, there]
                    for is_edge, a, n in pieces_of(i, n_rows)
                ],
                axis=0,
            ).astype(f32)

        sum_windows(block_of)

    total = acc[pl.ds(0, 9 * n_here, stride=8), :]
    for s in range(1, 8):
        total = total + acc[pl.ds(s, 9 * n_here, stride=8), :]
    weights = jnp.maximum(jnp.sum(total, axis=1, keepdims=True) * (1.0 / PATCH), 0.0)
    w = [weights[k * n_here : (k + 1) * n_here] for k in range(9)]
    scale = 1.0 / jnp.maximum(sum(w), 1.0)
    moves = (
        (w[6] + w[7] + w[8] - w[0] - w[1] - w[2]) * scale,
        (w[2] + w[5] + w[8] - w[0] - w[3] - w[6]) * scale,
    )
    lines = []
    share = smooth[h * here_cols : (h + 1) * here_cols, :]
    for c in range(2):
        flow = moves[c] + peak[c]
        for i in range(patch_rows):
            row = flow[i * here_cols : (i + 1) * here_cols, :] * share
            lines.append(jnp.sum(row, axis=0, keepdims=True))
    lines.append(jnp.zeros((8 - len(lines), LANES), f32))
    result = jnp.concatenate(lines, axis=0)
    for b in before:
        result = result + b[...]
    out_ref[...] = result


def partner_of(tile, n, d, second):
    up = (tile // d) % 2 == int(second)
    return (tile + jnp.where(up, d, -d) + n) % n


def fill_row_weights(n_ty, swaps, patch_rows, out_ref):
    all_rows = n_ty * patch_rows
    tile = lax.axis_index("ty")
    held = 2 * patch_rows
    depth = LANES
    at = lax.broadcasted_iota(jnp.int32, (8, depth), 0)
    slot = lax.broadcasted_iota(jnp.int32, (8, depth), 1)
    holder = jnp.full((8, depth), tile, jnp.int32)
    for k, (d, second) in enumerate(swaps):
        holder = jnp.where((slot >> 3) == k + 1, partner_of(tile, n_ty, d, second), holder)
    inner = slot & 7
    c_out = (at >= patch_rows).astype(jnp.int32)
    c_in = (inner >= patch_rows).astype(jnp.int32)
    row = tile * patch_rows + at - c_out * patch_rows
    source = holder * patch_rows + inner - c_in * patch_rows

    def inside(r):
        return (r >= 0) & (r < all_rows)

    def tap(delta):
        size = jnp.abs(delta)
        return jnp.where(
            size == 0, TAPS[2], jnp.where(size == 1, TAPS[1], jnp.where(size == 2, TAPS[0], 0.0))
        )

    def norm(r):
        return sum(jnp.where(inside(r + o), TAPS[o + 2], 0.0) for o in range(-2, 3))

    weight = jnp.zeros((8, depth), f32)
    for o in range(-2, 3):
        weight = weight + jnp.where(inside(row + o), TAPS[o + 2] * tap(source - row - o) / norm(row + o), 0.0)
    used = (inner < held) & (at < held) & (c_in == c_out) & inside(source)
    weight = jnp.where(used, weight / norm(row), 0.0)
    for k in range(len(swaps) + 1):
        for b in range(held):
            out_ref[k * held + b] = jnp.broadcast_to(weight[:, 8 * k + b : 8 * k + b + 1], (8, LANES))


def rows_kernel(row_weights, *refs):
    blocks, out_ref = refs[:-1], refs[-1]
    patch_rows, patch_cols = out_ref.shape[2], out_ref.shape[3]
    held = 2 * patch_rows
    result = None
    for k, block in enumerate(blocks):
        for b in range(held):
            term = row_weights[k * held + b] * block[b : b + 1, :]
            result = term if result is None else result + term
    for c in range(2):
        out_ref[c, 0] = result[c * patch_rows : (c + 1) * patch_rows, :patch_cols]


def column_smoother(n):
    kernel = np.zeros((n, n))
    for i in range(n):
        for o in range(-2, 3):
            if 0 <= i + o < n:
                kernel[i, i + o] = TAPS[o + 2]
    kernel = kernel / kernel.sum(1, keepdims=True)
    table = np.zeros((n, LANES), np.float32)
    table[:, :n] = np.linalg.matrix_power(kernel, SMOOTH_PASSES).T
    return table


def call(body, out_shape, in_specs, out_specs, scratch=(), flops=0, moved=0):
    return pl.pallas_call(
        body,
        out_shape=out_shape,
        in_specs=in_specs,
        out_specs=out_specs,
        scratch_shapes=scratch,
        compiler_params=pltpu.CompilerParams(vmem_limit_bytes=VMEM_LIMIT),
        cost_estimate=pl.CostEstimate(flops=flops, bytes_accessed=moved, transcendentals=0),
    )


def local(sections, boundary, row_shift, row_frac, col_shift, col_frac, peak_shift):
    section = sections[0]
    n_rows, n_cols = section.shape
    n_ty, n_gz = lax.axis_size("ty"), lax.axis_size("gz")
    patch_rows, patch_cols = n_rows // PATCH, n_cols // PATCH
    n_patches = patch_rows * patch_cols
    all_rows = n_rows * n_ty
    n_mid, half = n_rows - 2 * MARGIN, n_rows // 2
    n_blocks = n_cols // BLOCK
    vmem = pl.BlockSpec(memory_space=pltpu.VMEM)
    smem = pl.BlockSpec(memory_space=pltpu.SMEM)
    hbm = pl.BlockSpec(memory_space=pltpu.HBM)
    shape = jax.ShapeDtypeStruct

    held, send_first, send_second, mid_table, top_table, bottom_table, col_table = call(
        functools.partial(fetch_kernel, all_rows),
        (
            shape((n_rows, n_cols), bf16),
            shape((MARGIN, n_cols), bf16),
            shape((MARGIN, n_cols), bf16),
            shape((n_rows, n_mid), bf16),
            shape((2 * MARGIN + half, MARGIN), bf16),
            shape((2 * MARGIN + half, MARGIN), bf16),
            shape((n_blocks, BLOCK + 2 * LANES, BLOCK), bf16),
        ),
        [hbm] * 5,
        [vmem] * 7,
        [
            pltpu.VMEM((1, n_rows), jnp.int32),
            pltpu.VMEM((1, n_rows), jnp.int32),
            pltpu.VMEM((1, n_cols), jnp.int32),
            pltpu.VMEM((1, n_cols), jnp.int32),
            pltpu.SemaphoreType.DMA((7,)),
        ],
    )(*(pltpu.with_memory_space_constraint(x, pltpu.HBM) for x in (section, row_shift, row_frac, col_shift, col_frac)))
    first = lax.ppermute(send_first, ("gz", "ty"), halo_pairs(n_gz, n_ty, False))
    second = lax.ppermute(send_second, ("gz", "ty"), halo_pairs(n_gz, n_ty, True))

    mid = call(middle_kernel, shape((n_mid, n_cols), bf16), [vmem] * 3, vmem)(held, mid_table, col_table)
    to_next = [(i, (i + 1) % n_gz) for i in range(n_gz)]
    old_mid = lax.ppermute(mid, "gz", to_next)

    halves = 2
    wide = n_cols // halves
    edges, old_edges = [], []
    for h in range(halves):
        blocks = tuple(range(h * n_blocks // halves, (h + 1) * n_blocks // halves))
        edges.append(
            call(
                functools.partial(edges_kernel, blocks),
                shape((2 * MARGIN, wide), bf16),
                [vmem] * 6 + [pl.BlockSpec(memory_space=pl.ANY)] * h,
                vmem,
            )(first, second, held, top_table, bottom_table, col_table, *edges[-1:])
        )
        old_edges.append(lax.ppermute(edges[h], "gz", to_next))

    swaps, seen, tables = [], set(), []
    for d in range(1, -(-2 * SMOOTH_PASSES // patch_rows) + 1):
        for other in (False, True):
            pairs = swap_pairs(n_ty, d, other)
            if pairs and pairs not in seen:
                seen.add(pairs)
                swaps.append((d, other))
                tables.append(both_ways(pairs))
    peaks = peak_shift.reshape(2, n_patches)
    terms = (len(swaps) + 1) * 2 * patch_rows
    rendered, turned, row_weights = call(
        functools.partial(turned_kernel, n_ty, tuple(swaps)),
        (
            shape((n_rows, n_cols), bf16),
            shape((3 * n_patches, PATCH + 2 * PAD, LANES), f32),
            shape((terms, 8, LANES), f32),
        ),
        [smem] + [vmem] * (1 + halves),
        [hbm, vmem, vmem],
        [pltpu.SemaphoreType.DMA((1 + 2 * halves,))],
        flops=4_000_000_000,
        moved=12_000_000,
    )(peaks, mid, *edges)

    payload = []
    smooth = jnp.asarray(column_smoother(patch_cols))
    n_here = n_patches // halves
    for h in range(halves):
        payload = [
            call(
                functools.partial(window_kernel, h, halves),
                shape((8, LANES), f32),
                [smem] + [vmem] * 3 + [hbm] + [vmem] * (1 + len(payload)),
                vmem,
                [
                    pltpu.VMEM((9 * n_here * 8, LANES), f32),
                    pltpu.VMEM((2, n_here, LANES), f32),
                    pltpu.VMEM((n_rows, wide), bf16),
                    pltpu.SemaphoreType.DMA,
                ],
            )(peaks, turned, old_mid, old_edges[h], boundary, smooth, *payload)
        ]
    blocks = payload + [lax.ppermute(payload[0], "ty", table) for table in tables]
    flow = call(
        rows_kernel, shape((2, 1, patch_rows, patch_cols), f32), [vmem] * (1 + len(blocks)), vmem
    )(row_weights, *blocks)
    return rendered[None], flow


def solution(mesh):
    in_specs = (
        P(("parts", "gz"), "ty", None),
        P(("parts", "ty"), None),
        P(("parts", "gz"), "ty"),
        P(("parts", "gz"), "ty"),
        P(("parts", "gz"), None),
        P(("parts", "gz"), None),
        P(None, ("parts", "gz"), "ty", None),
    )
    out_specs = (P(("parts", "gz"), "ty", None), P(None, ("parts", "gz"), "ty", None))
    return jax.shard_map(local, mesh=mesh, in_specs=in_specs, out_specs=out_specs, check_vma=False)
```

```python
import functools

import jax
import jax.numpy as jnp
import numpy as np
from jax import lax
from jax.experimental import pallas as pl
from jax.experimental.pallas import tpu as pltpu
from jax.sharding import PartitionSpec as P

PATCH = 128
MARGIN = 64
SMOOTH_PASSES = 2
BLOCK = 256
LANES = 128
TAPS = (0.0625, 0.25, 0.375, 0.25, 0.0625)
FAR = 1 << 20
VMEM_LIMIT = 40 * 1024 * 1024
UNROLL = 4
TURN_UNROLL = 4
WINDOW_UNROLL = 4
EDGE_FIRST = {2: ((0, MARGIN), (3 * MARGIN, 2 * MARGIN))}

f32 = jnp.float32
bf16 = jnp.bfloat16


def swap_pairs(n, d, second):
    pairs = []
    for i in range(n):
        if (i // d) % 2 == int(second):
            j = i + d
            if j >= n:
                if not second or n % (2 * d):
                    continue
                j -= n
            pairs.append((i, j))
    return frozenset(frozenset(p) for p in pairs)


def both_ways(pairs):
    return sorted([tuple(sorted(p)) for p in pairs] + [tuple(sorted(p))[::-1] for p in pairs])


def halo_pairs(n_gz, n_ty, second):
    table = []
    for z in range(n_gz):
        for t in range(n_ty):
            partner = t + 1 if (t % 2 == 0) != second else t - 1
            if 0 <= partner < n_ty:
                table.append((z * n_ty + t, z * n_ty + partner))
            elif (z ^ 1) < n_gz:
                table.append((z * n_ty + t, (z ^ 1) * n_ty + t))
    return table


def hat(coord, position):
    return jnp.maximum(1.0 - jnp.abs(coord - position), 0.0)


def source_positions(ids, shift, frac, limit, base):
    source = jnp.clip(ids + shift, 0, limit) - base
    return source.astype(f32) + frac.astype(f32) * (1.0 / 256.0)


def times(left, right):
    return jnp.dot(left, right, preferred_element_type=f32).astype(bf16)


def fetch_kernel(all_rows, section, row_shift, row_frac, col_shift, col_frac, *rest):
    held, send_first, send_second, mid_table, top_table, bottom_table, col_table = rest[:7]
    row_shift_v, row_frac_v, col_shift_v, col_frac_v, sems = rest[7:]
    n_rows, n_cols = section.shape
    tile = lax.axis_index("ty")
    base = tile * n_rows
    even = tile % 2 == 0
    first_at = pl.multiple_of(jnp.where(even, n_rows - MARGIN, 0), MARGIN)
    second_at = pl.multiple_of(jnp.where(even, 0, n_rows - MARGIN), MARGIN)
    copies = [
        pltpu.make_async_copy(source, target, sems.at[k])
        for k, (source, target) in enumerate(
            (
                (col_shift, col_shift_v),
                (col_frac, col_frac_v),
                (row_shift, row_shift_v),
                (row_frac, row_frac_v),
                (section.at[pl.ds(first_at, MARGIN), :], send_first),
                (section.at[pl.ds(second_at, MARGIN), :], send_second),
                (section, held),
            )
        )
    ]
    for copy in copies:
        copy.start()
    for copy in copies[:4]:
        copy.wait()

    reach = BLOCK + LANES
    coord = lax.broadcasted_iota(jnp.int32, (reach, BLOCK), 0).astype(f32)
    ids = lax.broadcasted_iota(jnp.int32, (1, BLOCK), 1)
    edge = jnp.zeros((LANES // 2, BLOCK), bf16)

    @pl.loop(0, n_cols // BLOCK)
    def _(j):
        cols = pl.ds(pl.multiple_of(j * BLOCK, BLOCK), BLOCK)
        pos = source_positions(
            ids + j * BLOCK, col_shift_v[:, cols], col_frac_v[:, cols], n_cols - 2, j * BLOCK - LANES // 2
        )
        col_table[j, 0 : LANES // 2, :] = edge
        col_table[j, LANES // 2 : LANES // 2 + reach, :] = hat(coord, pos).astype(bf16)
        col_table[j, LANES // 2 + reach :, :] = edge

    ids = lax.broadcasted_iota(jnp.int32, (1, n_rows), 1) + base
    pos = source_positions(ids, row_shift_v[...], row_frac_v[...], all_rows - 2, base)
    coord = lax.broadcasted_iota(jnp.int32, (n_rows, n_rows - 2 * MARGIN), 0).astype(f32)
    mid_table[...] = hat(coord, pos[:, MARGIN : n_rows - MARGIN]).T.astype(bf16)
    half = n_rows // 2
    slot = lax.broadcasted_iota(jnp.int32, (MARGIN, MARGIN), 0)
    own = lax.broadcasted_iota(jnp.int32, (half, MARGIN), 0)
    for top, table in ((True, top_table), (False, bottom_table)):
        near = slot - MARGIN if top else slot + n_rows
        in_first = even != top
        coord = jnp.concatenate(
            [
                jnp.where(in_first, near, FAR),
                jnp.where(in_first, FAR, near),
                own if top else own + half,
            ],
            axis=0,
        ).astype(f32)
        here = pos[:, :MARGIN] if top else pos[:, n_rows - MARGIN :]
        table[...] = hat(coord, here).T.astype(bf16)
    for copy in copies[4:]:
        copy.wait()


def middle_kernel(held, mid_table, col_table, mid_ref, mix):
    n_blocks = held.shape[1] // BLOCK
    edge = jnp.zeros((mix.shape[0], LANES), bf16)
    mix[:, 0:LANES] = edge
    mix[:, LANES + held.shape[1] :] = edge

    @pl.loop(0, n_blocks, unroll=UNROLL)
    def _(j):
        at = pl.multiple_of(j * BLOCK, BLOCK)
        mix[:, pl.ds(LANES + at, BLOCK)] = times(mid_table[...], held[:, pl.ds(at, BLOCK)])

    @pl.loop(0, n_blocks, unroll=UNROLL)
    def _(j):
        at = pl.multiple_of(j * BLOCK, BLOCK)
        mid_ref[:, pl.ds(at, BLOCK)] = times(mix[:, pl.ds(at, BLOCK + 2 * LANES)], col_table[j])


def edges_kernel(h, n_parts, first, second, held, top_table, bottom_table, col_table, *rest):
    edge_ref, mix = rest[-2:]
    n_rows, n_cols = held.shape
    half = n_rows // 2
    n_blocks = n_cols // BLOCK // n_parts
    low = max(h * n_blocks * BLOCK - LANES, 0) // BLOCK * BLOCK
    high = min(-(-((h + 1) * n_blocks * BLOCK + LANES) // BLOCK) * BLOCK, n_cols)
    edge = jnp.zeros((2 * MARGIN, LANES), bf16)
    mix[:, 0:LANES] = edge
    mix[:, LANES + high - low : 2 * LANES + high - low] = edge

    @pl.loop(0, (high - low) // BLOCK, unroll=UNROLL)
    def _(j):
        at = pl.multiple_of(j * BLOCK, BLOCK)
        here = pl.ds(low + at, BLOCK)
        for rows, table, own in (
            (slice(0, MARGIN), top_table, slice(0, half)),
            (slice(MARGIN, 2 * MARGIN), bottom_table, slice(half, n_rows)),
        ):
            stack = jnp.concatenate([first[:, here], second[:, here], held[own, here]], axis=0)
            mix[rows, pl.ds(LANES + at, BLOCK)] = times(table[...], stack)

    @pl.loop(0, n_blocks, unroll=UNROLL)
    def _(j):
        at = pl.multiple_of(j * BLOCK, BLOCK)
        start = h * n_blocks * BLOCK - low
        edge_ref[:, pl.ds(at, BLOCK)] = times(
            mix[:, pl.ds(start + at, BLOCK + 2 * LANES)], col_table[h * n_blocks + j]
        )


def turn_patches(peaks, cols_of, source, turned):
    n_patches = turned.shape[0] // 3
    patch_rows = source.shape[0] // MARGIN
    here_cols = source.shape[1] // PATCH
    patch_cols = n_patches // patch_rows
    for i in range(patch_rows):

        @pl.loop(0, here_cols, unroll=TURN_UNROLL)
        def _(j):
            p = i * patch_cols + cols_of + j
            block = source[i * MARGIN : (i + 1) * MARGIN, pl.ds(pl.multiple_of(j * PATCH, PATCH), PATCH)]
            for dx in range(3):
                turned[dx * n_patches + p] = pltpu.roll(block, (peaks[1, p] + (dx - 1)) % PATCH, 1)


def turn_middle_kernel(n_ty, swaps, peaks, mid, turned, bands, peak, row_weights):
    n_patches = bands.shape[0]
    turn_patches(peaks, 0, mid, turned)
    lane = lax.broadcasted_iota(jnp.int32, (PATCH // 8, LANES), 1)
    offset = lane - 8 * lax.broadcasted_iota(jnp.int32, (PATCH // 8, LANES), 0) + 1

    @pl.loop(0, n_patches)
    def _(p):
        bands[p] = jnp.where(((offset - peaks[0, p]) & (PATCH - 1)) <= 9, 1.0, 0.0)
        for c in range(2):
            peak[c, pl.ds(p, 1), :] = jnp.full((1, LANES), peaks[c, p], jnp.int32).astype(f32)

    fill_row_weights(n_ty, swaps, mid.shape[0] // MARGIN, row_weights)


def turn_edges_kernel(peaks, mid, *rest):
    edges, (rendered, turned, sems) = rest[:-3], rest[-3:]
    n_mid, n_cols = mid.shape
    n_rows = n_mid + 2 * MARGIN
    wide = n_cols // len(edges)
    moves = [(mid, rendered.at[pl.ds(MARGIN, n_mid), :])]
    for h, edge in enumerate(edges):
        cols = pl.ds(h * wide, wide)
        moves.append((edge.at[pl.ds(0, MARGIN), :], rendered.at[pl.ds(0, MARGIN), cols]))
        moves.append((edge.at[pl.ds(MARGIN, MARGIN), :], rendered.at[pl.ds(n_rows - MARGIN, MARGIN), cols]))
    copies = [pltpu.make_async_copy(a, b, sems.at[k]) for k, (a, b) in enumerate(moves)]
    for copy in copies:
        copy.start()
    for h, edge in enumerate(edges):
        turn_patches(peaks, h * (wide // PATCH), edge, turned)
    for copy in copies:
        copy.wait()


def window_kernel(h, n_parts, turned_mid, turned_edge, bands, peak, old_mid, old_edge, boundary, smooth, *rest):
    before, (out_ref, acc, whole, sem) = rest[:-4], rest[-4:]
    n_rows = boundary.shape[0]
    wide = old_edge.shape[1]
    patch_rows, here_cols = n_rows // PATCH, wide // PATCH
    patch_cols = here_cols * n_parts
    n_patches = patch_rows * patch_cols
    n_here = patch_rows * here_cols
    lane = lax.broadcasted_iota(jnp.int32, (8, LANES), 1) - lax.broadcasted_iota(jnp.int32, (8, LANES), 0)

    def sum_windows(old_of):
        @pl.loop(0, n_here, unroll=WINDOW_UNROLL)
        def _(at):
            i, j = at // here_cols, at % here_cols
            p = i * patch_cols + h * here_cols + j
            left = []
            for dx in range(3):
                left += [turned_edge[dx * n_patches + p], turned_mid[dx * n_patches + p]]
            products = lax.dot_general(
                jnp.concatenate(left, axis=0), old_of(i, j), (((1,), (1,)), ((), ())), preferred_element_type=f32
            )
            band = bands[p]
            place = (lane - peak[0, pl.ds(p, 1), :].astype(jnp.int32)) & 15
            for dx in range(3):
                lines = [
                    products[dx * PATCH + 8 * r : dx * PATCH + 8 * r + 8, :] * band[r : r + 1, :]
                    for r in range(PATCH // 8)
                ]
                even, odd = sum(lines[2::2], lines[0]), sum(lines[3::2], lines[1])
                for dy in range(3):
                    kept = jnp.where(place == (dy - 1) % 16, even, 0.0) + jnp.where(
                        place == (dy + 7) % 16, odd, 0.0
                    )
                    acc[pl.ds(pl.multiple_of(((dy * 3 + dx) * n_here + at) * 8, 8), 8), :] = kept

    def block(ref, start, col):
        return ref[pl.ds(pl.multiple_of(start, MARGIN), MARGIN), pl.ds(pl.multiple_of(col, PATCH), PATCH)]

    @pl.when(lax.axis_index("gz") == 0)
    def _():
        copy = pltpu.make_async_copy(boundary.at[:, pl.ds(h * wide, wide)], whole, sem)
        copy.start()
        copy.wait()

        def old_of(i, j):
            in_order = EDGE_FIRST[patch_rows]
            starts = [sum(jnp.where(i == k, s[part], 0) for k, s in enumerate(in_order)) for part in range(2)]
            return jnp.concatenate([block(whole, s, j * PATCH) for s in starts], axis=0)

        sum_windows(old_of)

    @pl.when(lax.axis_index("gz") != 0)
    def _():
        sum_windows(
            lambda i, j: jnp.concatenate(
                [block(old_edge, i * MARGIN, j * PATCH), block(old_mid, i * MARGIN, h * wide + j * PATCH)], axis=0
            )
        )

    total = acc[pl.ds(0, 9 * n_here, stride=8), :]
    for s in range(1, 8):
        total = total + acc[pl.ds(s, 9 * n_here, stride=8), :]
    weights = jnp.maximum(jnp.sum(total, axis=1, keepdims=True) * (1.0 / PATCH), 0.0)
    w = [weights[k * n_here : (k + 1) * n_here] for k in range(9)]
    scale = 1.0 / jnp.maximum(sum(w), 1.0)
    moves = (
        (w[6] + w[7] + w[8] - w[0] - w[1] - w[2]) * scale,
        (w[2] + w[5] + w[8] - w[0] - w[3] - w[6]) * scale,
    )
    lines = []
    share = smooth[h * here_cols : (h + 1) * here_cols, :]
    for c in range(2):
        for i in range(patch_rows):
            first = i * patch_cols + h * here_cols
            flow = moves[c][i * here_cols : (i + 1) * here_cols] + peak[c, first : first + here_cols, :]
            lines.append(jnp.sum(flow * share, axis=0, keepdims=True))
    lines.append(jnp.zeros((8 - len(lines), LANES), f32))
    result = jnp.concatenate(lines, axis=0)
    for b in before:
        result = result + b[...]
    out_ref[...] = result


def partner_of(tile, n, d, second):
    up = (tile // d) % 2 == int(second)
    return (tile + jnp.where(up, d, -d) + n) % n


def fill_row_weights(n_ty, swaps, patch_rows, out_ref):
    all_rows = n_ty * patch_rows
    tile = lax.axis_index("ty")
    held = 2 * patch_rows
    depth = LANES
    at = lax.broadcasted_iota(jnp.int32, (8, depth), 0)
    slot = lax.broadcasted_iota(jnp.int32, (8, depth), 1)
    holder = jnp.full((8, depth), tile, jnp.int32)
    for k, (d, second) in enumerate(swaps):
        holder = jnp.where((slot >> 3) == k + 1, partner_of(tile, n_ty, d, second), holder)
    inner = slot & 7
    c_out = (at >= patch_rows).astype(jnp.int32)
    c_in = (inner >= patch_rows).astype(jnp.int32)
    row = tile * patch_rows + at - c_out * patch_rows
    source = holder * patch_rows + inner - c_in * patch_rows

    def inside(r):
        return (r >= 0) & (r < all_rows)

    def tap(delta):
        size = jnp.abs(delta)
        return jnp.where(
            size == 0, TAPS[2], jnp.where(size == 1, TAPS[1], jnp.where(size == 2, TAPS[0], 0.0))
        )

    def norm(r):
        return sum(jnp.where(inside(r + o), TAPS[o + 2], 0.0) for o in range(-2, 3))

    weight = jnp.zeros((8, depth), f32)
    for o in range(-2, 3):
        weight = weight + jnp.where(inside(row + o), TAPS[o + 2] * tap(source - row - o) / norm(row + o), 0.0)
    used = (inner < held) & (at < held) & (c_in == c_out) & inside(source)
    weight = jnp.where(used, weight / norm(row), 0.0)
    for k in range(len(swaps) + 1):
        for b in range(held):
            out_ref[k * held + b] = jnp.broadcast_to(weight[:, 8 * k + b : 8 * k + b + 1], (8, LANES))


def rows_kernel(row_weights, *refs):
    blocks, out_ref = refs[:-1], refs[-1]
    patch_rows, patch_cols = out_ref.shape[2], out_ref.shape[3]
    held = 2 * patch_rows
    result = None
    for k, block in enumerate(blocks):
        for b in range(held):
            term = row_weights[k * held + b] * block[b : b + 1, :]
            result = term if result is None else result + term
    for c in range(2):
        out_ref[c, 0] = result[c * patch_rows : (c + 1) * patch_rows, :patch_cols]


def column_smoother(n):
    kernel = np.zeros((n, n))
    for i in range(n):
        for o in range(-2, 3):
            if 0 <= i + o < n:
                kernel[i, i + o] = TAPS[o + 2]
    kernel = kernel / kernel.sum(1, keepdims=True)
    table = np.zeros((n, LANES), np.float32)
    table[:, :n] = np.linalg.matrix_power(kernel, SMOOTH_PASSES).T
    return table


def call(body, out_shape, in_specs, out_specs, scratch=(), flops=0, moved=0):
    return pl.pallas_call(
        body,
        out_shape=out_shape,
        in_specs=in_specs,
        out_specs=out_specs,
        scratch_shapes=scratch,
        compiler_params=pltpu.CompilerParams(vmem_limit_bytes=VMEM_LIMIT),
        cost_estimate=pl.CostEstimate(flops=flops, bytes_accessed=moved, transcendentals=0),
    )


def local(sections, boundary, row_shift, row_frac, col_shift, col_frac, peak_shift):
    section = sections[0]
    n_rows, n_cols = section.shape
    n_ty, n_gz = lax.axis_size("ty"), lax.axis_size("gz")
    patch_rows, patch_cols = n_rows // PATCH, n_cols // PATCH
    n_patches = patch_rows * patch_cols
    all_rows = n_rows * n_ty
    n_mid, half = n_rows - 2 * MARGIN, n_rows // 2
    n_blocks = n_cols // BLOCK
    vmem = pl.BlockSpec(memory_space=pltpu.VMEM)
    smem = pl.BlockSpec(memory_space=pltpu.SMEM)
    hbm = pl.BlockSpec(memory_space=pltpu.HBM)
    shape = jax.ShapeDtypeStruct

    held, send_first, send_second, mid_table, top_table, bottom_table, col_table = call(
        functools.partial(fetch_kernel, all_rows),
        (
            shape((n_rows, n_cols), bf16),
            shape((MARGIN, n_cols), bf16),
            shape((MARGIN, n_cols), bf16),
            shape((n_mid, n_rows), bf16),
            shape((MARGIN, 2 * MARGIN + half), bf16),
            shape((MARGIN, 2 * MARGIN + half), bf16),
            shape((n_blocks, BLOCK + 2 * LANES, BLOCK), bf16),
        ),
        [hbm] * 5,
        [vmem] * 7,
        [
            pltpu.VMEM((1, n_rows), jnp.int32),
            pltpu.VMEM((1, n_rows), jnp.int32),
            pltpu.VMEM((1, n_cols), jnp.int32),
            pltpu.VMEM((1, n_cols), jnp.int32),
            pltpu.SemaphoreType.DMA((7,)),
        ],
    )(*(pltpu.with_memory_space_constraint(x, pltpu.HBM) for x in (section, row_shift, row_frac, col_shift, col_frac)))
    first = lax.ppermute(send_first, ("gz", "ty"), halo_pairs(n_gz, n_ty, False))
    second = lax.ppermute(send_second, ("gz", "ty"), halo_pairs(n_gz, n_ty, True))

    swaps, seen, tables = [], set(), []
    for d in range(1, -(-2 * SMOOTH_PASSES // patch_rows) + 1):
        for other in (False, True):
            pairs = swap_pairs(n_ty, d, other)
            if pairs and pairs not in seen:
                seen.add(pairs)
                swaps.append((d, other))
                tables.append(both_ways(pairs))
    peaks = peak_shift.reshape(2, n_patches)
    terms = (len(swaps) + 1) * 2 * patch_rows
    mid = call(
        middle_kernel,
        shape((n_mid, n_cols), bf16),
        [vmem] * 3,
        vmem,
        [pltpu.VMEM((n_mid, n_cols + 2 * LANES), bf16)],
    )(held, mid_table, col_table)
    to_next = [(i, (i + 1) % n_gz) for i in range(n_gz)]
    old_mid = lax.ppermute(mid, "gz", to_next)
    turned_mid, bands, peak, row_weights = call(
        functools.partial(turn_middle_kernel, n_ty, tuple(swaps)),
        (
            shape((3 * n_patches, MARGIN, LANES), bf16),
            shape((n_patches, PATCH // 8, LANES), f32),
            shape((2, n_patches, LANES), f32),
            shape((terms, 8, LANES), f32),
        ),
        [smem, vmem],
        [vmem] * 4,
        flops=1_000_000_000,
        moved=3_000_000,
    )(peaks, mid)

    parts = 2
    wide = n_cols // parts
    edges, old_edges = [], []
    for h in range(parts):
        edges.append(
            call(
                functools.partial(edges_kernel, h, parts),
                shape((2 * MARGIN, wide), bf16),
                [vmem] * 6 + [pl.BlockSpec(memory_space=pl.ANY)] * h,
                vmem,
                [pltpu.VMEM((2 * MARGIN, n_cols + 2 * LANES), bf16)],
            )(first, second, held, top_table, bottom_table, col_table, *edges[-1:])
        )
        old_edges.append(lax.ppermute(edges[h], "gz", to_next))
    rendered, turned_edge = call(
        turn_edges_kernel,
        (shape((n_rows, n_cols), bf16), shape((3 * n_patches, MARGIN, LANES), bf16)),
        [smem] + [vmem] * (1 + parts),
        [hbm, vmem],
        [pltpu.SemaphoreType.DMA((1 + 2 * parts,))],
        flops=4_000_000_000,
        moved=6_000_000,
    )(peaks, mid, *edges)

    payload = []
    smooth = jnp.asarray(column_smoother(patch_cols))
    n_here = n_patches // parts
    for h in range(parts):
        payload = [
            call(
                functools.partial(window_kernel, h, parts),
                shape((8, LANES), f32),
                [vmem] * 6 + [hbm] + [vmem] * (1 + len(payload)),
                vmem,
                [
                    pltpu.VMEM((9 * n_here * 8, LANES), f32),
                    pltpu.VMEM((n_rows, wide), bf16),
                    pltpu.SemaphoreType.DMA,
                ],
            )(turned_mid, turned_edge, bands, peak, old_mid, old_edges[h], boundary, smooth, *payload)
        ]
    blocks = payload + [lax.ppermute(payload[0], "ty", table) for table in tables]
    flow = call(
        rows_kernel, shape((2, 1, patch_rows, patch_cols), f32), [vmem] * (1 + len(blocks)), vmem
    )(row_weights, *blocks)
    return rendered[None], flow


def solution(mesh):
    in_specs = (
        P(("parts", "gz"), "ty", None),
        P(("parts", "ty"), None),
        P(("parts", "gz"), "ty"),
        P(("parts", "gz"), "ty"),
        P(("parts", "gz"), None),
        P(("parts", "gz"), None),
        P(None, ("parts", "gz"), "ty", None),
    )
    out_specs = (P(("parts", "gz"), "ty", None), P(None, ("parts", "gz"), "ty", None))
    return jax.shard_map(local, mesh=mesh, in_specs=in_specs, out_specs=out_specs, check_vma=False)
```

```python
import functools

import jax
import jax.numpy as jnp
import numpy as np
from jax import lax
from jax.experimental import pallas as pl
from jax.experimental.pallas import tpu as pltpu
from jax.sharding import PartitionSpec as P

PATCH = 128
MARGIN = 64
SMOOTH_PASSES = 2
BLOCK = 256
LANES = 128
TAPS = (0.0625, 0.25, 0.375, 0.25, 0.0625)
FAR = 1 << 20
VMEM_LIMIT = 8 * 1024 * 1024
TURN_UNROLL = 4
WINDOW_UNROLL = 16
EDGE_FIRST = {2: ((0, MARGIN), (3 * MARGIN, 2 * MARGIN))}

f32 = jnp.float32
bf16 = jnp.bfloat16


def swap_pairs(n, d, second):
    pairs = []
    for i in range(n):
        if (i // d) % 2 == int(second):
            j = i + d
            if j >= n:
                if not second or n % (2 * d):
                    continue
                j -= n
            pairs.append((i, j))
    return frozenset(frozenset(p) for p in pairs)


def both_ways(pairs):
    return sorted([tuple(sorted(p)) for p in pairs] + [tuple(sorted(p))[::-1] for p in pairs])


def halo_pairs(n_gz, n_ty, second):
    table = []
    for z in range(n_gz):
        for t in range(n_ty):
            partner = t + 1 if (t % 2 == 0) != second else t - 1
            if 0 <= partner < n_ty:
                table.append((z * n_ty + t, z * n_ty + partner))
            elif (z ^ 1) < n_gz:
                table.append((z * n_ty + t, (z ^ 1) * n_ty + t))
    return table


def hat(coord, position):
    return jnp.maximum(1.0 - jnp.abs(coord - position), 0.0)


def source_positions(ids, shift, frac, limit, base):
    source = jnp.clip(ids + shift, 0, limit) - base
    return source.astype(f32) + frac.astype(f32) * (1.0 / 256.0)


def times(left, right):
    return jnp.dot(left, right, preferred_element_type=f32).astype(bf16)


def fetch_kernel(all_rows, section, row_shift, row_frac, col_shift, col_frac, *rest):
    held, send_first, send_second, mid_table, top_table, bottom_table, col_table = rest[:7]
    row_shift_v, row_frac_v, col_shift_v, col_frac_v, sems = rest[7:]
    n_rows, n_cols = section.shape
    tile = lax.axis_index("ty")
    base = tile * n_rows
    even = tile % 2 == 0
    first_at = pl.multiple_of(jnp.where(even, n_rows - MARGIN, 0), MARGIN)
    second_at = pl.multiple_of(jnp.where(even, 0, n_rows - MARGIN), MARGIN)
    copies = [
        pltpu.make_async_copy(source, target, sems.at[k])
        for k, (source, target) in enumerate(
            (
                (col_shift, col_shift_v),
                (col_frac, col_frac_v),
                (row_shift, row_shift_v),
                (row_frac, row_frac_v),
                (section.at[pl.ds(first_at, MARGIN), :], send_first),
                (section.at[pl.ds(second_at, MARGIN), :], send_second),
                (section, held),
            )
        )
    ]
    for copy in copies:
        copy.start()
    for copy in copies[:4]:
        copy.wait()

    reach = BLOCK + LANES
    coord = lax.broadcasted_iota(jnp.int32, (reach, BLOCK), 0).astype(f32)
    ids = lax.broadcasted_iota(jnp.int32, (1, BLOCK), 1)
    edge = jnp.zeros((LANES // 2, BLOCK), bf16)

    @pl.loop(0, n_cols // BLOCK)
    def _(j):
        cols = pl.ds(pl.multiple_of(j * BLOCK, BLOCK), BLOCK)
        pos = source_positions(
            ids + j * BLOCK, col_shift_v[:, cols], col_frac_v[:, cols], n_cols - 2, j * BLOCK - LANES // 2
        )
        col_table[j, 0 : LANES // 2, :] = edge
        col_table[j, LANES // 2 : LANES // 2 + reach, :] = hat(coord, pos).astype(bf16)
        col_table[j, LANES // 2 + reach :, :] = edge

    ids = lax.broadcasted_iota(jnp.int32, (1, n_rows), 1) + base
    pos = source_positions(ids, row_shift_v[...], row_frac_v[...], all_rows - 2, base)
    coord = lax.broadcasted_iota(jnp.int32, (n_rows, n_rows - 2 * MARGIN), 0).astype(f32)
    mid_table[...] = hat(coord, pos[:, MARGIN : n_rows - MARGIN]).T.astype(bf16)
    half = n_rows // 2
    slot = lax.broadcasted_iota(jnp.int32, (MARGIN, MARGIN), 0)
    own = lax.broadcasted_iota(jnp.int32, (half, MARGIN), 0)
    for top, table in ((True, top_table), (False, bottom_table)):
        near = slot - MARGIN if top else slot + n_rows
        in_first = even != top
        coord = jnp.concatenate(
            [
                jnp.where(in_first, near, FAR),
                jnp.where(in_first, FAR, near),
                own if top else own + half,
            ],
            axis=0,
        ).astype(f32)
        here = pos[:, :MARGIN] if top else pos[:, n_rows - MARGIN :]
        table[...] = hat(coord, here).T.astype(bf16)
    for copy in copies[4:]:
        copy.wait()


def middle_kernel(held, mid_table, col_table, mid_ref, mix):
    n_blocks = held.shape[1] // BLOCK
    edge = jnp.zeros((mix.shape[0], LANES), bf16)
    mix[:, 0:LANES] = edge
    mix[:, LANES + held.shape[1] :] = edge

    for j in range(n_blocks):
        here = slice(j * BLOCK, (j + 1) * BLOCK)
        mix[:, LANES + j * BLOCK : LANES + (j + 1) * BLOCK] = times(mid_table[...], held[:, here])
    columns_of(mix, col_table, range(n_blocks), mid_ref)


def columns_of(mix, col_table, blocks, out_ref):
    for at, j in enumerate(blocks):
        out_ref[:, at * BLOCK : (at + 1) * BLOCK] = times(
            mix[:, j * BLOCK : (j + 1) * BLOCK + 2 * LANES], col_table[j]
        )


def first_edges_kernel(first, second, held, top_table, bottom_table, col_table, edge_ref, mix):
    n_rows, n_cols = held.shape
    half = n_rows // 2
    n_blocks = n_cols // BLOCK
    edge = jnp.zeros((2 * MARGIN, LANES), bf16)
    mix[:, 0:LANES] = edge
    mix[:, LANES + n_cols :] = edge

    for j in range(n_blocks):
        here = slice(j * BLOCK, (j + 1) * BLOCK)
        for rows, table, own in (
            (slice(0, MARGIN), top_table, slice(0, half)),
            (slice(MARGIN, 2 * MARGIN), bottom_table, slice(half, n_rows)),
        ):
            stack = jnp.concatenate([first[:, here], second[:, here], held[own, here]], axis=0)
            mix[rows, LANES + j * BLOCK : LANES + (j + 1) * BLOCK] = times(table[...], stack)
    columns_of(mix, col_table, range(edge_ref.shape[1] // BLOCK), edge_ref)


def more_edges_kernel(mix, col_table, *rest):
    edge_ref = rest[-1]
    n_blocks, wide = col_table.shape[0], edge_ref.shape[1] // BLOCK
    columns_of(mix, col_table, range(n_blocks - wide, n_blocks), edge_ref)


def turn_patches(peaks, cols_of, source, turned):
    n_patches = turned.shape[0] // 3
    patch_rows = source.shape[0] // MARGIN
    here_cols = source.shape[1] // PATCH
    patch_cols = n_patches // patch_rows
    for i in range(patch_rows):

        @pl.loop(0, here_cols, unroll=TURN_UNROLL)
        def _(j):
            p = i * patch_cols + cols_of + j
            block = source[i * MARGIN : (i + 1) * MARGIN, pl.ds(pl.multiple_of(j * PATCH, PATCH), PATCH)]
            for dx in range(3):
                turned[dx * n_patches + p] = pltpu.roll(block, (peaks[1, 0, i, cols_of + j] + (dx - 1)) % PATCH, 1)


def turn_middle_kernel(n_ty, swaps, peaks, mid, turned, bands, peak, row_weights):
    n_patches = bands.shape[0]
    turn_patches(peaks, 0, mid, turned)
    lane = lax.broadcasted_iota(jnp.int32, (PATCH // 8, LANES), 1)
    offset = lane - 8 * lax.broadcasted_iota(jnp.int32, (PATCH // 8, LANES), 0) + 1

    patch_rows, patch_cols = peaks.shape[2:]
    for i in range(patch_rows):

        @pl.loop(0, patch_cols)
        def _(j):
            p = i * patch_cols + j
            bands[p] = jnp.where(((offset - peaks[0, 0, i, j]) & (PATCH - 1)) <= 9, 1.0, 0.0)
            for c in range(2):
                peak[c, pl.ds(p, 1), :] = jnp.full((1, LANES), peaks[c, 0, i, j], jnp.int32).astype(f32)

    fill_row_weights(n_ty, swaps, mid.shape[0] // MARGIN, row_weights)


def turn_edges_kernel(peaks, mid, *rest):
    edges, (rendered, turned, sems) = rest[:-3], rest[-3:]
    n_mid, n_cols = mid.shape
    n_rows = n_mid + 2 * MARGIN
    wide = n_cols // len(edges)
    moves = [(mid, rendered.at[pl.ds(MARGIN, n_mid), :])]
    for h, edge in enumerate(edges):
        cols = pl.ds(h * wide, wide)
        moves.append((edge.at[pl.ds(0, MARGIN), :], rendered.at[pl.ds(0, MARGIN), cols]))
        moves.append((edge.at[pl.ds(MARGIN, MARGIN), :], rendered.at[pl.ds(n_rows - MARGIN, MARGIN), cols]))
    copies = [pltpu.make_async_copy(a, b, sems.at[k]) for k, (a, b) in enumerate(moves)]
    for copy in copies:
        copy.start()
    for h, edge in enumerate(edges):
        turn_patches(peaks, h * (wide // PATCH), edge, turned)
    for copy in copies:
        copy.wait()


def window_kernel(h, n_parts, turned_mid, turned_edge, bands, peak, old_mid, old_edge, boundary, smooth, *rest):
    before, (out_ref, acc, whole, sem) = rest[:-4], rest[-4:]
    n_rows = boundary.shape[0]
    wide = old_edge.shape[1]
    patch_rows, here_cols = n_rows // PATCH, wide // PATCH
    patch_cols = here_cols * n_parts
    n_patches = patch_rows * patch_cols
    n_here = patch_rows * here_cols
    lane = lax.broadcasted_iota(jnp.int32, (8, LANES), 1) - lax.broadcasted_iota(jnp.int32, (8, LANES), 0)

    def sum_windows(old_of):
        @pl.loop(0, n_here, unroll=WINDOW_UNROLL)
        def _(at):
            i, j = at // here_cols, at % here_cols
            p = i * patch_cols + h * here_cols + j
            left = []
            for dx in range(3):
                left += [turned_edge[dx * n_patches + p], turned_mid[dx * n_patches + p]]
            products = lax.dot_general(
                jnp.concatenate(left, axis=0), old_of(i, j), (((1,), (1,)), ((), ())), preferred_element_type=f32
            )
            band = bands[p]
            place = (lane - peak[0, pl.ds(p, 1), :].astype(jnp.int32)) & 15
            for dx in range(3):
                lines = [
                    products[dx * PATCH + 8 * r : dx * PATCH + 8 * r + 8, :] * band[r : r + 1, :]
                    for r in range(PATCH // 8)
                ]
                even, odd = sum(lines[2::2], lines[0]), sum(lines[3::2], lines[1])
                for dy in range(3):
                    kept = jnp.where(place == (dy - 1) % 16, even, 0.0) + jnp.where(
                        place == (dy + 7) % 16, odd, 0.0
                    )
                    acc[pl.ds(pl.multiple_of(((dy * 3 + dx) * n_here + at) * 8, 8), 8), :] = kept

    def block(ref, start, col):
        return ref[pl.ds(pl.multiple_of(start, MARGIN), MARGIN), pl.ds(pl.multiple_of(col, PATCH), PATCH)]

    @pl.when(lax.axis_index("gz") == 0)
    def _():
        copy = pltpu.make_async_copy(boundary.at[:, pl.ds(h * wide, wide)], whole, sem)
        copy.start()
        copy.wait()

        def old_of(i, j):
            in_order = EDGE_FIRST[patch_rows]
            starts = [sum(jnp.where(i == k, s[part], 0) for k, s in enumerate(in_order)) for part in range(2)]
            return jnp.concatenate([block(whole, s, j * PATCH) for s in starts], axis=0)

        sum_windows(old_of)

    @pl.when(lax.axis_index("gz") != 0)
    def _():
        sum_windows(
            lambda i, j: jnp.concatenate(
                [block(old_edge, i * MARGIN, j * PATCH), block(old_mid, i * MARGIN, h * wide + j * PATCH)], axis=0
            )
        )

    total = acc[pl.ds(0, 9 * n_here, stride=8), :]
    for s in range(1, 8):
        total = total + acc[pl.ds(s, 9 * n_here, stride=8), :]
    weights = jnp.maximum(jnp.sum(total, axis=1, keepdims=True) * (1.0 / PATCH), 0.0)
    w = [weights[k * n_here : (k + 1) * n_here] for k in range(9)]
    scale = 1.0 / jnp.maximum(sum(w), 1.0)
    moves = (
        (w[6] + w[7] + w[8] - w[0] - w[1] - w[2]) * scale,
        (w[2] + w[5] + w[8] - w[0] - w[3] - w[6]) * scale,
    )
    lines = []
    share = smooth[h * here_cols : (h + 1) * here_cols, :]
    for c in range(2):
        for i in range(patch_rows):
            first = i * patch_cols + h * here_cols
            flow = moves[c][i * here_cols : (i + 1) * here_cols] + peak[c, first : first + here_cols, :]
            lines.append(jnp.sum(flow * share, axis=0, keepdims=True))
    lines.append(jnp.zeros((8 - len(lines), LANES), f32))
    result = jnp.concatenate(lines, axis=0)
    for b in before:
        result = result + b[...]
    out_ref[...] = result


def partner_of(tile, n, d, second):
    up = (tile // d) % 2 == int(second)
    return (tile + jnp.where(up, d, -d) + n) % n


def fill_row_weights(n_ty, swaps, patch_rows, out_ref):
    all_rows = n_ty * patch_rows
    tile = lax.axis_index("ty")
    held = 2 * patch_rows
    depth = LANES
    at = lax.broadcasted_iota(jnp.int32, (8, depth), 0)
    slot = lax.broadcasted_iota(jnp.int32, (8, depth), 1)
    holder = jnp.full((8, depth), tile, jnp.int32)
    for k, (d, second) in enumerate(swaps):
        holder = jnp.where((slot >> 3) == k + 1, partner_of(tile, n_ty, d, second), holder)
    inner = slot & 7
    c_out = (at >= patch_rows).astype(jnp.int32)
    c_in = (inner >= patch_rows).astype(jnp.int32)
    row = tile * patch_rows + at - c_out * patch_rows
    source = holder * patch_rows + inner - c_in * patch_rows

    def inside(r):
        return (r >= 0) & (r < all_rows)

    def tap(delta):
        size = jnp.abs(delta)
        return jnp.where(
            size == 0, TAPS[2], jnp.where(size == 1, TAPS[1], jnp.where(size == 2, TAPS[0], 0.0))
        )

    def norm(r):
        return sum(jnp.where(inside(r + o), TAPS[o + 2], 0.0) for o in range(-2, 3))

    weight = jnp.zeros((8, depth), f32)
    for o in range(-2, 3):
        weight = weight + jnp.where(inside(row + o), TAPS[o + 2] * tap(source - row - o) / norm(row + o), 0.0)
    used = (inner < held) & (at < held) & (c_in == c_out) & inside(source)
    weight = jnp.where(used, weight / norm(row), 0.0)
    for k in range(len(swaps) + 1):
        for b in range(held):
            out_ref[k * held + b] = jnp.broadcast_to(weight[:, 8 * k + b : 8 * k + b + 1], (8, LANES))


def rows_kernel(row_weights, *refs):
    blocks, out_ref = refs[:-1], refs[-1]
    patch_rows, patch_cols = out_ref.shape[2], out_ref.shape[3]
    held = 2 * patch_rows
    result = None
    for k, block in enumerate(blocks):
        for b in range(held):
            term = row_weights[k * held + b] * block[b : b + 1, :]
            result = term if result is None else result + term
    for c in range(2):
        out_ref[c, 0] = result[c * patch_rows : (c + 1) * patch_rows, :patch_cols]


def column_smoother(n):
    kernel = np.zeros((n, n))
    for i in range(n):
        for o in range(-2, 3):
            if 0 <= i + o < n:
                kernel[i, i + o] = TAPS[o + 2]
    kernel = kernel / kernel.sum(1, keepdims=True)
    table = np.zeros((n, LANES), np.float32)
    table[:, :n] = np.linalg.matrix_power(kernel, SMOOTH_PASSES).T
    return table


def call(body, out_shape, in_specs, out_specs, scratch=(), flops=0, moved=0):
    return pl.pallas_call(
        body,
        out_shape=out_shape,
        in_specs=in_specs,
        out_specs=out_specs,
        scratch_shapes=scratch,
        compiler_params=pltpu.CompilerParams(vmem_limit_bytes=VMEM_LIMIT),
        cost_estimate=pl.CostEstimate(flops=flops, bytes_accessed=moved, transcendentals=0),
    )


def local(sections, boundary, row_shift, row_frac, col_shift, col_frac, peak_shift):
    section = sections[0]
    n_rows, n_cols = section.shape
    n_ty, n_gz = lax.axis_size("ty"), lax.axis_size("gz")
    patch_rows, patch_cols = n_rows // PATCH, n_cols // PATCH
    n_patches = patch_rows * patch_cols
    all_rows = n_rows * n_ty
    n_mid, half = n_rows - 2 * MARGIN, n_rows // 2
    n_blocks = n_cols // BLOCK
    vmem = pl.BlockSpec(memory_space=pltpu.VMEM)
    smem = pl.BlockSpec(memory_space=pltpu.SMEM)
    hbm = pl.BlockSpec(memory_space=pltpu.HBM)
    shape = jax.ShapeDtypeStruct

    held, send_first, send_second, mid_table, top_table, bottom_table, col_table = call(
        functools.partial(fetch_kernel, all_rows),
        (
            shape((n_rows, n_cols), bf16),
            shape((MARGIN, n_cols), bf16),
            shape((MARGIN, n_cols), bf16),
            shape((n_mid, n_rows), bf16),
            shape((MARGIN, 2 * MARGIN + half), bf16),
            shape((MARGIN, 2 * MARGIN + half), bf16),
            shape((n_blocks, BLOCK + 2 * LANES, BLOCK), bf16),
        ),
        [hbm] * 5,
        [vmem] * 7,
        [
            pltpu.VMEM((1, n_rows), jnp.int32),
            pltpu.VMEM((1, n_rows), jnp.int32),
            pltpu.VMEM((1, n_cols), jnp.int32),
            pltpu.VMEM((1, n_cols), jnp.int32),
            pltpu.SemaphoreType.DMA((7,)),
        ],
    )(*(pltpu.with_memory_space_constraint(x, pltpu.HBM) for x in (section, row_shift, row_frac, col_shift, col_frac)))
    first = lax.ppermute(send_first, ("gz", "ty"), halo_pairs(n_gz, n_ty, False))
    second = lax.ppermute(send_second, ("gz", "ty"), halo_pairs(n_gz, n_ty, True))

    swaps, seen, tables = [], set(), []
    for d in range(1, -(-2 * SMOOTH_PASSES // patch_rows) + 1):
        for other in (False, True):
            pairs = swap_pairs(n_ty, d, other)
            if pairs and pairs not in seen:
                seen.add(pairs)
                swaps.append((d, other))
                tables.append(both_ways(pairs))
    peaks = peak_shift
    terms = (len(swaps) + 1) * 2 * patch_rows
    mid = call(
        middle_kernel,
        shape((n_mid, n_cols), bf16),
        [vmem] * 3,
        vmem,
        [pltpu.VMEM((n_mid, n_cols + 2 * LANES), bf16)],
    )(held, mid_table, col_table)
    to_next = [(i, (i + 1) % n_gz) for i in range(n_gz)]
    old_mid = lax.ppermute(mid, "gz", to_next)
    turned_mid, bands, peak, row_weights = call(
        functools.partial(turn_middle_kernel, n_ty, tuple(swaps)),
        (
            shape((3 * n_patches, MARGIN, LANES), bf16),
            shape((n_patches, PATCH // 8, LANES), f32),
            shape((2, n_patches, LANES), f32),
            shape((terms, 8, LANES), f32),
        ),
        [smem, vmem],
        [vmem] * 4,
        flops=1_000_000_000,
        moved=3_000_000,
    )(peaks, mid)

    parts = 2
    wide = n_cols // parts
    first_edge, mix = call(
        first_edges_kernel,
        (shape((2 * MARGIN, wide), bf16), shape((2 * MARGIN, n_cols + 2 * LANES), bf16)),
        [vmem] * 6,
        [vmem] * 2,
    )(first, second, held, top_table, bottom_table, col_table)
    first_old = lax.ppermute(first_edge, "gz", to_next)
    second_edge = call(more_edges_kernel, shape((2 * MARGIN, n_cols - wide), bf16), [vmem] * 2 + [pl.BlockSpec(memory_space=pl.ANY)], vmem)(
        mix, col_table, first_edge
    )
    second_old = lax.ppermute(second_edge, "gz", to_next)
    edges, old_edges = (first_edge, second_edge), (first_old, second_old)
    rendered, turned_edge = call(
        turn_edges_kernel,
        (shape((n_rows, n_cols), bf16), shape((3 * n_patches, MARGIN, LANES), bf16)),
        [smem] + [vmem] * (1 + parts),
        [hbm, vmem],
        [pltpu.SemaphoreType.DMA((1 + 2 * parts,))],
        flops=4_000_000_000,
        moved=6_000_000,
    )(peaks, mid, *edges)

    payload = []
    smooth = jnp.asarray(column_smoother(patch_cols))
    n_here = n_patches // parts
    for h in range(parts):
        payload = [
            call(
                functools.partial(window_kernel, h, parts),
                shape((8, LANES), f32),
                [vmem] * 6 + [hbm] + [vmem] * (1 + len(payload)),
                vmem,
                [
                    pltpu.VMEM((9 * n_here * 8, LANES), f32),
                    pltpu.VMEM((n_rows, wide), bf16),
                    pltpu.SemaphoreType.DMA,
                ],
            )(turned_mid, turned_edge, bands, peak, old_mid, old_edges[h], boundary, smooth, *payload)
        ]
    blocks = payload + [lax.ppermute(payload[0], "ty", table) for table in tables]
    flow = call(
        rows_kernel, shape((2, 1, patch_rows, patch_cols), f32), [vmem] * (1 + len(blocks)), vmem
    )(row_weights, *blocks)
    return rendered[None], flow


def solution(mesh):
    in_specs = (
        P(("parts", "gz"), "ty", None),
        P(("parts", "ty"), None),
        P(("parts", "gz"), "ty"),
        P(("parts", "gz"), "ty"),
        P(("parts", "gz"), None),
        P(("parts", "gz"), None),
        P(None, ("parts", "gz"), "ty", None),
    )
    out_specs = (P(("parts", "gz"), "ty", None), P(None, ("parts", "gz"), "ty", None))
    return jax.shard_map(local, mesh=mesh, in_specs=in_specs, out_specs=out_specs, check_vma=False)
```

```python
import functools

import jax
import jax.numpy as jnp
import numpy as np
from jax import lax
from jax.experimental import pallas as pl
from jax.experimental.pallas import tpu as pltpu
from jax.sharding import PartitionSpec as P

PATCH = 128
MARGIN = 64
SMOOTH_PASSES = 2
BLOCK = 256
LANES = 128
TAPS = (0.0625, 0.25, 0.375, 0.25, 0.0625)
FAR = 1 << 20
VMEM_LIMIT = 16 * 1024 * 1024
TURN_UNROLL = 4

f32 = jnp.float32
bf16 = jnp.bfloat16


def swap_table(n_gz, n_ty, d, second):
    table = []
    for z in range(n_gz):
        for t in range(n_ty):
            partner = t + d if ((t // d) % 2 == 0) != second else t - d
            if 0 <= partner < n_ty:
                table.append((z * n_ty + t, z * n_ty + partner))
            elif (z ^ 1) < n_gz:
                table.append((z * n_ty + t, (z ^ 1) * n_ty + t))
    return tuple(table)


def partner_of(tile, d, second):
    up = (tile // d) % 2 == int(second)
    return tile + jnp.where(up, d, -d)


def has_partners(n_ty, d, second):
    return any(((t // d) % 2 == 0) != second and t + d < n_ty for t in range(n_ty))


def takes_bottom(second):
    return (lax.axis_index("ty") % 2 == 0) != second


def hat(coord, position):
    return jnp.maximum(1.0 - jnp.abs(coord - position), 0.0)


def source_positions(ids, shift, frac, limit, base):
    source = jnp.clip(ids + shift, 0, limit) - base
    return source.astype(f32) + frac.astype(f32) * (1.0 / 256.0)


def times(left, right):
    return jnp.dot(left, right, preferred_element_type=f32).astype(bf16)


def fetch_kernel(all_rows, section, row_shift, row_frac, col_shift, col_frac, *rest):
    held, send_first, mid_table, first_table, second_table, col_table = rest[:6]
    row_shift_v, row_frac_v, col_shift_v, col_frac_v, sems = rest[6:]
    n_rows, n_cols = section.shape
    tile = lax.axis_index("ty")
    base = tile * n_rows
    first_at = pl.multiple_of(jnp.where(takes_bottom(False), n_rows - MARGIN, 0), MARGIN)
    copies = [
        pltpu.make_async_copy(source, target, sems.at[k])
        for k, (source, target) in enumerate(
            (
                (col_shift, col_shift_v),
                (col_frac, col_frac_v),
                (row_shift, row_shift_v),
                (row_frac, row_frac_v),
                (section.at[pl.ds(first_at, MARGIN), :], send_first),
                (section, held),
            )
        )
    ]
    for copy in copies:
        copy.start()
    for copy in copies[:4]:
        copy.wait()

    reach = BLOCK + LANES
    coord = lax.broadcasted_iota(jnp.int32, (reach, BLOCK), 0).astype(f32)
    ids = lax.broadcasted_iota(jnp.int32, (1, BLOCK), 1)
    edge = jnp.zeros((LANES // 2, BLOCK), bf16)

    @pl.loop(0, n_cols // BLOCK)
    def _(j):
        cols = pl.ds(pl.multiple_of(j * BLOCK, BLOCK), BLOCK)
        pos = source_positions(
            ids + j * BLOCK, col_shift_v[:, cols], col_frac_v[:, cols], n_cols - 2, j * BLOCK - LANES // 2
        )
        col_table[j, 0 : LANES // 2, :] = edge
        col_table[j, LANES // 2 : LANES // 2 + reach, :] = hat(coord, pos).astype(bf16)
        col_table[j, LANES // 2 + reach :, :] = edge

    ids = lax.broadcasted_iota(jnp.int32, (1, n_rows), 1) + base
    pos = source_positions(ids, row_shift_v[...], row_frac_v[...], all_rows - 2, base)
    coord = lax.broadcasted_iota(jnp.int32, (n_rows, n_rows - 2 * MARGIN), 0).astype(f32)
    mid_table[...] = hat(coord, pos[:, MARGIN : n_rows - MARGIN]).T.astype(bf16)
    half = n_rows // 2
    slot = lax.broadcasted_iota(jnp.int32, (MARGIN + half, MARGIN), 0)
    for second, table in ((False, first_table), (True, second_table)):
        bottom = takes_bottom(second)
        start = jnp.where(
            slot < MARGIN, jnp.where(bottom, n_rows, -MARGIN), jnp.where(bottom, half - MARGIN, -MARGIN)
        )
        here = jnp.where(bottom, pos[:, n_rows - MARGIN :], pos[:, :MARGIN])
        table[...] = hat((slot + start).astype(f32), here).T.astype(bf16)
    for copy in copies[4:]:
        copy.wait()


def columns_of(mix, col_table, out_ref):
    for j in range(col_table.shape[0]):
        out_ref[:, j * BLOCK : (j + 1) * BLOCK] = times(mix[:, j * BLOCK : (j + 1) * BLOCK + 2 * LANES], col_table[j])


def clear_sides(mix):
    edge = jnp.zeros((mix.shape[0], LANES), bf16)
    mix[:, 0:LANES] = edge
    mix[:, mix.shape[1] - LANES :] = edge


def middle_kernel(held, mid_table, col_table, mid_ref, send_second, mix):
    n_rows = held.shape[0]
    clear_sides(mix)
    for j in range(col_table.shape[0]):
        mix[:, LANES + j * BLOCK : LANES + (j + 1) * BLOCK] = times(
            mid_table[...], held[:, j * BLOCK : (j + 1) * BLOCK]
        )
    columns_of(mix, col_table, mid_ref)
    at = pl.multiple_of(jnp.where(takes_bottom(True), n_rows - MARGIN, 0), MARGIN)
    send_second[...] = held[pl.ds(at, MARGIN), :]


def edges_kernel(second, halo, held, table, col_table, *rest):
    edge_ref, mix = rest[-2:]
    half = held.shape[0] // 2
    own = pl.ds(pl.multiple_of(jnp.where(takes_bottom(second), half, 0), half), half)
    clear_sides(mix)
    for j in range(col_table.shape[0]):
        here = slice(j * BLOCK, (j + 1) * BLOCK)
        stack = jnp.concatenate([halo[:, here], held[own, here]], axis=0)
        mix[:, LANES + j * BLOCK : LANES + (j + 1) * BLOCK] = times(table[...], stack)
    columns_of(mix, col_table, edge_ref)


def turn_patches(peaks, i, rows, source, turned, first):
    patch_cols = source.shape[1] // PATCH
    n_turned = turned.shape[0] // 3

    @pl.loop(0, patch_cols, unroll=TURN_UNROLL)
    def _(j):
        block = source[rows, pl.ds(pl.multiple_of(j * PATCH, PATCH), PATCH)]
        for dx in range(3):
            turned[dx * n_turned + first + j] = pltpu.roll(block, (peaks[1, 0, i, j] + (dx - 1)) % PATCH, 1)


def turn_middle_kernel(n_ty, swaps, peaks, mid, turned, bands, peak, row_weights):
    n_patches = bands.shape[0]
    for i in range(mid.shape[0] // MARGIN):
        turn_patches(peaks, i, slice(i * MARGIN, (i + 1) * MARGIN), mid, turned, i * (mid.shape[1] // PATCH))
    lane = lax.broadcasted_iota(jnp.int32, (PATCH // 8, LANES), 1)
    offset = lane - 8 * lax.broadcasted_iota(jnp.int32, (PATCH // 8, LANES), 0) + 1

    patch_rows, patch_cols = peaks.shape[2:]
    for i in range(patch_rows):

        @pl.loop(0, patch_cols)
        def _(j):
            p = i * patch_cols + j
            bands[p] = jnp.where(((offset - peaks[0, 0, i, j]) & (PATCH - 1)) <= 9, 1.0, 0.0)
            for c in range(2):
                peak[c, pl.ds(p, 1), :] = jnp.full((1, LANES), peaks[c, 0, i, j], jnp.int32).astype(f32)

    fill_row_weights(n_ty, swaps, mid.shape[0] // MARGIN, row_weights)


def edge_patch_row(second, patch_rows):
    return jnp.where(takes_bottom(second), patch_rows - 1, 0)


def turn_first_kernel(patch_rows, peaks, edge, turned):
    turn_patches(peaks, edge_patch_row(False, patch_rows), slice(None), edge, turned, 0)


def turn_second_kernel(patch_rows, peaks, mid, first, second, rendered, turned, sems):
    n_mid = mid.shape[0]
    n_rows = n_mid + 2 * MARGIN
    moves = [(mid, pl.ds(MARGIN, n_mid))]
    for edge, which in ((first, False), (second, True)):
        at = pl.multiple_of(jnp.where(takes_bottom(which), n_rows - MARGIN, 0), MARGIN)
        moves.append((edge, pl.ds(at, MARGIN)))
    copies = [pltpu.make_async_copy(a, rendered.at[b, :], sems.at[k]) for k, (a, b) in enumerate(moves)]
    for copy in copies:
        copy.start()
    turn_patches(peaks, edge_patch_row(True, patch_rows), slice(None), second, turned, 0)
    for copy in copies:
        copy.wait()


def patch_row_flow(i, turned_edge, turned_mid, bands, peak, smooth, old_of, acc):
    patch_cols = turned_edge.shape[0] // 3
    n_patches = bands.shape[0]
    lane = lax.broadcasted_iota(jnp.int32, (8, LANES), 1) - lax.broadcasted_iota(jnp.int32, (8, LANES), 0)
    for j in range(patch_cols):
        p = i * patch_cols + j
        left = []
        for dx in range(3):
            left += [turned_edge[dx * patch_cols + j], turned_mid[dx * n_patches + p]]
        products = lax.dot_general(
            jnp.concatenate(left, axis=0), old_of(j), (((1,), (1,)), ((), ())), preferred_element_type=f32
        )
        band = bands[p]
        place = (lane - peak[0, pl.ds(p, 1), :].astype(jnp.int32)) & 15
        for dx in range(3):
            lines = [
                products[dx * PATCH + 8 * r : dx * PATCH + 8 * r + 8, :] * band[r : r + 1, :]
                for r in range(PATCH // 8)
            ]
            even, odd = sum(lines[2::2], lines[0]), sum(lines[3::2], lines[1])
            for dy in range(3):
                at = ((dy * 3 + dx) * patch_cols + j) * 8
                acc[at : at + 8, :] = jnp.where(place == (dy - 1) % 16, even, 0.0) + jnp.where(
                    place == (dy + 7) % 16, odd, 0.0
                )
    total = acc[pl.ds(0, 9 * patch_cols, stride=8), :]
    for s in range(1, 8):
        total = total + acc[pl.ds(s, 9 * patch_cols, stride=8), :]
    weights = jnp.maximum(jnp.sum(total, axis=1, keepdims=True) * (1.0 / PATCH), 0.0)
    w = [weights[k * patch_cols : (k + 1) * patch_cols] for k in range(9)]
    scale = 1.0 / jnp.maximum(sum(w), 1.0)
    moves = (
        (w[6] + w[7] + w[8] - w[0] - w[1] - w[2]) * scale,
        (w[2] + w[5] + w[8] - w[0] - w[3] - w[6]) * scale,
    )
    here = pl.ds(pl.multiple_of(i * patch_cols, patch_cols), patch_cols)
    return [jnp.sum((moves[c] + peak[c, here, :]) * smooth[...], axis=0, keepdims=True) for c in range(2)]


def put_lines(lines, i, patch_rows):
    at = lax.broadcasted_iota(jnp.int32, (8, LANES), 0)
    return sum(jnp.where(at == c * patch_rows + i, line, 0.0) for c, line in enumerate(lines))


def boundary_kernel(turned_mid, turned_first, turned_second, bands, peak, boundary, smooth, out_ref, acc, whole, sem):
    n_rows = boundary.shape[0]
    patch_rows = n_rows // PATCH
    out_ref[...] = jnp.zeros_like(out_ref)

    @pl.when(lax.axis_index("gz") == 0)
    def _():
        copy = pltpu.make_async_copy(boundary, whole, sem)
        copy.start()
        copy.wait()

        @pl.loop(0, patch_rows)
        def _(k):
            i = jnp.where(k == 0, edge_patch_row(False, patch_rows), edge_patch_row(True, patch_rows))
            at_edge = pl.multiple_of(i * (n_rows - MARGIN), MARGIN)
            at_mid = pl.multiple_of(MARGIN + i * MARGIN, MARGIN)

            def old_of(j):
                cols = slice(j * PATCH, (j + 1) * PATCH)
                return jnp.concatenate([whole[pl.ds(at_edge, MARGIN), cols], whole[pl.ds(at_mid, MARGIN), cols]], axis=0)

            def flow_with(turned_edge):
                out_ref[...] += put_lines(
                    patch_row_flow(i, turned_edge, turned_mid, bands, peak, smooth, old_of, acc), i, patch_rows
                )

            @pl.when(k == 0)
            def _():
                flow_with(turned_first)

            @pl.when(k != 0)
            def _():
                flow_with(turned_second)


def window_kernel(second, turned_mid, turned_edge, bands, peak, old_mid, old_edge, smooth, before, out_ref, acc):
    patch_rows = old_mid.shape[0] // MARGIN
    out_ref[...] = before[...]

    @pl.when(lax.axis_index("gz") != 0)
    def _():
        i = edge_patch_row(second, patch_rows)
        at_mid = pl.multiple_of(i * MARGIN, MARGIN)

        def old_of(j):
            cols = slice(j * PATCH, (j + 1) * PATCH)
            return jnp.concatenate([old_edge[:, cols], old_mid[pl.ds(at_mid, MARGIN), cols]], axis=0)

        lines = patch_row_flow(i, turned_edge, turned_mid, bands, peak, smooth, old_of, acc)
        out_ref[...] = before[...] + put_lines(lines, i, patch_rows)


def fill_row_weights(n_ty, swaps, patch_rows, out_ref):
    all_rows = n_ty * patch_rows
    tile = lax.axis_index("ty")
    held = 2 * patch_rows
    depth = LANES
    at = lax.broadcasted_iota(jnp.int32, (8, depth), 0)
    slot = lax.broadcasted_iota(jnp.int32, (8, depth), 1)
    holder = jnp.full((8, depth), tile, jnp.int32)
    for k, (d, second) in enumerate(swaps):
        holder = jnp.where((slot >> 3) == k + 1, partner_of(tile, d, second), holder)
    inner = slot & 7
    c_out = (at >= patch_rows).astype(jnp.int32)
    c_in = (inner >= patch_rows).astype(jnp.int32)
    row = tile * patch_rows + at - c_out * patch_rows
    source = holder * patch_rows + inner - c_in * patch_rows

    def inside(r):
        return (r >= 0) & (r < all_rows)

    def tap(delta):
        size = jnp.abs(delta)
        return jnp.where(
            size == 0, TAPS[2], jnp.where(size == 1, TAPS[1], jnp.where(size == 2, TAPS[0], 0.0))
        )

    def norm(r):
        return sum(jnp.where(inside(r + o), TAPS[o + 2], 0.0) for o in range(-2, 3))

    weight = jnp.zeros((8, depth), f32)
    for o in range(-2, 3):
        weight = weight + jnp.where(inside(row + o), TAPS[o + 2] * tap(source - row - o) / norm(row + o), 0.0)
    used = (inner < held) & (at < held) & (c_in == c_out) & inside(source)
    weight = jnp.where(used, weight / norm(row), 0.0)
    for k in range(len(swaps) + 1):
        for b in range(held):
            out_ref[k * held + b] = jnp.broadcast_to(weight[:, 8 * k + b : 8 * k + b + 1], (8, LANES))


def rows_kernel(row_weights, *refs):
    blocks, out_ref = refs[:-1], refs[-1]
    patch_rows, patch_cols = out_ref.shape[2], out_ref.shape[3]
    held = 2 * patch_rows
    result = None
    for k, block in enumerate(blocks):
        for b in range(held):
            term = row_weights[k * held + b] * block[b : b + 1, :]
            result = term if result is None else result + term
    for c in range(2):
        out_ref[c, 0] = result[c * patch_rows : (c + 1) * patch_rows, :patch_cols]


def column_smoother(n):
    kernel = np.zeros((n, n))
    for i in range(n):
        for o in range(-2, 3):
            if 0 <= i + o < n:
                kernel[i, i + o] = TAPS[o + 2]
    kernel = kernel / kernel.sum(1, keepdims=True)
    table = np.zeros((n, LANES), np.float32)
    table[:, :n] = np.linalg.matrix_power(kernel, SMOOTH_PASSES).T
    return table


def call(body, out_shape, in_specs, out_specs, scratch=(), flops=0, moved=0):
    return pl.pallas_call(
        body,
        out_shape=out_shape,
        in_specs=in_specs,
        out_specs=out_specs,
        scratch_shapes=scratch,
        compiler_params=pltpu.CompilerParams(vmem_limit_bytes=VMEM_LIMIT),
        cost_estimate=pl.CostEstimate(flops=flops, bytes_accessed=moved, transcendentals=0),
    )


def local(sections, boundary, row_shift, row_frac, col_shift, col_frac, peak_shift):
    section = sections[0]
    n_rows, n_cols = section.shape
    n_ty, n_gz = lax.axis_size("ty"), lax.axis_size("gz")
    patch_rows, patch_cols = n_rows // PATCH, n_cols // PATCH
    n_patches = patch_rows * patch_cols
    all_rows = n_rows * n_ty
    n_mid, half = n_rows - 2 * MARGIN, n_rows // 2
    n_blocks = n_cols // BLOCK
    vmem = pl.BlockSpec(memory_space=pltpu.VMEM)
    smem = pl.BlockSpec(memory_space=pltpu.SMEM)
    hbm = pl.BlockSpec(memory_space=pltpu.HBM)
    unread = pl.BlockSpec(memory_space=pl.ANY)
    shape = jax.ShapeDtypeStruct
    to_next = [(i, (i + 1) % n_gz) for i in range(n_gz)]

    swaps, tables = [], []
    for d in range(-(-2 * SMOOTH_PASSES // patch_rows), 0, -1):
        for other in (False, True):
            if has_partners(n_ty, d, other):
                swaps.append((d, other))
                tables.append(swap_table(n_gz, n_ty, d, other))

    held, send_first, mid_table, first_table, second_table, col_table = call(
        functools.partial(fetch_kernel, all_rows),
        (
            shape((n_rows, n_cols), bf16),
            shape((MARGIN, n_cols), bf16),
            shape((n_mid, n_rows), bf16),
            shape((MARGIN, MARGIN + half), bf16),
            shape((MARGIN, MARGIN + half), bf16),
            shape((n_blocks, BLOCK + 2 * LANES, BLOCK), bf16),
        ),
        [hbm] * 5,
        [vmem] * 6,
        [
            pltpu.VMEM((1, n_rows), jnp.int32),
            pltpu.VMEM((1, n_rows), jnp.int32),
            pltpu.VMEM((1, n_cols), jnp.int32),
            pltpu.VMEM((1, n_cols), jnp.int32),
            pltpu.SemaphoreType.DMA((6,)),
        ],
    )(*(pltpu.with_memory_space_constraint(x, pltpu.HBM) for x in (section, row_shift, row_frac, col_shift, col_frac)))
    first = lax.ppermute(send_first, ("gz", "ty"), swap_table(n_gz, n_ty, 1, False))

    mid, send_second = call(
        middle_kernel,
        (shape((n_mid, n_cols), bf16), shape((MARGIN, n_cols), bf16)),
        [vmem] * 3,
        [vmem] * 2,
        [pltpu.VMEM((n_mid, n_cols + 2 * LANES), bf16)],
    )(held, mid_table, col_table)
    old_mid = lax.ppermute(mid, "gz", to_next)
    second = lax.ppermute(send_second, ("gz", "ty"), swap_table(n_gz, n_ty, 1, True))

    terms = (len(swaps) + 1) * 2 * patch_rows
    turned_mid, bands, peak, row_weights = call(
        functools.partial(turn_middle_kernel, n_ty, tuple(swaps)),
        (
            shape((3 * n_patches, MARGIN, LANES), bf16),
            shape((n_patches, PATCH // 8, LANES), f32),
            shape((2, n_patches, LANES), f32),
            shape((terms, 8, LANES), f32),
        ),
        [smem, vmem],
        [vmem] * 4,
        flops=1_000_000_000,
        moved=3_000_000,
    )(peak_shift, mid)

    def render_edges(which, *args):
        return call(
            functools.partial(edges_kernel, which),
            shape((MARGIN, n_cols), bf16),
            [vmem] * 4 + [unread] * (len(args) - 4),
            vmem,
            [pltpu.VMEM((MARGIN, n_cols + 2 * LANES), bf16)],
        )(*args)

    turned_shape = shape((3 * patch_cols, MARGIN, LANES), bf16)
    first_edge = render_edges(False, first, held, first_table, col_table)
    old_first = lax.ppermute(first_edge, "gz", to_next)
    turned_first = call(
        functools.partial(turn_first_kernel, patch_rows),
        turned_shape,
        [smem, vmem],
        vmem,
        flops=500_000_000,
        moved=1_000_000,
    )(peak_shift, first_edge)
    second_edge = render_edges(True, second, held, second_table, col_table, first_edge)
    old_second = lax.ppermute(second_edge, "gz", to_next)
    rendered, turned_second = call(
        functools.partial(turn_second_kernel, patch_rows),
        (shape((n_rows, n_cols), bf16), turned_shape),
        [smem] + [vmem] * 3,
        [hbm, vmem],
        [pltpu.SemaphoreType.DMA((3,))],
        flops=1_000_000_000,
        moved=3_000_000,
    )(peak_shift, mid, first_edge, second_edge)

    smooth = jnp.asarray(column_smoother(patch_cols))
    acc = pltpu.VMEM((9 * patch_cols * 8, LANES), f32)
    payload = call(
        boundary_kernel,
        shape((8, LANES), f32),
        [vmem] * 5 + [hbm, vmem],
        vmem,
        [acc, pltpu.VMEM((n_rows, n_cols), bf16), pltpu.SemaphoreType.DMA],
        flops=1_000_000_000,
        moved=3_000_000,
    )(turned_mid, turned_first, turned_second, bands, peak, boundary, smooth)
    for which, turned, old in ((False, turned_first, old_first), (True, turned_second, old_second)):
        payload = call(
            functools.partial(window_kernel, which), shape((8, LANES), f32), [vmem] * 8, vmem, [acc]
        )(turned_mid, turned, bands, peak, old_mid, old, smooth, payload)
    blocks = [payload] + [lax.ppermute(payload, ("gz", "ty"), table) for table in tables]
    flow = call(
        rows_kernel, shape((2, 1, patch_rows, patch_cols), f32), [vmem] * (1 + len(blocks)), vmem
    )(row_weights, *blocks)
    return rendered[None], flow


def solution(mesh):
    in_specs = (
        P(("parts", "gz"), "ty", None),
        P(("parts", "ty"), None),
        P(("parts", "gz"), "ty"),
        P(("parts", "gz"), "ty"),
        P(("parts", "gz"), None),
        P(("parts", "gz"), None),
        P(None, ("parts", "gz"), "ty", None),
    )
    out_specs = (P(("parts", "gz"), "ty", None), P(None, ("parts", "gz"), "ty", None))
    return jax.shard_map(local, mesh=mesh, in_specs=in_specs, out_specs=out_specs, check_vma=False)
```

```python
import functools

import jax
import jax.numpy as jnp
import numpy as np
from jax import lax
from jax.experimental import pallas as pl
from jax.experimental.pallas import tpu as pltpu
from jax.sharding import PartitionSpec as P

PATCH = 128
MARGIN = 64
SMOOTH_PASSES = 2
BLOCK = 256
LANES = 128
TAPS = (0.0625, 0.25, 0.375, 0.25, 0.0625)
FAR = 1 << 20
VMEM_LIMIT = 16 * 1024 * 1024
TURN_UNROLL = 16
PLAN_UNROLL = 8
EARLY_BLOCKS = 5 / 8

f32 = jnp.float32
bf16 = jnp.bfloat16


def swap_table(n_gz, n_ty, d, second):
    table = []
    for z in range(n_gz):
        for t in range(n_ty):
            partner = t + d if ((t // d) % 2 == 0) != second else t - d
            if 0 <= partner < n_ty:
                table.append((z * n_ty + t, z * n_ty + partner))
            elif (z ^ 1) < n_gz:
                table.append((z * n_ty + t, (z ^ 1) * n_ty + t))
    return tuple(table)


def halo_table(n_parts, n_gz, n_ty, second):
    table = []
    for p in range(n_parts):
        for z in range(n_gz):
            for t in range(n_ty):
                partner = t + 1 if (t % 2 == 0) != (second != (z % 2 == 1)) else t - 1
                if 0 <= partner < n_ty:
                    there = (p, z, partner)
                elif (p ^ 1) < n_parts:
                    there = (p ^ 1, z, t)
                else:
                    continue
                table.append(tuple((a * n_gz + b) * n_ty + c for a, b, c in ((p, z, t), there)))
    return tuple(table)


def partner_of(tile, d, second):
    up = (tile // d) % 2 == int(second)
    return tile + jnp.where(up, d, -d)


def has_partners(n_ty, d, second):
    return any(((t // d) % 2 == 0) != second and t + d < n_ty for t in range(n_ty))


def takes_bottom(second):
    return (lax.axis_index("ty") + lax.axis_index("gz")) % 2 == int(second)


def hat(coord, position):
    return jnp.maximum(1.0 - jnp.abs(coord - position), 0.0)


def source_positions(ids, shift, frac, limit, base):
    source = jnp.clip(ids + shift, 0, limit) - base
    return source.astype(f32) + frac.astype(f32) * (1.0 / 256.0)


def times(left, right):
    return jnp.dot(left, right, preferred_element_type=f32).astype(bf16)


def build_tables(col_pos, first, tables):
    reach = BLOCK + LANES
    coord = lax.broadcasted_iota(jnp.int32, (reach, BLOCK), 0).astype(f32) - float(LANES // 2)
    edge = jnp.zeros((LANES // 2, BLOCK), bf16)

    @pl.loop(0, tables.shape[0])
    def _(k):
        at = pl.multiple_of((first + k) * BLOCK, BLOCK)
        pos = col_pos[:, pl.ds(at, BLOCK)] - at.astype(f32)
        tables[k, 0 : LANES // 2, :] = edge
        tables[k, LANES // 2 : LANES // 2 + reach, :] = hat(coord, pos).astype(bf16)
        tables[k, LANES // 2 + reach :, :] = edge


def fetch_kernel(all_rows, section, row_shift, row_frac, col_shift, col_frac, *rest):
    send_first, held, row_pos, col_pos, tables = rest[:5]
    row_shift_v, row_frac_v, col_shift_v, col_frac_v, sems = rest[5:]
    n_rows, n_cols = section.shape
    base = lax.axis_index("ty") * n_rows
    at = pl.multiple_of(jnp.where(takes_bottom(False), n_rows - MARGIN, 0), MARGIN)
    copies = [
        pltpu.make_async_copy(source, target, sems.at[k])
        for k, (source, target) in enumerate(
            (
                (col_shift, col_shift_v),
                (col_frac, col_frac_v),
                (row_shift, row_shift_v),
                (row_frac, row_frac_v),
                (section.at[pl.ds(at, MARGIN), :], send_first),
                (section, held),
            )
        )
    ]
    for copy in copies:
        copy.start()
    for copy in copies[:4]:
        copy.wait()
    ids = lax.broadcasted_iota(jnp.int32, (1, n_cols), 1)
    col_pos[...] = source_positions(ids, col_shift_v[...], col_frac_v[...], n_cols - 2, 0)
    ids = lax.broadcasted_iota(jnp.int32, (1, n_rows), 1) + base
    row_pos[...] = source_positions(ids, row_shift_v[...], row_frac_v[...], all_rows - 2, base)
    build_tables(col_pos, 0, tables)
    for copy in copies[4:]:
        copy.wait()


def columns_of(mix, tables, out_ref):
    j = 0
    for table in tables:
        for k in range(table.shape[0]):
            out_ref[:, j * BLOCK : (j + 1) * BLOCK] = times(
                mix[:, j * BLOCK : (j + 1) * BLOCK + 2 * LANES], table[k]
            )
            j += 1


def clear_sides(mix):
    edge = jnp.zeros((mix.shape[0], LANES), bf16)
    mix[:, 0:LANES] = edge
    mix[:, mix.shape[1] - LANES :] = edge


def edge_table(second, row_pos, table):
    n_rows = row_pos.shape[1]
    half = n_rows // 2
    slot = lax.broadcasted_iota(jnp.int32, (MARGIN + half, MARGIN), 0)
    bottom = takes_bottom(second)
    start = jnp.where(
        slot < MARGIN, jnp.where(bottom, n_rows, -MARGIN), jnp.where(bottom, half - MARGIN, -MARGIN)
    )
    here = jnp.where(bottom, row_pos[:, n_rows - MARGIN :], row_pos[:, :MARGIN])
    table[...] = hat((slot + start).astype(f32), here).T.astype(bf16)


def middle_kernel(held, row_pos, col_pos, tables, mid_ref, more_tables, first_table, second_table, mix):
    n_rows, n_cols = held.shape
    build_tables(col_pos, tables.shape[0], more_tables)
    edge_table(False, row_pos, first_table)
    edge_table(True, row_pos, second_table)
    coord = lax.broadcasted_iota(jnp.int32, (n_rows, n_rows - 2 * MARGIN), 0).astype(f32)
    mid_table = hat(coord, row_pos[:, MARGIN : n_rows - MARGIN]).T.astype(bf16)
    clear_sides(mix)
    for j in range(n_cols // BLOCK):
        mix[:, LANES + j * BLOCK : LANES + (j + 1) * BLOCK] = times(
            mid_table, held[:, j * BLOCK : (j + 1) * BLOCK]
        )
    columns_of(mix, (tables, more_tables), mid_ref)


def send_kernel(held, _, send_second):
    n_rows = held.shape[0]
    at = pl.multiple_of(jnp.where(takes_bottom(True), n_rows - MARGIN, 0), MARGIN)
    send_second[...] = held[pl.ds(at, MARGIN), :]


def edges_kernel(second, halo, held, table, tables, more_tables, *rest):
    edge_ref, mix = rest[-2:]
    n_rows, n_cols = held.shape
    half = n_rows // 2
    own = pl.ds(pl.multiple_of(jnp.where(takes_bottom(second), half, 0), half), half)
    clear_sides(mix)
    for j in range(n_cols // BLOCK):
        here = slice(j * BLOCK, (j + 1) * BLOCK)
        stack = jnp.concatenate([halo[:, here], held[own, here]], axis=0)
        mix[:, LANES + j * BLOCK : LANES + (j + 1) * BLOCK] = times(table[...], stack)
    columns_of(mix, (tables, more_tables), edge_ref)


def turn_patches(peaks, i, rows, source, turned, first):
    patch_cols = source.shape[1] // PATCH
    n_turned = turned.shape[0] // 3

    @pl.loop(0, patch_cols, unroll=TURN_UNROLL)
    def _(j):
        block = source[rows, pl.ds(pl.multiple_of(j * PATCH, PATCH), PATCH)]
        for dx in range(3):
            turned[dx * n_turned + first + j] = pltpu.roll(block, (peaks[1, 0, i, j] + (dx - 1)) % PATCH, 1)


def plan_windows(peaks, bands, peak):
    lane = lax.broadcasted_iota(jnp.int32, (PATCH // 8, LANES), 1)
    offset = lane - 8 * lax.broadcasted_iota(jnp.int32, (PATCH // 8, LANES), 0) + 1
    patch_rows, patch_cols = peaks.shape[2:]
    for i in range(patch_rows):

        @pl.loop(0, patch_cols, unroll=PLAN_UNROLL)
        def _(j):
            p = i * patch_cols + j
            bands[p] = jnp.where(((offset - peaks[0, 0, i, j]) & (PATCH - 1)) <= 9, 1.0, 0.0)
            for c in range(2):
                peak[c, pl.ds(p, 1), :] = jnp.full((1, LANES), peaks[c, 0, i, j], jnp.int32).astype(f32)


def turn_middle_kernel(peaks, mid, turned):
    for i in range(mid.shape[0] // MARGIN):
        turn_patches(peaks, i, slice(i * MARGIN, (i + 1) * MARGIN), mid, turned, i * (mid.shape[1] // PATCH))


def edge_patch_row(second, patch_rows):
    return jnp.where(takes_bottom(second), patch_rows - 1, 0)


def turn_first_kernel(patch_rows, peaks, edge, turned):
    turn_patches(peaks, edge_patch_row(False, patch_rows), slice(None), edge, turned, 0)


def patch_row_flow(i, turned_edge, turned_mid, bands, peak, smooth, old_of, acc):
    patch_cols = turned_edge.shape[0] // 3
    n_patches = bands.shape[0]
    lane = lax.broadcasted_iota(jnp.int32, (8, LANES), 1) - lax.broadcasted_iota(jnp.int32, (8, LANES), 0)
    for j in range(patch_cols):
        p = i * patch_cols + j
        left = []
        for dx in range(3):
            left += [turned_edge[dx * patch_cols + j], turned_mid[dx * n_patches + p]]
        products = lax.dot_general(
            jnp.concatenate(left, axis=0), old_of(j), (((1,), (1,)), ((), ())), preferred_element_type=f32
        )
        band = bands[p]
        place = (lane - peak[0, pl.ds(p, 1), :].astype(jnp.int32)) & 15
        for dx in range(3):
            lines = [
                products[dx * PATCH + 8 * r : dx * PATCH + 8 * r + 8, :] * band[r : r + 1, :]
                for r in range(PATCH // 8)
            ]
            even, odd = sum(lines[2::2], lines[0]), sum(lines[3::2], lines[1])
            for dy in range(3):
                at = ((dy * 3 + dx) * patch_cols + j) * 8
                acc[at : at + 8, :] = jnp.where(place == (dy - 1) % 16, even, 0.0) + jnp.where(
                    place == (dy + 7) % 16, odd, 0.0
                )
    total = acc[pl.ds(0, 9 * patch_cols, stride=8), :]
    for s in range(1, 8):
        total = total + acc[pl.ds(s, 9 * patch_cols, stride=8), :]
    weights = jnp.maximum(jnp.sum(total, axis=1, keepdims=True) * (1.0 / PATCH), 0.0)
    w = [weights[k * patch_cols : (k + 1) * patch_cols] for k in range(9)]
    scale = 1.0 / jnp.maximum(sum(w), 1.0)
    moves = (
        (w[6] + w[7] + w[8] - w[0] - w[1] - w[2]) * scale,
        (w[2] + w[5] + w[8] - w[0] - w[3] - w[6]) * scale,
    )
    here = pl.ds(pl.multiple_of(i * patch_cols, patch_cols), patch_cols)
    return [jnp.sum((moves[c] + peak[c, here, :]) * smooth[...], axis=0, keepdims=True) for c in range(2)]


def put_lines(lines, i, patch_rows):
    at = lax.broadcasted_iota(jnp.int32, (8, LANES), 0)
    return sum(jnp.where(at == c * patch_rows + i, line, 0.0) for c, line in enumerate(lines))


def waiting_kernel(n_ty, swaps, peaks, mid, first, second, turned_mid, turned_first, boundary, smooth, _, *rest):
    rendered, turned_second, bands, peak, row_weights, flow, acc, whole, sems = rest
    n_rows = boundary.shape[0]
    patch_rows = n_rows // PATCH
    moves = [(mid, pl.ds(MARGIN, mid.shape[0]))]
    for edge, which in ((first, False), (second, True)):
        at = pl.multiple_of(jnp.where(takes_bottom(which), n_rows - MARGIN, 0), MARGIN)
        moves.append((edge, pl.ds(at, MARGIN)))
    copies = [pltpu.make_async_copy(a, rendered.at[b, :], sems.at[k]) for k, (a, b) in enumerate(moves)]
    fetch = pltpu.make_async_copy(boundary, whole, sems.at[len(moves)])
    has_boundary = lax.axis_index("gz") == 0

    @pl.when(has_boundary)
    def _():
        fetch.start()

    for copy in copies:
        copy.start()
    flow[...] = jnp.zeros_like(flow)
    turn_patches(peaks, edge_patch_row(True, patch_rows), slice(None), second, turned_second, 0)
    plan_windows(peaks, bands, peak)
    fill_row_weights(n_ty, swaps, patch_rows, row_weights)

    @pl.when(has_boundary)
    def _():
        fetch.wait()

        @pl.loop(0, patch_rows)
        def _(k):
            i = jnp.where(k == 0, edge_patch_row(False, patch_rows), edge_patch_row(True, patch_rows))
            at_edge = pl.multiple_of(i * (n_rows - MARGIN), MARGIN)
            at_mid = pl.multiple_of(MARGIN + i * MARGIN, MARGIN)

            def old_of(j):
                cols = slice(j * PATCH, (j + 1) * PATCH)
                return jnp.concatenate([whole[pl.ds(at_edge, MARGIN), cols], whole[pl.ds(at_mid, MARGIN), cols]], axis=0)

            def flow_with(turned_edge):
                flow[...] += put_lines(
                    patch_row_flow(i, turned_edge, turned_mid, bands, peak, smooth, old_of, acc), i, patch_rows
                )

            @pl.when(k == 0)
            def _():
                flow_with(turned_first)

            @pl.when(k != 0)
            def _():
                flow_with(turned_second)

    for copy in copies:
        copy.wait()


def window_kernel(second, turned_mid, turned_edge, bands, peak, old_mid, old_edge, smooth, before, out_ref, acc):
    patch_rows = old_mid.shape[0] // MARGIN
    out_ref[...] = before[...]

    @pl.when(lax.axis_index("gz") != 0)
    def _():
        i = edge_patch_row(second, patch_rows)
        at_mid = pl.multiple_of(i * MARGIN, MARGIN)

        def old_of(j):
            cols = slice(j * PATCH, (j + 1) * PATCH)
            return jnp.concatenate([old_edge[:, cols], old_mid[pl.ds(at_mid, MARGIN), cols]], axis=0)

        lines = patch_row_flow(i, turned_edge, turned_mid, bands, peak, smooth, old_of, acc)
        out_ref[...] = before[...] + put_lines(lines, i, patch_rows)


def fill_row_weights(n_ty, swaps, patch_rows, out_ref):
    all_rows = n_ty * patch_rows
    tile = lax.axis_index("ty")
    held = 2 * patch_rows
    depth = LANES
    at = lax.broadcasted_iota(jnp.int32, (8, depth), 0)
    slot = lax.broadcasted_iota(jnp.int32, (8, depth), 1)
    holder = jnp.full((8, depth), tile, jnp.int32)
    for k, (d, second) in enumerate(swaps):
        holder = jnp.where((slot >> 3) == k + 1, partner_of(tile, d, second), holder)
    inner = slot & 7
    c_out = (at >= patch_rows).astype(jnp.int32)
    c_in = (inner >= patch_rows).astype(jnp.int32)
    row = tile * patch_rows + at - c_out * patch_rows
    source = holder * patch_rows + inner - c_in * patch_rows

    def inside(r):
        return (r >= 0) & (r < all_rows)

    def tap(delta):
        size = jnp.abs(delta)
        return jnp.where(
            size == 0, TAPS[2], jnp.where(size == 1, TAPS[1], jnp.where(size == 2, TAPS[0], 0.0))
        )

    def norm(r):
        return sum(jnp.where(inside(r + o), TAPS[o + 2], 0.0) for o in range(-2, 3))

    weight = jnp.zeros((8, depth), f32)
    for o in range(-2, 3):
        weight = weight + jnp.where(inside(row + o), TAPS[o + 2] * tap(source - row - o) / norm(row + o), 0.0)
    used = (inner < held) & (at < held) & (c_in == c_out) & inside(source)
    weight = jnp.where(used, weight / norm(row), 0.0)
    for k in range(len(swaps) + 1):
        for b in range(held):
            out_ref[k * held + b] = jnp.broadcast_to(weight[:, 8 * k + b : 8 * k + b + 1], (8, LANES))


def rows_kernel(row_weights, *refs):
    blocks, out_ref = refs[:-1], refs[-1]
    patch_rows, patch_cols = out_ref.shape[2], out_ref.shape[3]
    held = 2 * patch_rows
    result = None
    for k, block in enumerate(blocks):
        for b in range(held):
            term = row_weights[k * held + b] * block[b : b + 1, :]
            result = term if result is None else result + term
    for c in range(2):
        out_ref[c, 0] = result[c * patch_rows : (c + 1) * patch_rows, :patch_cols]


def column_smoother(n):
    kernel = np.zeros((n, n))
    for i in range(n):
        for o in range(-2, 3):
            if 0 <= i + o < n:
                kernel[i, i + o] = TAPS[o + 2]
    kernel = kernel / kernel.sum(1, keepdims=True)
    table = np.zeros((n, LANES), np.float32)
    table[:, :n] = np.linalg.matrix_power(kernel, SMOOTH_PASSES).T
    return table


def call(body, out_shape, in_specs, out_specs, scratch=(), flops=0, moved=0):
    return pl.pallas_call(
        body,
        out_shape=out_shape,
        in_specs=in_specs,
        out_specs=out_specs,
        scratch_shapes=scratch,
        compiler_params=pltpu.CompilerParams(vmem_limit_bytes=VMEM_LIMIT),
        cost_estimate=pl.CostEstimate(flops=flops, bytes_accessed=moved, transcendentals=0),
    )


def in_hbm(x):
    return pltpu.with_memory_space_constraint(x, pltpu.HBM)


def local(sections, boundary, row_shift, row_frac, col_shift, col_frac, peak_shift):
    section = sections[0]
    n_rows, n_cols = section.shape
    n_ty, n_gz, n_parts = lax.axis_size("ty"), lax.axis_size("gz"), lax.axis_size("parts")
    patch_rows, patch_cols = n_rows // PATCH, n_cols // PATCH
    n_patches = patch_rows * patch_cols
    all_rows = n_rows * n_ty
    n_mid, half = n_rows - 2 * MARGIN, n_rows // 2
    n_blocks = n_cols // BLOCK
    vmem = pl.BlockSpec(memory_space=pltpu.VMEM)
    smem = pl.BlockSpec(memory_space=pltpu.SMEM)
    hbm = pl.BlockSpec(memory_space=pltpu.HBM)
    unread = pl.BlockSpec(memory_space=pl.ANY)
    shape = jax.ShapeDtypeStruct
    to_next = [(i, (i + 1) % n_gz) for i in range(n_gz)]

    swaps, routes = [], []
    for d in range(-(-2 * SMOOTH_PASSES // patch_rows), 0, -1):
        for other in (False, True):
            if has_partners(n_ty, d, other):
                swaps.append((d, other))
                routes.append(swap_table(n_gz, n_ty, d, other))

    early = max(1, min(n_blocks - 1, int(n_blocks * EARLY_BLOCKS)))
    window = BLOCK + 2 * LANES
    send_first, held, row_pos, col_pos, tables = call(
        functools.partial(fetch_kernel, all_rows),
        (
            shape((MARGIN, n_cols), bf16),
            shape((n_rows, n_cols), bf16),
            shape((1, n_rows), f32),
            shape((1, n_cols), f32),
            shape((early, window, BLOCK), bf16),
        ),
        [hbm] * 5,
        [vmem] * 5,
        [
            pltpu.VMEM((1, n_rows), jnp.int32),
            pltpu.VMEM((1, n_rows), jnp.int32),
            pltpu.VMEM((1, n_cols), jnp.int32),
            pltpu.VMEM((1, n_cols), jnp.int32),
            pltpu.SemaphoreType.DMA((6,)),
        ],
    )(*(in_hbm(x) for x in (section, row_shift, row_frac, col_shift, col_frac)))
    first = lax.ppermute(send_first, ("parts", "gz", "ty"), halo_table(n_parts, n_gz, n_ty, False))

    edge_shape = shape((MARGIN, MARGIN + half), bf16)
    mid, more_tables, first_table, second_table = call(
        middle_kernel,
        (shape((n_mid, n_cols), bf16), shape((n_blocks - early, window, BLOCK), bf16), edge_shape, edge_shape),
        [vmem] * 4,
        [vmem] * 4,
        [pltpu.VMEM((n_mid, n_cols + 2 * LANES), bf16)],
    )(held, row_pos, col_pos, tables)
    old_mid = lax.ppermute(mid, "gz", to_next)
    turned_mid = call(
        turn_middle_kernel,
        shape((3 * n_patches, MARGIN, LANES), bf16),
        [smem, vmem],
        vmem,
        flops=1_000_000_000,
        moved=3_000_000,
    )(peak_shift, mid)

    send_second = call(send_kernel, shape((MARGIN, n_cols), bf16), [vmem, unread], vmem, flops=4_000_000_000)(
        held, turned_mid
    )
    second = lax.ppermute(send_second, ("parts", "gz", "ty"), halo_table(n_parts, n_gz, n_ty, True))
    def render_edges(which, *args):
        return call(
            functools.partial(edges_kernel, which),
            shape((MARGIN, n_cols), bf16),
            [vmem] * 5 + [unread] * (len(args) - 5),
            vmem,
            [pltpu.VMEM((MARGIN, n_cols + 2 * LANES), bf16)],
        )(*args)

    turned_shape = shape((3 * patch_cols, MARGIN, LANES), bf16)
    first_edge = render_edges(False, first, held, first_table, tables, more_tables, send_second)
    old_first = lax.ppermute(first_edge, "gz", to_next)
    turned_first = call(
        functools.partial(turn_first_kernel, patch_rows),
        turned_shape,
        [smem, vmem],
        vmem,
        flops=500_000_000,
        moved=1_000_000,
    )(peak_shift, first_edge)
    second_edge = render_edges(True, second, held, second_table, tables, more_tables, turned_first)
    old_second = lax.ppermute(second_edge, "gz", to_next)
    smooth = jnp.asarray(column_smoother(patch_cols))
    acc = pltpu.VMEM((9 * patch_cols * 8, LANES), f32)
    terms = (len(swaps) + 1) * 2 * patch_rows
    rendered, turned_second, bands, peak, row_weights, payload = call(
        functools.partial(waiting_kernel, n_ty, tuple(swaps)),
        (
            shape((n_rows, n_cols), bf16),
            turned_shape,
            shape((n_patches, PATCH // 8, LANES), f32),
            shape((2, n_patches, LANES), f32),
            shape((terms, 8, LANES), f32),
            shape((8, LANES), f32),
        ),
        [smem] + [vmem] * 5 + [hbm, vmem, unread],
        [hbm] + [vmem] * 5,
        [acc, pltpu.VMEM((n_rows, n_cols), bf16), pltpu.SemaphoreType.DMA((4,))],
        flops=1_000_000_000,
        moved=3_000_000,
    )(peak_shift, mid, first_edge, second_edge, turned_mid, turned_first, in_hbm(boundary), smooth, old_mid)
    for which, turned, old in ((True, turned_second, old_first), (False, turned_first, old_second)):
        payload = call(
            functools.partial(window_kernel, which), shape((8, LANES), f32), [vmem] * 8, vmem, [acc]
        )(turned_mid, turned, bands, peak, old_mid, old, smooth, payload)
    blocks = [payload] + [lax.ppermute(payload, ("gz", "ty"), route) for route in routes]
    flow = call(
        rows_kernel, shape((2, 1, patch_rows, patch_cols), f32), [vmem] * (1 + len(blocks)), vmem
    )(row_weights, *blocks)
    return rendered[None], flow


def solution(mesh):
    in_specs = (
        P(("parts", "gz"), "ty", None),
        P(("parts", "ty"), None),
        P(("parts", "gz"), "ty"),
        P(("parts", "gz"), "ty"),
        P(("parts", "gz"), None),
        P(("parts", "gz"), None),
        P(None, ("parts", "gz"), "ty", None),
    )
    out_specs = (P(("parts", "gz"), "ty", None), P(None, ("parts", "gz"), "ty", None))
    return jax.shard_map(local, mesh=mesh, in_specs=in_specs, out_specs=out_specs, check_vma=False)
```

```python
import functools

import jax
import jax.numpy as jnp
import numpy as np
from jax import lax
from jax.experimental import pallas as pl
from jax.experimental.pallas import tpu as pltpu
from jax.sharding import PartitionSpec as P

PATCH = 128
MARGIN = 64
SMOOTH_PASSES = 2
BLOCK = 256
LANES = 128
TAPS = (0.0625, 0.25, 0.375, 0.25, 0.0625)
FAR = 1 << 20
VMEM_LIMIT = 16 * 1024 * 1024
TURN_UNROLL = 16
PLAN_UNROLL = 8
EARLY_BLOCKS = 7 / 8
EDGE_PARTS = 2

f32 = jnp.float32
bf16 = jnp.bfloat16


def swap_table(n_gz, n_ty, d, second):
    table = []
    for z in range(n_gz):
        for t in range(n_ty):
            partner = t + d if ((t // d) % 2 == 0) != second else t - d
            if 0 <= partner < n_ty:
                table.append((z * n_ty + t, z * n_ty + partner))
            elif (z ^ 1) < n_gz:
                table.append((z * n_ty + t, (z ^ 1) * n_ty + t))
    return tuple(table)


def halo_table(n_parts, n_gz, n_ty, second):
    table = []
    for p in range(n_parts):
        for z in range(n_gz):
            for t in range(n_ty):
                partner = t + 1 if (t % 2 == 0) != (second != (z % 2 == 1)) else t - 1
                if 0 <= partner < n_ty:
                    there = (p, z, partner)
                elif (p ^ 1) < n_parts:
                    there = (p ^ 1, z, t)
                else:
                    continue
                table.append(tuple((a * n_gz + b) * n_ty + c for a, b, c in ((p, z, t), there)))
    return tuple(table)


def partner_of(tile, d, second):
    up = (tile // d) % 2 == int(second)
    return tile + jnp.where(up, d, -d)


def has_partners(n_ty, d, second):
    return any(((t // d) % 2 == 0) != second and t + d < n_ty for t in range(n_ty))


def takes_bottom(second):
    return (lax.axis_index("ty") + lax.axis_index("gz")) % 2 == int(second)


def hat(coord, position):
    return jnp.maximum(1.0 - jnp.abs(coord - position), 0.0)


def source_positions(ids, shift, frac, limit, base):
    source = jnp.clip(ids + shift, 0, limit) - base
    return source.astype(f32) + frac.astype(f32) * (1.0 / 256.0)


def times(left, right):
    return jnp.dot(left, right, preferred_element_type=f32).astype(bf16)


def build_tables(col_pos, first, tables):
    reach = BLOCK + LANES
    coord = lax.broadcasted_iota(jnp.int32, (reach, BLOCK), 0).astype(f32) - float(LANES // 2)
    edge = jnp.zeros((LANES // 2, BLOCK), bf16)

    @pl.loop(0, tables.shape[0])
    def _(k):
        at = pl.multiple_of((first + k) * BLOCK, BLOCK)
        pos = col_pos[:, pl.ds(at, BLOCK)] - at.astype(f32)
        tables[k, 0 : LANES // 2, :] = edge
        tables[k, LANES // 2 : LANES // 2 + reach, :] = hat(coord, pos).astype(bf16)
        tables[k, LANES // 2 + reach :, :] = edge


def fetch_kernel(all_rows, section, row_shift, row_frac, col_shift, col_frac, *rest):
    send_first, held, row_pos, col_pos, tables = rest[:5]
    row_shift_v, row_frac_v, col_shift_v, col_frac_v, sems = rest[5:]
    n_rows, n_cols = section.shape
    base = lax.axis_index("ty") * n_rows
    at = pl.multiple_of(jnp.where(takes_bottom(False), n_rows - MARGIN, 0), MARGIN)
    copies = [
        pltpu.make_async_copy(source, target, sems.at[k])
        for k, (source, target) in enumerate(
            (
                (col_shift, col_shift_v),
                (col_frac, col_frac_v),
                (row_shift, row_shift_v),
                (row_frac, row_frac_v),
                (section.at[pl.ds(at, MARGIN), :], send_first),
                (section, held),
            )
        )
    ]
    for copy in copies:
        copy.start()
    for copy in copies[:4]:
        copy.wait()
    ids = lax.broadcasted_iota(jnp.int32, (1, n_cols), 1)
    col_pos[...] = source_positions(ids, col_shift_v[...], col_frac_v[...], n_cols - 2, 0)
    ids = lax.broadcasted_iota(jnp.int32, (1, n_rows), 1) + base
    row_pos[...] = source_positions(ids, row_shift_v[...], row_frac_v[...], all_rows - 2, base)
    build_tables(col_pos, 0, tables)
    for copy in copies[4:]:
        copy.wait()


def columns_of(mix, tables, *out_refs):
    j = 0
    wide = out_refs[0].shape[1] // BLOCK
    for table in tables:
        for k in range(table.shape[0]):
            at = j % wide
            out_refs[j // wide][:, at * BLOCK : (at + 1) * BLOCK] = times(
                mix[:, j * BLOCK : (j + 1) * BLOCK + 2 * LANES], table[k]
            )
            j += 1


def clear_sides(mix):
    edge = jnp.zeros((mix.shape[0], LANES), bf16)
    mix[:, 0:LANES] = edge
    mix[:, mix.shape[1] - LANES :] = edge


def edge_table(second, row_pos, table):
    n_rows = row_pos.shape[1]
    half = n_rows // 2
    slot = lax.broadcasted_iota(jnp.int32, (MARGIN + half, MARGIN), 0)
    bottom = takes_bottom(second)
    start = jnp.where(
        slot < MARGIN, jnp.where(bottom, n_rows, -MARGIN), jnp.where(bottom, half - MARGIN, -MARGIN)
    )
    here = jnp.where(bottom, row_pos[:, n_rows - MARGIN :], row_pos[:, :MARGIN])
    table[...] = hat((slot + start).astype(f32), here).T.astype(bf16)


def middle_kernel(held, row_pos, col_pos, tables, mid_ref, more_tables, first_table, second_table, mix):
    n_rows, n_cols = held.shape
    build_tables(col_pos, tables.shape[0], more_tables)
    edge_table(False, row_pos, first_table)
    edge_table(True, row_pos, second_table)
    coord = lax.broadcasted_iota(jnp.int32, (n_rows, n_rows - 2 * MARGIN), 0).astype(f32)
    mid_table = hat(coord, row_pos[:, MARGIN : n_rows - MARGIN]).T.astype(bf16)
    clear_sides(mix)
    for j in range(n_cols // BLOCK):
        mix[:, LANES + j * BLOCK : LANES + (j + 1) * BLOCK] = times(
            mid_table, held[:, j * BLOCK : (j + 1) * BLOCK]
        )
    columns_of(mix, (tables, more_tables), mid_ref)


def send_kernel(held, _, send_second):
    n_rows = held.shape[0]
    at = pl.multiple_of(jnp.where(takes_bottom(True), n_rows - MARGIN, 0), MARGIN)
    send_second[...] = held[pl.ds(at, MARGIN), :]


def edges_kernel(second, parts, halo, held, table, tables, more_tables, *rest):
    edge_refs, mix = rest[-1 - parts : -1], rest[-1]
    n_rows, n_cols = held.shape
    half = n_rows // 2
    own = pl.ds(pl.multiple_of(jnp.where(takes_bottom(second), half, 0), half), half)
    clear_sides(mix)
    for j in range(n_cols // BLOCK):
        here = slice(j * BLOCK, (j + 1) * BLOCK)
        stack = jnp.concatenate([halo[:, here], held[own, here]], axis=0)
        mix[:, LANES + j * BLOCK : LANES + (j + 1) * BLOCK] = times(table[...], stack)
    columns_of(mix, (tables, more_tables), *edge_refs)


def turn_patches(peaks, i, rows, source, turned, first):
    patch_cols = source.shape[1] // PATCH
    n_turned = turned.shape[0] // 3
    first_col = first % peaks.shape[3]

    @pl.loop(0, patch_cols, unroll=min(TURN_UNROLL, patch_cols))
    def _(j):
        block = source[rows, pl.ds(pl.multiple_of(j * PATCH, PATCH), PATCH)]
        for dx in range(3):
            turned[dx * n_turned + first + j] = pltpu.roll(block, (peaks[1, 0, i, first_col + j] + (dx - 1)) % PATCH, 1)


def plan_windows(peaks, bands, peak):
    lane = lax.broadcasted_iota(jnp.int32, (PATCH // 8, LANES), 1)
    offset = lane - 8 * lax.broadcasted_iota(jnp.int32, (PATCH // 8, LANES), 0) + 1
    patch_rows, patch_cols = peaks.shape[2:]
    for i in range(patch_rows):

        @pl.loop(0, patch_cols, unroll=PLAN_UNROLL)
        def _(j):
            p = i * patch_cols + j
            bands[p] = jnp.where(((offset - peaks[0, 0, i, j]) & (PATCH - 1)) <= 9, 1.0, 0.0)
            for c in range(2):
                peak[c, pl.ds(p, 1), :] = jnp.full((1, LANES), peaks[c, 0, i, j], jnp.int32).astype(f32)


def turn_middle_kernel(peaks, mid, turned):
    for i in range(mid.shape[0] // MARGIN):
        turn_patches(peaks, i, slice(i * MARGIN, (i + 1) * MARGIN), mid, turned, i * (mid.shape[1] // PATCH))


def edge_patch_row(second, patch_rows):
    return jnp.where(takes_bottom(second), patch_rows - 1, 0)


def turn_first_kernel(patch_rows, peaks, edge, turned):
    turn_patches(peaks, edge_patch_row(False, patch_rows), slice(None), edge, turned, 0)


def patch_row_flow(i, cols, turned_edge, turned_mid, bands, peak, smooth, old_of, acc):
    patch_cols = turned_edge.shape[0] // 3
    n_patches = bands.shape[0]
    lane = lax.broadcasted_iota(jnp.int32, (8, LANES), 1) - lax.broadcasted_iota(jnp.int32, (8, LANES), 0)
    n_here = len(cols)
    for at_j, j in enumerate(cols):
        p = i * patch_cols + j
        left = []
        for dx in range(3):
            left += [turned_edge[dx * patch_cols + j], turned_mid[dx * n_patches + p]]
        products = lax.dot_general(
            jnp.concatenate(left, axis=0), old_of(j), (((1,), (1,)), ((), ())), preferred_element_type=f32
        )
        band = bands[p]
        place = (lane - peak[0, pl.ds(p, 1), :].astype(jnp.int32)) & 15
        for dx in range(3):
            lines = [
                products[dx * PATCH + 8 * r : dx * PATCH + 8 * r + 8, :] * band[r : r + 1, :]
                for r in range(PATCH // 8)
            ]
            even, odd = sum(lines[2::2], lines[0]), sum(lines[3::2], lines[1])
            for dy in range(3):
                at = ((dy * 3 + dx) * n_here + at_j) * 8
                acc[at : at + 8, :] = jnp.where(place == (dy - 1) % 16, even, 0.0) + jnp.where(
                    place == (dy + 7) % 16, odd, 0.0
                )
    total = acc[pl.ds(0, 9 * n_here, stride=8), :]
    for s in range(1, 8):
        total = total + acc[pl.ds(s, 9 * n_here, stride=8), :]
    weights = jnp.maximum(jnp.sum(total, axis=1, keepdims=True) * (1.0 / PATCH), 0.0)
    w = [weights[k * n_here : (k + 1) * n_here] for k in range(9)]
    scale = 1.0 / jnp.maximum(sum(w), 1.0)
    moves = (
        (w[6] + w[7] + w[8] - w[0] - w[1] - w[2]) * scale,
        (w[2] + w[5] + w[8] - w[0] - w[3] - w[6]) * scale,
    )
    here = pl.ds(pl.multiple_of(i * patch_cols + cols[0], 8), n_here)
    share = smooth[cols[0] : cols[0] + n_here, :]
    return [jnp.sum((moves[c] + peak[c, here, :]) * share, axis=0, keepdims=True) for c in range(2)]


def put_lines(lines, i, patch_rows):
    at = lax.broadcasted_iota(jnp.int32, (8, LANES), 0)
    return sum(jnp.where(at == c * patch_rows + i, line, 0.0) for c, line in enumerate(lines))


def waiting_kernel(n_ty, swaps, peaks, mid, first, *rest):
    seconds, rest = rest[:EDGE_PARTS], rest[EDGE_PARTS:]
    turned_mid, turned_first, boundary, smooth, _ = rest[:5]
    rendered, turned_second, bands, peak, row_weights, flow, acc, whole, sems = rest[5:]
    n_rows, n_cols = boundary.shape
    patch_rows = n_rows // PATCH
    moves = [(mid, pl.ds(MARGIN, mid.shape[0]), pl.ds(0, n_cols))]
    wide = n_cols // EDGE_PARTS
    for edge, which, start in [(first, False, 0)] + [(e, True, k * wide) for k, e in enumerate(seconds)]:
        at = pl.multiple_of(jnp.where(takes_bottom(which), n_rows - MARGIN, 0), MARGIN)
        moves.append((edge, pl.ds(at, MARGIN), pl.ds(start, edge.shape[1])))
    copies = [pltpu.make_async_copy(a, rendered.at[b, c], sems.at[k]) for k, (a, b, c) in enumerate(moves)]
    fetch = pltpu.make_async_copy(boundary, whole, sems.at[len(moves)])
    has_boundary = lax.axis_index("gz") == 0

    @pl.when(has_boundary)
    def _():
        fetch.start()

    for copy in copies:
        copy.start()
    flow[...] = jnp.zeros_like(flow)
    for k, edge in enumerate(seconds):
        turn_patches(peaks, edge_patch_row(True, patch_rows), slice(None), edge, turned_second, k * (wide // PATCH))
    plan_windows(peaks, bands, peak)
    fill_row_weights(n_ty, swaps, patch_rows, row_weights)

    @pl.when(has_boundary)
    def _():
        fetch.wait()

        @pl.loop(0, patch_rows)
        def _(k):
            i = jnp.where(k == 0, edge_patch_row(False, patch_rows), edge_patch_row(True, patch_rows))
            at_edge = pl.multiple_of(i * (n_rows - MARGIN), MARGIN)
            at_mid = pl.multiple_of(MARGIN + i * MARGIN, MARGIN)

            def old_of(j):
                cols = slice(j * PATCH, (j + 1) * PATCH)
                return jnp.concatenate([whole[pl.ds(at_edge, MARGIN), cols], whole[pl.ds(at_mid, MARGIN), cols]], axis=0)

            def flow_with(turned_edge):
                flow[...] += put_lines(
                    patch_row_flow(i, range(n_cols // PATCH), turned_edge, turned_mid, bands, peak, smooth, old_of, acc), i, patch_rows
                )

            @pl.when(k == 0)
            def _():
                flow_with(turned_first)

            @pl.when(k != 0)
            def _():
                flow_with(turned_second)

    for copy in copies:
        copy.wait()


def window_kernel(second, cols, turned_mid, turned_edge, bands, peak, old_mid, old_edge, smooth, before, out_ref, acc):
    patch_rows = old_mid.shape[0] // MARGIN
    out_ref[...] = before[...]

    @pl.when(lax.axis_index("gz") != 0)
    def _():
        i = edge_patch_row(second, patch_rows)
        at_mid = pl.multiple_of(i * MARGIN, MARGIN)

        def old_of(j):
            here = slice((j - cols[0]) * PATCH, (j - cols[0] + 1) * PATCH)
            there = slice(j * PATCH, (j + 1) * PATCH)
            return jnp.concatenate([old_edge[:, here], old_mid[pl.ds(at_mid, MARGIN), there]], axis=0)

        lines = patch_row_flow(i, cols, turned_edge, turned_mid, bands, peak, smooth, old_of, acc)
        out_ref[...] = before[...] + put_lines(lines, i, patch_rows)


def fill_row_weights(n_ty, swaps, patch_rows, out_ref):
    all_rows = n_ty * patch_rows
    tile = lax.axis_index("ty")
    held = 2 * patch_rows
    depth = LANES
    at = lax.broadcasted_iota(jnp.int32, (8, depth), 0)
    slot = lax.broadcasted_iota(jnp.int32, (8, depth), 1)
    holder = jnp.full((8, depth), tile, jnp.int32)
    for k, (d, second) in enumerate(swaps):
        holder = jnp.where((slot >> 3) == k + 1, partner_of(tile, d, second), holder)
    inner = slot & 7
    c_out = (at >= patch_rows).astype(jnp.int32)
    c_in = (inner >= patch_rows).astype(jnp.int32)
    row = tile * patch_rows + at - c_out * patch_rows
    source = holder * patch_rows + inner - c_in * patch_rows

    def inside(r):
        return (r >= 0) & (r < all_rows)

    def tap(delta):
        size = jnp.abs(delta)
        return jnp.where(
            size == 0, TAPS[2], jnp.where(size == 1, TAPS[1], jnp.where(size == 2, TAPS[0], 0.0))
        )

    def norm(r):
        return sum(jnp.where(inside(r + o), TAPS[o + 2], 0.0) for o in range(-2, 3))

    weight = jnp.zeros((8, depth), f32)
    for o in range(-2, 3):
        weight = weight + jnp.where(inside(row + o), TAPS[o + 2] * tap(source - row - o) / norm(row + o), 0.0)
    used = (inner < held) & (at < held) & (c_in == c_out) & inside(source)
    weight = jnp.where(used, weight / norm(row), 0.0)
    for k in range(len(swaps) + 1):
        for b in range(held):
            out_ref[k * held + b] = jnp.broadcast_to(weight[:, 8 * k + b : 8 * k + b + 1], (8, LANES))


def rows_kernel(row_weights, *refs):
    blocks, out_ref = refs[:-1], refs[-1]
    patch_rows, patch_cols = out_ref.shape[2], out_ref.shape[3]
    held = 2 * patch_rows
    result = None
    for k, block in enumerate(blocks):
        for b in range(held):
            term = row_weights[k * held + b] * block[b : b + 1, :]
            result = term if result is None else result + term
    for c in range(2):
        out_ref[c, 0] = result[c * patch_rows : (c + 1) * patch_rows, :patch_cols]


def column_smoother(n):
    kernel = np.zeros((n, n))
    for i in range(n):
        for o in range(-2, 3):
            if 0 <= i + o < n:
                kernel[i, i + o] = TAPS[o + 2]
    kernel = kernel / kernel.sum(1, keepdims=True)
    table = np.zeros((n, LANES), np.float32)
    table[:, :n] = np.linalg.matrix_power(kernel, SMOOTH_PASSES).T
    return table


def call(body, out_shape, in_specs, out_specs, scratch=(), flops=0, moved=0):
    return pl.pallas_call(
        body,
        out_shape=out_shape,
        in_specs=in_specs,
        out_specs=out_specs,
        scratch_shapes=scratch,
        compiler_params=pltpu.CompilerParams(vmem_limit_bytes=VMEM_LIMIT),
        cost_estimate=pl.CostEstimate(flops=flops, bytes_accessed=moved, transcendentals=0),
    )


def in_hbm(x):
    return pltpu.with_memory_space_constraint(x, pltpu.HBM)


def local(sections, boundary, row_shift, row_frac, col_shift, col_frac, peak_shift):
    section = sections[0]
    n_rows, n_cols = section.shape
    n_ty, n_gz, n_parts = lax.axis_size("ty"), lax.axis_size("gz"), lax.axis_size("parts")
    patch_rows, patch_cols = n_rows // PATCH, n_cols // PATCH
    n_patches = patch_rows * patch_cols
    all_rows = n_rows * n_ty
    n_mid, half = n_rows - 2 * MARGIN, n_rows // 2
    n_blocks = n_cols // BLOCK
    vmem = pl.BlockSpec(memory_space=pltpu.VMEM)
    smem = pl.BlockSpec(memory_space=pltpu.SMEM)
    hbm = pl.BlockSpec(memory_space=pltpu.HBM)
    unread = pl.BlockSpec(memory_space=pl.ANY)
    shape = jax.ShapeDtypeStruct
    to_next = [(i, (i + 1) % n_gz) for i in range(n_gz)]

    reach = -(-2 * SMOOTH_PASSES // patch_rows)
    steps = [(1, False)] + [(d, other) for d in range(reach, 1, -1) for other in (False, True)] + [(1, True)]
    swaps = [step for step in steps if has_partners(n_ty, *step)]
    routes = [swap_table(n_gz, n_ty, *step) for step in swaps]

    early = max(1, min(n_blocks - 1, int(n_blocks * EARLY_BLOCKS)))
    window = BLOCK + 2 * LANES
    send_first, held, row_pos, col_pos, tables = call(
        functools.partial(fetch_kernel, all_rows),
        (
            shape((MARGIN, n_cols), bf16),
            shape((n_rows, n_cols), bf16),
            shape((1, n_rows), f32),
            shape((1, n_cols), f32),
            shape((early, window, BLOCK), bf16),
        ),
        [hbm] * 5,
        [vmem] * 5,
        [
            pltpu.VMEM((1, n_rows), jnp.int32),
            pltpu.VMEM((1, n_rows), jnp.int32),
            pltpu.VMEM((1, n_cols), jnp.int32),
            pltpu.VMEM((1, n_cols), jnp.int32),
            pltpu.SemaphoreType.DMA((6,)),
        ],
    )(*(in_hbm(x) for x in (section, row_shift, row_frac, col_shift, col_frac)))
    first = lax.ppermute(send_first, ("parts", "gz", "ty"), halo_table(n_parts, n_gz, n_ty, False))

    edge_shape = shape((MARGIN, MARGIN + half), bf16)
    mid, more_tables, first_table, second_table = call(
        middle_kernel,
        (shape((n_mid, n_cols), bf16), shape((n_blocks - early, window, BLOCK), bf16), edge_shape, edge_shape),
        [vmem] * 4,
        [vmem] * 4,
        [pltpu.VMEM((n_mid, n_cols + 2 * LANES), bf16)],
    )(held, row_pos, col_pos, tables)
    old_mid = lax.ppermute(mid, "gz", to_next)
    turned_mid = call(
        turn_middle_kernel,
        shape((3 * n_patches, MARGIN, LANES), bf16),
        [smem, vmem],
        vmem,
        flops=1_000_000_000,
        moved=3_000_000,
    )(peak_shift, mid)

    send_second = call(send_kernel, shape((MARGIN, n_cols), bf16), [vmem, unread], vmem, flops=4_000_000_000)(
        held, turned_mid
    )
    second = lax.ppermute(send_second, ("parts", "gz", "ty"), halo_table(n_parts, n_gz, n_ty, True))
    def render_edges(which, parts, *args):
        return call(
            functools.partial(edges_kernel, which, parts),
            [shape((MARGIN, n_cols // parts), bf16)] * parts,
            [vmem] * 5 + [unread] * (len(args) - 5),
            [vmem] * parts,
            [pltpu.VMEM((MARGIN, n_cols + 2 * LANES), bf16)],
        )(*args)

    turned_shape = shape((3 * patch_cols, MARGIN, LANES), bf16)
    (first_edge,) = render_edges(False, 1, first, held, first_table, tables, more_tables, send_second)
    old_first = lax.ppermute(first_edge, "gz", to_next)
    turned_first = call(
        functools.partial(turn_first_kernel, patch_rows),
        turned_shape,
        [smem, vmem],
        vmem,
        flops=500_000_000,
        moved=1_000_000,
    )(peak_shift, first_edge)
    second_edges = render_edges(True, EDGE_PARTS, second, held, second_table, tables, more_tables, turned_first)
    part_cols = patch_cols // EDGE_PARTS
    old_seconds = [lax.ppermute(e, "gz", to_next) for e in second_edges]
    smooth = jnp.asarray(column_smoother(patch_cols))
    acc = pltpu.VMEM((9 * patch_cols * 8, LANES), f32)
    terms = (len(swaps) + 1) * 2 * patch_rows
    rendered, turned_second, bands, peak, row_weights, payload = call(
        functools.partial(waiting_kernel, n_ty, tuple(swaps)),
        (
            shape((n_rows, n_cols), bf16),
            turned_shape,
            shape((n_patches, PATCH // 8, LANES), f32),
            shape((2, n_patches, LANES), f32),
            shape((terms, 8, LANES), f32),
            shape((8, LANES), f32),
        ),
        [smem] + [vmem] * (4 + EDGE_PARTS) + [hbm, vmem, unread],
        [hbm] + [vmem] * 5,
        [acc, pltpu.VMEM((n_rows, n_cols), bf16), pltpu.SemaphoreType.DMA((3 + EDGE_PARTS,))],
        flops=1_000_000_000,
        moved=3_000_000,
    )(peak_shift, mid, first_edge, *second_edges, turned_mid, turned_first, in_hbm(boundary), smooth, old_mid)
    windows = [(True, range(patch_cols), turned_second, old_first)]
    for k, old in enumerate(old_seconds):
        windows.append((False, range(k * part_cols, (k + 1) * part_cols), turned_first, old))
    for which, cols, turned, old in windows:
        payload = call(
            functools.partial(window_kernel, which, cols), shape((8, LANES), f32), [vmem] * 8, vmem, [acc]
        )(turned_mid, turned, bands, peak, old_mid, old, smooth, payload)
    blocks = [payload] + [lax.ppermute(payload, ("gz", "ty"), route) for route in routes]
    flow = call(
        rows_kernel, shape((2, 1, patch_rows, patch_cols), f32), [vmem] * (1 + len(blocks)), vmem
    )(row_weights, *blocks)
    return rendered[None], flow


def solution(mesh):
    in_specs = (
        P(("parts", "gz"), "ty", None),
        P(("parts", "ty"), None),
        P(("parts", "gz"), "ty"),
        P(("parts", "gz"), "ty"),
        P(("parts", "gz"), None),
        P(("parts", "gz"), None),
        P(None, ("parts", "gz"), "ty", None),
    )
    out_specs = (P(("parts", "gz"), "ty", None), P(None, ("parts", "gz"), "ty", None))
    return jax.shard_map(local, mesh=mesh, in_specs=in_specs, out_specs=out_specs, check_vma=False)
```

```python
import functools

import jax
import jax.numpy as jnp
import numpy as np
from jax import lax
from jax.experimental import pallas as pl
from jax.experimental.pallas import tpu as pltpu
from jax.sharding import PartitionSpec as P

PATCH = 128
MARGIN = 64
SMOOTH_PASSES = 2
BLOCK = 256
LANES = 128
TAPS = (0.0625, 0.25, 0.375, 0.25, 0.0625)
FAR = 1 << 20
VMEM_LIMIT = 16 * 1024 * 1024
TURN_UNROLL = 16
PLAN_UNROLL = 8
EARLY_BLOCKS = 3 / 8
EDGE_PARTS = 2

f32 = jnp.float32
bf16 = jnp.bfloat16


def swap_table(n_gz, n_ty, steps):
    table = []
    for z in range(n_gz):
        d, second = steps[z // 2 % 2]
        for t in range(n_ty):
            partner = t + d if ((t // d) % 2 == 0) != second else t - d
            if 0 <= partner < n_ty:
                table.append((z * n_ty + t, z * n_ty + partner))
            elif (z ^ 1) < n_gz:
                table.append((z * n_ty + t, (z ^ 1) * n_ty + t))
    return tuple(table)


def halo_table(n_parts, n_gz, n_ty, second):
    table = []
    for p in range(n_parts):
        for z in range(n_gz):
            for t in range(n_ty):
                partner = t + 1 if (t % 2 == 0) != (second != (z % 2 == 1)) else t - 1
                if 0 <= partner < n_ty:
                    there = (p, z, partner)
                elif (p ^ 1) < n_parts:
                    there = (p ^ 1, z, t)
                else:
                    continue
                table.append(tuple((a * n_gz + b) * n_ty + c for a, b, c in ((p, z, t), there)))
    return tuple(table)


def partner_of(tile, d, second):
    up = (tile // d) % 2 == int(second)
    return tile + jnp.where(up, d, -d)


def has_partners(n_ty, d, second):
    return any(((t // d) % 2 == 0) != second and t + d < n_ty for t in range(n_ty))


def takes_bottom(second):
    return (lax.axis_index("ty") + lax.axis_index("gz")) % 2 == int(second)


def hat(coord, position):
    return jnp.maximum(1.0 - jnp.abs(coord - position), 0.0)


def source_positions(ids, shift, frac, limit, base):
    source = jnp.clip(ids + shift, 0, limit) - base
    return source.astype(f32) + frac.astype(f32) * (1.0 / 256.0)


def times(left, right):
    return jnp.dot(left, right, preferred_element_type=f32).astype(bf16)


def build_tables(col_pos, first, tables):
    reach = BLOCK + LANES
    coord = lax.broadcasted_iota(jnp.int32, (reach, BLOCK), 0).astype(f32) - float(LANES // 2)
    edge = jnp.zeros((LANES // 2, BLOCK), bf16)

    @pl.loop(0, tables.shape[0])
    def _(k):
        at = pl.multiple_of((first + k) * BLOCK, BLOCK)
        pos = col_pos[:, pl.ds(at, BLOCK)] - at.astype(f32)
        tables[k, 0 : LANES // 2, :] = edge
        tables[k, LANES // 2 : LANES // 2 + reach, :] = hat(coord, pos).astype(bf16)
        tables[k, LANES // 2 + reach :, :] = edge


def fetch_kernel(all_rows, section, row_shift, row_frac, col_shift, col_frac, *rest):
    send_first, row_pos, col_pos, tables = rest[:4]
    row_shift_v, row_frac_v, col_shift_v, col_frac_v, sems = rest[4:]
    n_rows, n_cols = section.shape
    base = lax.axis_index("ty") * n_rows
    at = pl.multiple_of(jnp.where(takes_bottom(False), n_rows - MARGIN, 0), MARGIN)
    copies = [
        pltpu.make_async_copy(source, target, sems.at[k])
        for k, (source, target) in enumerate(
            (
                (col_shift, col_shift_v),
                (col_frac, col_frac_v),
                (row_shift, row_shift_v),
                (row_frac, row_frac_v),
                (section.at[pl.ds(at, MARGIN), :], send_first),
            )
        )
    ]
    for copy in copies:
        copy.start()
    for copy in copies[:4]:
        copy.wait()
    ids = lax.broadcasted_iota(jnp.int32, (1, n_cols), 1)
    col_pos[...] = source_positions(ids, col_shift_v[...], col_frac_v[...], n_cols - 2, 0)
    ids = lax.broadcasted_iota(jnp.int32, (1, n_rows), 1) + base
    row_pos[...] = source_positions(ids, row_shift_v[...], row_frac_v[...], all_rows - 2, base)
    build_tables(col_pos, 0, tables)
    for copy in copies[4:]:
        copy.wait()


def columns_of(mix, tables, *out_refs):
    j = 0
    wide = out_refs[0].shape[1] // BLOCK
    for table in tables:
        for k in range(table.shape[0]):
            at = j % wide
            out_refs[j // wide][:, at * BLOCK : (at + 1) * BLOCK] = times(
                mix[:, j * BLOCK : (j + 1) * BLOCK + 2 * LANES], table[k]
            )
            j += 1


def clear_sides(mix):
    edge = jnp.zeros((mix.shape[0], LANES), bf16)
    mix[:, 0:LANES] = edge
    mix[:, mix.shape[1] - LANES :] = edge


def edge_table(second, row_pos, table):
    n_rows = row_pos.shape[1]
    half = n_rows // 2
    slot = lax.broadcasted_iota(jnp.int32, (MARGIN + half, MARGIN), 0)
    bottom = takes_bottom(second)
    start = jnp.where(
        slot < MARGIN, jnp.where(bottom, n_rows, -MARGIN), jnp.where(bottom, half - MARGIN, -MARGIN)
    )
    here = jnp.where(bottom, row_pos[:, n_rows - MARGIN :], row_pos[:, :MARGIN])
    table[...] = hat((slot + start).astype(f32), here).T.astype(bf16)


def middle_kernel(held, row_pos, col_pos, tables, mid_ref, more_tables, first_table, second_table, mix):
    n_rows, n_cols = held.shape
    build_tables(col_pos, tables.shape[0], more_tables)
    edge_table(False, row_pos, first_table)
    edge_table(True, row_pos, second_table)
    coord = lax.broadcasted_iota(jnp.int32, (n_rows, n_rows - 2 * MARGIN), 0).astype(f32)
    mid_table = hat(coord, row_pos[:, MARGIN : n_rows - MARGIN]).T.astype(bf16)
    clear_sides(mix)
    for j in range(n_cols // BLOCK):
        mix[:, LANES + j * BLOCK : LANES + (j + 1) * BLOCK] = times(
            mid_table, held[:, j * BLOCK : (j + 1) * BLOCK]
        )
    columns_of(mix, (tables, more_tables), mid_ref)


def send_kernel(held, _, send_second):
    n_rows = held.shape[0]
    at = pl.multiple_of(jnp.where(takes_bottom(True), n_rows - MARGIN, 0), MARGIN)
    send_second[...] = held[pl.ds(at, MARGIN), :]


def edges_kernel(second, parts, halo, held, table, tables, more_tables, *rest):
    edge_refs, mix = rest[-1 - parts : -1], rest[-1]
    n_rows, n_cols = held.shape
    half = n_rows // 2
    own = pl.ds(pl.multiple_of(jnp.where(takes_bottom(second), half, 0), half), half)
    clear_sides(mix)
    for j in range(n_cols // BLOCK):
        here = slice(j * BLOCK, (j + 1) * BLOCK)
        stack = jnp.concatenate([halo[:, here], held[own, here]], axis=0)
        mix[:, LANES + j * BLOCK : LANES + (j + 1) * BLOCK] = times(table[...], stack)
    columns_of(mix, (tables, more_tables), *edge_refs)


def turn_patches(peaks, i, rows, source, turned, first):
    patch_cols = source.shape[1] // PATCH
    n_turned = turned.shape[0] // 3
    first_col = first % peaks.shape[3]

    @pl.loop(0, patch_cols, unroll=min(TURN_UNROLL, patch_cols))
    def _(j):
        block = source[rows, pl.ds(pl.multiple_of(j * PATCH, PATCH), PATCH)]
        for dx in range(3):
            turned[dx * n_turned + first + j] = pltpu.roll(block, (peaks[1, 0, i, first_col + j] + (dx - 1)) % PATCH, 1)


def plan_windows(peaks, bands, peak):
    lane = lax.broadcasted_iota(jnp.int32, (PATCH // 8, LANES), 1)
    offset = lane - 8 * lax.broadcasted_iota(jnp.int32, (PATCH // 8, LANES), 0) + 1
    patch_rows, patch_cols = peaks.shape[2:]
    for i in range(patch_rows):

        @pl.loop(0, patch_cols, unroll=PLAN_UNROLL)
        def _(j):
            p = i * patch_cols + j
            bands[p] = jnp.where(((offset - peaks[0, 0, i, j]) & (PATCH - 1)) <= 9, 1.0, 0.0)
            for c in range(2):
                peak[c, pl.ds(p, 1), :] = jnp.full((1, LANES), peaks[c, 0, i, j], jnp.int32).astype(f32)


def turn_middle_kernel(peaks, mid, turned):
    for i in range(mid.shape[0] // MARGIN):
        turn_patches(peaks, i, slice(i * MARGIN, (i + 1) * MARGIN), mid, turned, i * (mid.shape[1] // PATCH))


def edge_patch_row(second, patch_rows):
    return jnp.where(takes_bottom(second), patch_rows - 1, 0)


def turn_first_kernel(patch_rows, peaks, edge, turned):
    turn_patches(peaks, edge_patch_row(False, patch_rows), slice(None), edge, turned, 0)


def patch_row_flow(i, cols, turned_edge, turned_mid, bands, peak, smooth, old_of, acc):
    patch_cols = turned_edge.shape[0] // 3
    n_patches = bands.shape[0]
    lane = lax.broadcasted_iota(jnp.int32, (8, LANES), 1) - lax.broadcasted_iota(jnp.int32, (8, LANES), 0)
    n_here = len(cols)
    for at_j, j in enumerate(cols):
        p = i * patch_cols + j
        left = []
        for dx in range(3):
            left += [turned_edge[dx * patch_cols + j], turned_mid[dx * n_patches + p]]
        products = lax.dot_general(
            jnp.concatenate(left, axis=0), old_of(j), (((1,), (1,)), ((), ())), preferred_element_type=f32
        )
        band = bands[p]
        place = (lane - peak[0, pl.ds(p, 1), :].astype(jnp.int32)) & 15
        for dx in range(3):
            lines = [
                products[dx * PATCH + 8 * r : dx * PATCH + 8 * r + 8, :] * band[r : r + 1, :]
                for r in range(PATCH // 8)
            ]
            even, odd = sum(lines[2::2], lines[0]), sum(lines[3::2], lines[1])
            for dy in range(3):
                at = ((dy * 3 + dx) * n_here + at_j) * 8
                acc[at : at + 8, :] = jnp.where(place == (dy - 1) % 16, even, 0.0) + jnp.where(
                    place == (dy + 7) % 16, odd, 0.0
                )
    total = acc[pl.ds(0, 9 * n_here, stride=8), :]
    for s in range(1, 8):
        total = total + acc[pl.ds(s, 9 * n_here, stride=8), :]
    weights = jnp.maximum(jnp.sum(total, axis=1, keepdims=True) * (1.0 / PATCH), 0.0)
    w = [weights[k * n_here : (k + 1) * n_here] for k in range(9)]
    scale = 1.0 / jnp.maximum(sum(w), 1.0)
    moves = (
        (w[6] + w[7] + w[8] - w[0] - w[1] - w[2]) * scale,
        (w[2] + w[5] + w[8] - w[0] - w[3] - w[6]) * scale,
    )
    here = pl.ds(pl.multiple_of(i * patch_cols + cols[0], 8), n_here)
    share = smooth[cols[0] : cols[0] + n_here, :]
    return [jnp.sum((moves[c] + peak[c, here, :]) * share, axis=0, keepdims=True) for c in range(2)]


def put_lines(lines, i, patch_rows):
    at = lax.broadcasted_iota(jnp.int32, (8, LANES), 0)
    return sum(jnp.where(at == c * patch_rows + i, line, 0.0) for c, line in enumerate(lines))


def waiting_kernel(n_ty, swaps, peaks, mid, first, *rest):
    seconds, rest = rest[:EDGE_PARTS], rest[EDGE_PARTS:]
    turned_mid, turned_first, boundary, smooth, _ = rest[:5]
    rendered, turned_second, bands, peak, row_weights, flow, acc, whole, sems = rest[5:]
    n_rows, n_cols = boundary.shape
    patch_rows = n_rows // PATCH
    moves = [(mid, pl.ds(MARGIN, mid.shape[0]), pl.ds(0, n_cols))]
    wide = n_cols // EDGE_PARTS
    for edge, which, start in [(first, False, 0)] + [(e, True, k * wide) for k, e in enumerate(seconds)]:
        at = pl.multiple_of(jnp.where(takes_bottom(which), n_rows - MARGIN, 0), MARGIN)
        moves.append((edge, pl.ds(at, MARGIN), pl.ds(start, edge.shape[1])))
    copies = [pltpu.make_async_copy(a, rendered.at[b, c], sems.at[k]) for k, (a, b, c) in enumerate(moves)]
    fetch = pltpu.make_async_copy(boundary, whole, sems.at[len(moves)])
    has_boundary = lax.axis_index("gz") == 0

    @pl.when(has_boundary)
    def _():
        fetch.start()

    for copy in copies:
        copy.start()
    flow[...] = jnp.zeros_like(flow)
    for k, edge in enumerate(seconds):
        turn_patches(peaks, edge_patch_row(True, patch_rows), slice(None), edge, turned_second, k * (wide // PATCH))
    plan_windows(peaks, bands, peak)
    fill_row_weights(n_ty, swaps, patch_rows, row_weights)

    @pl.when(has_boundary)
    def _():
        fetch.wait()

        @pl.loop(0, patch_rows)
        def _(k):
            i = jnp.where(k == 0, edge_patch_row(False, patch_rows), edge_patch_row(True, patch_rows))
            at_edge = pl.multiple_of(i * (n_rows - MARGIN), MARGIN)
            at_mid = pl.multiple_of(MARGIN + i * MARGIN, MARGIN)

            def old_of(j):
                cols = slice(j * PATCH, (j + 1) * PATCH)
                return jnp.concatenate([whole[pl.ds(at_edge, MARGIN), cols], whole[pl.ds(at_mid, MARGIN), cols]], axis=0)

            def flow_with(turned_edge):
                flow[...] += put_lines(
                    patch_row_flow(i, range(n_cols // PATCH), turned_edge, turned_mid, bands, peak, smooth, old_of, acc), i, patch_rows
                )

            @pl.when(k == 0)
            def _():
                flow_with(turned_first)

            @pl.when(k != 0)
            def _():
                flow_with(turned_second)

    for copy in copies:
        copy.wait()


def window_kernel(second, cols, turned_mid, turned_edge, bands, peak, old_mid, old_edge, smooth, before, out_ref, acc):
    patch_rows = old_mid.shape[0] // MARGIN
    out_ref[...] = before[...]

    @pl.when(lax.axis_index("gz") != 0)
    def _():
        i = edge_patch_row(second, patch_rows)
        at_mid = pl.multiple_of(i * MARGIN, MARGIN)

        def old_of(j):
            here = slice((j - cols[0]) * PATCH, (j - cols[0] + 1) * PATCH)
            there = slice(j * PATCH, (j + 1) * PATCH)
            return jnp.concatenate([old_edge[:, here], old_mid[pl.ds(at_mid, MARGIN), there]], axis=0)

        lines = patch_row_flow(i, cols, turned_edge, turned_mid, bands, peak, smooth, old_of, acc)
        out_ref[...] = before[...] + put_lines(lines, i, patch_rows)


def fill_row_weights(n_ty, swaps, patch_rows, out_ref):
    all_rows = n_ty * patch_rows
    tile = lax.axis_index("ty")
    held = 2 * patch_rows
    depth = LANES
    at = lax.broadcasted_iota(jnp.int32, (8, depth), 0)
    slot = lax.broadcasted_iota(jnp.int32, (8, depth), 1)
    holder = jnp.full((8, depth), tile, jnp.int32)
    even_chip = (lax.axis_index("gz") // 2) % 2 == 0
    for k, (step, other) in enumerate(swaps):
        partner = jnp.where(even_chip, partner_of(tile, *step), partner_of(tile, *other))
        holder = jnp.where((slot >> 3) == k + 1, partner, holder)
    inner = slot & 7
    c_out = (at >= patch_rows).astype(jnp.int32)
    c_in = (inner >= patch_rows).astype(jnp.int32)
    row = tile * patch_rows + at - c_out * patch_rows
    source = holder * patch_rows + inner - c_in * patch_rows

    def inside(r):
        return (r >= 0) & (r < all_rows)

    def tap(delta):
        size = jnp.abs(delta)
        return jnp.where(
            size == 0, TAPS[2], jnp.where(size == 1, TAPS[1], jnp.where(size == 2, TAPS[0], 0.0))
        )

    def norm(r):
        return sum(jnp.where(inside(r + o), TAPS[o + 2], 0.0) for o in range(-2, 3))

    weight = jnp.zeros((8, depth), f32)
    for o in range(-2, 3):
        weight = weight + jnp.where(inside(row + o), TAPS[o + 2] * tap(source - row - o) / norm(row + o), 0.0)
    used = (inner < held) & (at < held) & (c_in == c_out) & inside(source)
    weight = jnp.where(used, weight / norm(row), 0.0)
    for k in range(len(swaps) + 1):
        for b in range(held):
            out_ref[k * held + b] = jnp.broadcast_to(weight[:, 8 * k + b : 8 * k + b + 1], (8, LANES))


def rows_kernel(row_weights, *refs):
    blocks, out_ref = refs[:-1], refs[-1]
    patch_rows, patch_cols = out_ref.shape[2], out_ref.shape[3]
    held = 2 * patch_rows
    result = None
    for k, block in enumerate(blocks):
        for b in range(held):
            term = row_weights[k * held + b] * block[b : b + 1, :]
            result = term if result is None else result + term
    for c in range(2):
        out_ref[c, 0] = result[c * patch_rows : (c + 1) * patch_rows, :patch_cols]


def column_smoother(n):
    kernel = np.zeros((n, n))
    for i in range(n):
        for o in range(-2, 3):
            if 0 <= i + o < n:
                kernel[i, i + o] = TAPS[o + 2]
    kernel = kernel / kernel.sum(1, keepdims=True)
    table = np.zeros((n, LANES), np.float32)
    table[:, :n] = np.linalg.matrix_power(kernel, SMOOTH_PASSES).T
    return table


def call(body, out_shape, in_specs, out_specs, scratch=(), flops=0, moved=0):
    return pl.pallas_call(
        body,
        out_shape=out_shape,
        in_specs=in_specs,
        out_specs=out_specs,
        scratch_shapes=scratch,
        compiler_params=pltpu.CompilerParams(vmem_limit_bytes=VMEM_LIMIT),
        cost_estimate=pl.CostEstimate(flops=flops, bytes_accessed=moved, transcendentals=0),
    )


def in_hbm(x):
    return pltpu.with_memory_space_constraint(x, pltpu.HBM)


def local(sections, boundary, row_shift, row_frac, col_shift, col_frac, peak_shift):
    section = sections[0]
    n_rows, n_cols = section.shape
    n_ty, n_gz, n_parts = lax.axis_size("ty"), lax.axis_size("gz"), lax.axis_size("parts")
    patch_rows, patch_cols = n_rows // PATCH, n_cols // PATCH
    n_patches = patch_rows * patch_cols
    all_rows = n_rows * n_ty
    n_mid, half = n_rows - 2 * MARGIN, n_rows // 2
    n_blocks = n_cols // BLOCK
    vmem = pl.BlockSpec(memory_space=pltpu.VMEM)
    smem = pl.BlockSpec(memory_space=pltpu.SMEM)
    hbm = pl.BlockSpec(memory_space=pltpu.HBM)
    unread = pl.BlockSpec(memory_space=pl.ANY)
    shape = jax.ShapeDtypeStruct
    to_next = [(i, (i + 1) % n_gz) for i in range(n_gz)]

    reach = -(-2 * SMOOTH_PASSES // patch_rows)
    far = [(d, other) for d in range(reach, 1, -1) for other in (False, True)]
    swaps = list(zip([(1, False), *far, (1, True)], [(1, True), *far, (1, False)]))
    swaps = [steps for steps in swaps if any(has_partners(n_ty, *step) for step in steps)]
    routes = [swap_table(n_gz, n_ty, steps) for steps in swaps]

    early = max(1, min(n_blocks - 1, int(n_blocks * EARLY_BLOCKS)))
    window = BLOCK + 2 * LANES
    held = section
    send_first, row_pos, col_pos, tables = call(
        functools.partial(fetch_kernel, all_rows),
        (
            shape((MARGIN, n_cols), bf16),
            shape((1, n_rows), f32),
            shape((1, n_cols), f32),
            shape((early, window, BLOCK), bf16),
        ),
        [hbm] * 5,
        [vmem] * 4,
        [
            pltpu.VMEM((1, n_rows), jnp.int32),
            pltpu.VMEM((1, n_rows), jnp.int32),
            pltpu.VMEM((1, n_cols), jnp.int32),
            pltpu.VMEM((1, n_cols), jnp.int32),
            pltpu.SemaphoreType.DMA((5,)),
        ],
        flops=0,
        moved=0,
    )(*(in_hbm(x) for x in (section, row_shift, row_frac, col_shift, col_frac)))
    first = lax.ppermute(send_first, ("parts", "gz", "ty"), halo_table(n_parts, n_gz, n_ty, False))

    edge_shape = shape((MARGIN, MARGIN + half), bf16)
    mid, more_tables, first_table, second_table = call(
        middle_kernel,
        (shape((n_mid, n_cols), bf16), shape((n_blocks - early, window, BLOCK), bf16), edge_shape, edge_shape),
        [vmem] * 4,
        [vmem] * 4,
        [pltpu.VMEM((n_mid, n_cols + 2 * LANES), bf16)],
    )(held, row_pos, col_pos, tables)
    old_mid = lax.ppermute(mid, "gz", to_next)
    turned_mid = call(
        turn_middle_kernel,
        shape((3 * n_patches, MARGIN, LANES), bf16),
        [smem, vmem],
        vmem,
        flops=1_000_000_000,
        moved=3_000_000,
    )(peak_shift, mid)

    send_second = call(send_kernel, shape((MARGIN, n_cols), bf16), [vmem, unread], vmem, flops=4_000_000_000)(
        held, turned_mid
    )
    second = lax.ppermute(send_second, ("parts", "gz", "ty"), halo_table(n_parts, n_gz, n_ty, True))
    def render_edges(which, parts, *args):
        return call(
            functools.partial(edges_kernel, which, parts),
            [shape((MARGIN, n_cols // parts), bf16)] * parts,
            [vmem] * 5 + [unread] * (len(args) - 5),
            [vmem] * parts,
            [pltpu.VMEM((MARGIN, n_cols + 2 * LANES), bf16)],
        )(*args)

    turned_shape = shape((3 * patch_cols, MARGIN, LANES), bf16)
    (first_edge,) = render_edges(False, 1, first, held, first_table, tables, more_tables, send_second)
    old_first = lax.ppermute(first_edge, "gz", to_next)
    turned_first = call(
        functools.partial(turn_first_kernel, patch_rows),
        turned_shape,
        [smem, vmem],
        vmem,
        flops=500_000_000,
        moved=1_000_000,
    )(peak_shift, first_edge)
    second_edges = render_edges(True, EDGE_PARTS, second, held, second_table, tables, more_tables, turned_first)
    part_cols = patch_cols // EDGE_PARTS
    old_seconds = [lax.ppermute(e, "gz", to_next) for e in second_edges]
    smooth = jnp.asarray(column_smoother(patch_cols))
    acc = pltpu.VMEM((9 * patch_cols * 8, LANES), f32)
    terms = (len(swaps) + 1) * 2 * patch_rows
    rendered, turned_second, bands, peak, row_weights, payload = call(
        functools.partial(waiting_kernel, n_ty, tuple(swaps)),
        (
            shape((n_rows, n_cols), bf16),
            turned_shape,
            shape((n_patches, PATCH // 8, LANES), f32),
            shape((2, n_patches, LANES), f32),
            shape((terms, 8, LANES), f32),
            shape((8, LANES), f32),
        ),
        [smem] + [vmem] * (4 + EDGE_PARTS) + [hbm, vmem, unread],
        [hbm] + [vmem] * 5,
        [acc, pltpu.VMEM((n_rows, n_cols), bf16), pltpu.SemaphoreType.DMA((3 + EDGE_PARTS,))],
        flops=1_000_000_000,
        moved=3_000_000,
    )(peak_shift, mid, first_edge, *second_edges, turned_mid, turned_first, in_hbm(boundary), smooth, old_mid)
    windows = [(True, range(patch_cols), turned_second, old_first)]
    for k, old in enumerate(old_seconds):
        windows.append((False, range(k * part_cols, (k + 1) * part_cols), turned_first, old))
    for which, cols, turned, old in windows:
        payload = call(
            functools.partial(window_kernel, which, cols), shape((8, LANES), f32), [vmem] * 8, vmem, [acc]
        )(turned_mid, turned, bands, peak, old_mid, old, smooth, payload)
    blocks = [payload] + [lax.ppermute(payload, ("gz", "ty"), route) for route in routes]
    flow = call(
        rows_kernel, shape((2, 1, patch_rows, patch_cols), f32), [vmem] * (1 + len(blocks)), vmem
    )(row_weights, *blocks)
    return rendered[None], flow


def solution(mesh):
    in_specs = (
        P(("parts", "gz"), "ty", None),
        P(("parts", "ty"), None),
        P(("parts", "gz"), "ty"),
        P(("parts", "gz"), "ty"),
        P(("parts", "gz"), None),
        P(("parts", "gz"), None),
        P(None, ("parts", "gz"), "ty", None),
    )
    out_specs = (P(("parts", "gz"), "ty", None), P(None, ("parts", "gz"), "ty", None))
    return jax.shard_map(local, mesh=mesh, in_specs=in_specs, out_specs=out_specs, check_vma=False)
```

```python
import functools

import jax
import jax.numpy as jnp
import numpy as np
from jax import lax
from jax.experimental import pallas as pl
from jax.experimental.pallas import tpu as pltpu
from jax.sharding import PartitionSpec as P

PATCH = 128
MARGIN = 64
SMOOTH_PASSES = 2
BLOCK = 256
LANES = 128
TAPS = (0.0625, 0.25, 0.375, 0.25, 0.0625)
FAR = 1 << 20
VMEM_LIMIT = 16 * 1024 * 1024
TURN_UNROLL = 16
PLAN_UNROLL = 8
EARLY_BLOCKS = 6 / 8
EDGE_PARTS = 2

f32 = jnp.float32
bf16 = jnp.bfloat16


def swap_table(n_gz, n_ty, steps):
    table = []
    for z in range(n_gz):
        d, second = steps[z // 2 % 2]
        for t in range(n_ty):
            partner = t + d if ((t // d) % 2 == 0) != second else t - d
            if 0 <= partner < n_ty:
                table.append((z * n_ty + t, z * n_ty + partner))
            elif (z ^ 1) < n_gz:
                table.append((z * n_ty + t, (z ^ 1) * n_ty + t))
    return tuple(table)


def halo_table(n_parts, n_gz, n_ty, second):
    table = []
    for p in range(n_parts):
        for z in range(n_gz):
            for t in range(n_ty):
                partner = t + 1 if (t % 2 == 0) != (second != (z % 2 == 1)) else t - 1
                if 0 <= partner < n_ty:
                    there = (p, z, partner)
                elif (p ^ 1) < n_parts:
                    there = (p ^ 1, z, t)
                else:
                    continue
                table.append(tuple((a * n_gz + b) * n_ty + c for a, b, c in ((p, z, t), there)))
    return tuple(table)


def partner_of(tile, d, second):
    up = (tile // d) % 2 == int(second)
    return tile + jnp.where(up, d, -d)


def has_partners(n_ty, d, second):
    return any(((t // d) % 2 == 0) != second and t + d < n_ty for t in range(n_ty))


def takes_bottom(second):
    return (lax.axis_index("ty") + lax.axis_index("gz")) % 2 == int(second)


def hat(coord, position):
    return jnp.maximum(1.0 - jnp.abs(coord - position), 0.0)


def source_positions(ids, shift, frac, limit, base):
    source = jnp.clip(ids + shift, 0, limit) - base
    return source.astype(f32) + frac.astype(f32) * (1.0 / 256.0)


def times(left, right):
    return jnp.dot(left, right, preferred_element_type=f32).astype(bf16)


def build_tables(col_pos, first, tables):
    reach = BLOCK + LANES
    whole = (reach, BLOCK)
    slot = lax.broadcasted_iota(jnp.int16, whole, 0)
    edge = jnp.zeros((LANES // 2, BLOCK), bf16)

    @pl.loop(0, tables.shape[0])
    def _(k):
        at = pl.multiple_of((first + k) * BLOCK, BLOCK)
        pos = col_pos[:, pl.ds(at, BLOCK)] - at.astype(f32) + float(LANES // 2)
        low = pos.astype(jnp.int32)
        part = pos - low.astype(f32)
        near = jnp.broadcast_to(low, whole).astype(jnp.int16)
        left = jnp.broadcast_to(1.0 - part, whole).astype(bf16)
        right = jnp.broadcast_to(part, whole).astype(bf16)
        weight = jnp.where(slot == near, left, jnp.where(slot == near + 1, right, jnp.zeros((), bf16)))
        tables[k, 0 : LANES // 2, :] = edge
        tables[k, LANES // 2 : LANES // 2 + reach, :] = weight
        tables[k, LANES // 2 + reach :, :] = edge


def fetch_kernel(all_rows, section, row_shift, row_frac, col_shift, col_frac, *rest):
    send_first, row_pos, col_pos, tables = rest[:4]
    row_shift_v, row_frac_v, col_shift_v, col_frac_v, sems = rest[4:]
    n_rows, n_cols = section.shape
    base = lax.axis_index("ty") * n_rows
    at = pl.multiple_of(jnp.where(takes_bottom(False), n_rows - MARGIN, 0), MARGIN)
    copies = [
        pltpu.make_async_copy(source, target, sems.at[k])
        for k, (source, target) in enumerate(
            (
                (col_shift, col_shift_v),
                (col_frac, col_frac_v),
                (row_shift, row_shift_v),
                (row_frac, row_frac_v),
                (section.at[pl.ds(at, MARGIN), :], send_first),
            )
        )
    ]
    for copy in copies:
        copy.start()
    for copy in copies[:4]:
        copy.wait()
    ids = lax.broadcasted_iota(jnp.int32, (1, n_cols), 1)
    col_pos[...] = source_positions(ids, col_shift_v[...], col_frac_v[...], n_cols - 2, 0)
    ids = lax.broadcasted_iota(jnp.int32, (1, n_rows), 1) + base
    row_pos[...] = source_positions(ids, row_shift_v[...], row_frac_v[...], all_rows - 2, base)
    build_tables(col_pos, 0, tables)
    for copy in copies[4:]:
        copy.wait()


def columns_of(mix, tables, *out_refs):
    j = 0
    wide = out_refs[0].shape[1] // BLOCK
    for table in tables:
        for k in range(table.shape[0]):
            at = j % wide
            out_refs[j // wide][:, at * BLOCK : (at + 1) * BLOCK] = times(
                mix[:, j * BLOCK : (j + 1) * BLOCK + 2 * LANES], table[k]
            )
            j += 1


def clear_sides(mix):
    edge = jnp.zeros((mix.shape[0], LANES), bf16)
    mix[:, 0:LANES] = edge
    mix[:, mix.shape[1] - LANES :] = edge


def edge_table(second, row_pos, table):
    n_rows = row_pos.shape[1]
    half = n_rows // 2
    slot = lax.broadcasted_iota(jnp.int32, (MARGIN + half, MARGIN), 0)
    bottom = takes_bottom(second)
    start = jnp.where(
        slot < MARGIN, jnp.where(bottom, n_rows, -MARGIN), jnp.where(bottom, half - MARGIN, -MARGIN)
    )
    here = jnp.where(bottom, row_pos[:, n_rows - MARGIN :], row_pos[:, :MARGIN])
    table[...] = hat((slot + start).astype(f32), here).T.astype(bf16)


def middle_kernel(held, row_pos, col_pos, tables, mid_ref, more_tables, first_table, second_table, mix):
    n_rows, n_cols = held.shape
    build_tables(col_pos, tables.shape[0], more_tables)
    edge_table(False, row_pos, first_table)
    edge_table(True, row_pos, second_table)
    coord = lax.broadcasted_iota(jnp.int32, (n_rows, n_rows - 2 * MARGIN), 0).astype(f32)
    mid_table = hat(coord, row_pos[:, MARGIN : n_rows - MARGIN]).T.astype(bf16)
    clear_sides(mix)
    for j in range(n_cols // BLOCK):
        mix[:, LANES + j * BLOCK : LANES + (j + 1) * BLOCK] = times(
            mid_table, held[:, j * BLOCK : (j + 1) * BLOCK]
        )
    columns_of(mix, (tables, more_tables), mid_ref)


def send_kernel(held, _, send_second):
    n_rows = held.shape[0]
    at = pl.multiple_of(jnp.where(takes_bottom(True), n_rows - MARGIN, 0), MARGIN)
    send_second[...] = held[pl.ds(at, MARGIN), :]


def edges_kernel(second, parts, halo, held, table, tables, more_tables, *rest):
    edge_refs, mix = rest[-1 - parts : -1], rest[-1]
    n_rows, n_cols = held.shape
    half = n_rows // 2
    own = pl.ds(pl.multiple_of(jnp.where(takes_bottom(second), half, 0), half), half)
    clear_sides(mix)
    for j in range(n_cols // BLOCK):
        here = slice(j * BLOCK, (j + 1) * BLOCK)
        stack = jnp.concatenate([halo[:, here], held[own, here]], axis=0)
        mix[:, LANES + j * BLOCK : LANES + (j + 1) * BLOCK] = times(table[...], stack)
    columns_of(mix, (tables, more_tables), *edge_refs)


def turn_patches(peaks, i, rows, source, turned, first):
    patch_cols = source.shape[1] // PATCH
    n_turned = turned.shape[0] // 3
    first_col = first % peaks.shape[3]

    @pl.loop(0, patch_cols, unroll=min(TURN_UNROLL, patch_cols))
    def _(j):
        block = source[rows, pl.ds(pl.multiple_of(j * PATCH, PATCH), PATCH)]
        for dx in range(3):
            turned[dx * n_turned + first + j] = pltpu.roll(block, (peaks[1, 0, i, first_col + j] + (dx - 1)) % PATCH, 1)


def plan_windows(peaks, bands, peak):
    lane = lax.broadcasted_iota(jnp.int32, (PATCH // 8, LANES), 1)
    offset = lane - 8 * lax.broadcasted_iota(jnp.int32, (PATCH // 8, LANES), 0) + 1
    patch_rows, patch_cols = peaks.shape[2:]
    for i in range(patch_rows):

        @pl.loop(0, patch_cols, unroll=PLAN_UNROLL)
        def _(j):
            p = i * patch_cols + j
            bands[p] = jnp.where(((offset - peaks[0, 0, i, j]) & (PATCH - 1)) <= 9, 1.0, 0.0)
            for c in range(2):
                peak[c, pl.ds(p, 1), :] = jnp.full((1, LANES), peaks[c, 0, i, j], jnp.int32).astype(f32)


def turn_middle_kernel(peaks, mid, turned):
    for i in range(mid.shape[0] // MARGIN):
        turn_patches(peaks, i, slice(i * MARGIN, (i + 1) * MARGIN), mid, turned, i * (mid.shape[1] // PATCH))


def edge_patch_row(second, patch_rows):
    return jnp.where(takes_bottom(second), patch_rows - 1, 0)


def turn_first_kernel(patch_rows, peaks, edge, turned):
    turn_patches(peaks, edge_patch_row(False, patch_rows), slice(None), edge, turned, 0)


def patch_row_flow(i, cols, turned_edge, turned_mid, bands, peak, smooth, old_of, acc):
    patch_cols = turned_edge.shape[0] // 3
    n_patches = bands.shape[0]
    lane = lax.broadcasted_iota(jnp.int32, (8, LANES), 1) - lax.broadcasted_iota(jnp.int32, (8, LANES), 0)
    n_here = len(cols)
    for at_j, j in enumerate(cols):
        p = i * patch_cols + j
        left = []
        for dx in range(3):
            left += [turned_edge[dx * patch_cols + j], turned_mid[dx * n_patches + p]]
        products = lax.dot_general(
            jnp.concatenate(left, axis=0), old_of(j), (((1,), (1,)), ((), ())), preferred_element_type=f32
        )
        band = bands[p]
        place = (lane - peak[0, pl.ds(p, 1), :].astype(jnp.int32)) & 15
        for dx in range(3):
            lines = [
                products[dx * PATCH + 8 * r : dx * PATCH + 8 * r + 8, :] * band[r : r + 1, :]
                for r in range(PATCH // 8)
            ]
            even, odd = sum(lines[2::2], lines[0]), sum(lines[3::2], lines[1])
            for dy in range(3):
                at = ((dy * 3 + dx) * n_here + at_j) * 8
                acc[at : at + 8, :] = jnp.where(place == (dy - 1) % 16, even, 0.0) + jnp.where(
                    place == (dy + 7) % 16, odd, 0.0
                )
    total = acc[pl.ds(0, 9 * n_here, stride=8), :]
    for s in range(1, 8):
        total = total + acc[pl.ds(s, 9 * n_here, stride=8), :]
    weights = jnp.maximum(jnp.sum(total, axis=1, keepdims=True) * (1.0 / PATCH), 0.0)
    w = [weights[k * n_here : (k + 1) * n_here] for k in range(9)]
    scale = 1.0 / jnp.maximum(sum(w), 1.0)
    moves = (
        (w[6] + w[7] + w[8] - w[0] - w[1] - w[2]) * scale,
        (w[2] + w[5] + w[8] - w[0] - w[3] - w[6]) * scale,
    )
    here = pl.ds(pl.multiple_of(i * patch_cols + cols[0], 8), n_here)
    share = smooth[cols[0] : cols[0] + n_here, :]
    return [jnp.sum((moves[c] + peak[c, here, :]) * share, axis=0, keepdims=True) for c in range(2)]


def put_lines(lines, i, patch_rows):
    at = lax.broadcasted_iota(jnp.int32, (8, LANES), 0)
    return sum(jnp.where(at == c * patch_rows + i, line, 0.0) for c, line in enumerate(lines))


def waiting_kernel(n_ty, swaps, peaks, mid, first, *rest):
    seconds, rest = rest[:EDGE_PARTS], rest[EDGE_PARTS:]
    turned_mid, turned_first, boundary, smooth, _ = rest[:5]
    rendered, turned_second, bands, peak, row_weights, flow, acc, whole, sems = rest[5:]
    n_rows, n_cols = boundary.shape
    patch_rows = n_rows // PATCH
    moves = [(mid, pl.ds(MARGIN, mid.shape[0]), pl.ds(0, n_cols))]
    wide = n_cols // EDGE_PARTS
    for edge, which, start in [(first, False, 0)] + [(e, True, k * wide) for k, e in enumerate(seconds)]:
        at = pl.multiple_of(jnp.where(takes_bottom(which), n_rows - MARGIN, 0), MARGIN)
        moves.append((edge, pl.ds(at, MARGIN), pl.ds(start, edge.shape[1])))
    copies = [pltpu.make_async_copy(a, rendered.at[b, c], sems.at[k]) for k, (a, b, c) in enumerate(moves)]
    fetch = pltpu.make_async_copy(boundary, whole, sems.at[len(moves)])
    has_boundary = lax.axis_index("gz") == 0

    @pl.when(has_boundary)
    def _():
        fetch.start()

    for copy in copies:
        copy.start()
    flow[...] = jnp.zeros_like(flow)
    for k, edge in enumerate(seconds):
        turn_patches(peaks, edge_patch_row(True, patch_rows), slice(None), edge, turned_second, k * (wide // PATCH))
    plan_windows(peaks, bands, peak)
    fill_row_weights(n_ty, swaps, patch_rows, row_weights)

    @pl.when(has_boundary)
    def _():
        fetch.wait()

        @pl.loop(0, patch_rows)
        def _(k):
            i = jnp.where(k == 0, edge_patch_row(False, patch_rows), edge_patch_row(True, patch_rows))
            at_edge = pl.multiple_of(i * (n_rows - MARGIN), MARGIN)
            at_mid = pl.multiple_of(MARGIN + i * MARGIN, MARGIN)

            def old_of(j):
                cols = slice(j * PATCH, (j + 1) * PATCH)
                return jnp.concatenate([whole[pl.ds(at_edge, MARGIN), cols], whole[pl.ds(at_mid, MARGIN), cols]], axis=0)

            def flow_with(turned_edge):
                flow[...] += put_lines(
                    patch_row_flow(i, range(n_cols // PATCH), turned_edge, turned_mid, bands, peak, smooth, old_of, acc), i, patch_rows
                )

            @pl.when(k == 0)
            def _():
                flow_with(turned_first)

            @pl.when(k != 0)
            def _():
                flow_with(turned_second)

    for copy in copies:
        copy.wait()


def window_kernel(second, cols, turned_mid, turned_edge, bands, peak, old_mid, old_edge, smooth, before, out_ref, acc):
    patch_rows = old_mid.shape[0] // MARGIN
    out_ref[...] = before[...]

    @pl.when(lax.axis_index("gz") != 0)
    def _():
        i = edge_patch_row(second, patch_rows)
        at_mid = pl.multiple_of(i * MARGIN, MARGIN)

        def old_of(j):
            here = slice((j - cols[0]) * PATCH, (j - cols[0] + 1) * PATCH)
            there = slice(j * PATCH, (j + 1) * PATCH)
            return jnp.concatenate([old_edge[:, here], old_mid[pl.ds(at_mid, MARGIN), there]], axis=0)

        lines = patch_row_flow(i, cols, turned_edge, turned_mid, bands, peak, smooth, old_of, acc)
        out_ref[...] = before[...] + put_lines(lines, i, patch_rows)


def fill_row_weights(n_ty, swaps, patch_rows, out_ref):
    all_rows = n_ty * patch_rows
    tile = lax.axis_index("ty")
    held = 2 * patch_rows
    depth = LANES
    at = lax.broadcasted_iota(jnp.int32, (8, depth), 0)
    slot = lax.broadcasted_iota(jnp.int32, (8, depth), 1)
    holder = jnp.full((8, depth), tile, jnp.int32)
    even_chip = (lax.axis_index("gz") // 2) % 2 == 0
    for k, (step, other) in enumerate(swaps):
        partner = jnp.where(even_chip, partner_of(tile, *step), partner_of(tile, *other))
        holder = jnp.where((slot >> 3) == k + 1, partner, holder)
    inner = slot & 7
    c_out = (at >= patch_rows).astype(jnp.int32)
    c_in = (inner >= patch_rows).astype(jnp.int32)
    row = tile * patch_rows + at - c_out * patch_rows
    source = holder * patch_rows + inner - c_in * patch_rows

    def inside(r):
        return (r >= 0) & (r < all_rows)

    def tap(delta):
        size = jnp.abs(delta)
        return jnp.where(
            size == 0, TAPS[2], jnp.where(size == 1, TAPS[1], jnp.where(size == 2, TAPS[0], 0.0))
        )

    def norm(r):
        return sum(jnp.where(inside(r + o), TAPS[o + 2], 0.0) for o in range(-2, 3))

    weight = jnp.zeros((8, depth), f32)
    for o in range(-2, 3):
        weight = weight + jnp.where(inside(row + o), TAPS[o + 2] * tap(source - row - o) / norm(row + o), 0.0)
    used = (inner < held) & (at < held) & (c_in == c_out) & inside(source)
    weight = jnp.where(used, weight / norm(row), 0.0)
    for k in range(len(swaps) + 1):
        for b in range(held):
            out_ref[k * held + b] = jnp.broadcast_to(weight[:, 8 * k + b : 8 * k + b + 1], (8, LANES))


def rows_kernel(row_weights, *refs):
    blocks, out_ref = refs[:-1], refs[-1]
    patch_rows, patch_cols = out_ref.shape[2], out_ref.shape[3]
    held = 2 * patch_rows
    result = None
    for k, block in enumerate(blocks):
        for b in range(held):
            term = row_weights[k * held + b] * block[b : b + 1, :]
            result = term if result is None else result + term
    for c in range(2):
        out_ref[c, 0] = result[c * patch_rows : (c + 1) * patch_rows, :patch_cols]


def column_smoother(n):
    kernel = np.zeros((n, n))
    for i in range(n):
        for o in range(-2, 3):
            if 0 <= i + o < n:
                kernel[i, i + o] = TAPS[o + 2]
    kernel = kernel / kernel.sum(1, keepdims=True)
    table = np.zeros((n, LANES), np.float32)
    table[:, :n] = np.linalg.matrix_power(kernel, SMOOTH_PASSES).T
    return table


def call(body, out_shape, in_specs, out_specs, scratch=(), flops=0, moved=0):
    return pl.pallas_call(
        body,
        out_shape=out_shape,
        in_specs=in_specs,
        out_specs=out_specs,
        scratch_shapes=scratch,
        compiler_params=pltpu.CompilerParams(vmem_limit_bytes=VMEM_LIMIT),
        cost_estimate=pl.CostEstimate(flops=flops, bytes_accessed=moved, transcendentals=0),
    )


def in_hbm(x):
    return pltpu.with_memory_space_constraint(x, pltpu.HBM)


def local(sections, boundary, row_shift, row_frac, col_shift, col_frac, peak_shift):
    section = sections[0]
    n_rows, n_cols = section.shape
    n_ty, n_gz, n_parts = lax.axis_size("ty"), lax.axis_size("gz"), lax.axis_size("parts")
    patch_rows, patch_cols = n_rows // PATCH, n_cols // PATCH
    n_patches = patch_rows * patch_cols
    all_rows = n_rows * n_ty
    n_mid, half = n_rows - 2 * MARGIN, n_rows // 2
    n_blocks = n_cols // BLOCK
    vmem = pl.BlockSpec(memory_space=pltpu.VMEM)
    smem = pl.BlockSpec(memory_space=pltpu.SMEM)
    hbm = pl.BlockSpec(memory_space=pltpu.HBM)
    unread = pl.BlockSpec(memory_space=pl.ANY)
    shape = jax.ShapeDtypeStruct
    to_next = [(i, (i + 1) % n_gz) for i in range(n_gz)]

    reach = -(-2 * SMOOTH_PASSES // patch_rows)
    far = [(d, other) for d in range(reach, 1, -1) for other in (False, True)]
    swaps = list(zip([(1, False), *far, (1, True)], [(1, True), *far, (1, False)]))
    swaps = [steps for steps in swaps if any(has_partners(n_ty, *step) for step in steps)]
    routes = [swap_table(n_gz, n_ty, steps) for steps in swaps]

    early = max(1, min(n_blocks - 1, int(n_blocks * EARLY_BLOCKS)))
    window = BLOCK + 2 * LANES
    held = section
    send_first, row_pos, col_pos, tables = call(
        functools.partial(fetch_kernel, all_rows),
        (
            shape((MARGIN, n_cols), bf16),
            shape((1, n_rows), f32),
            shape((1, n_cols), f32),
            shape((early, window, BLOCK), bf16),
        ),
        [hbm] * 5,
        [vmem] * 4,
        [
            pltpu.VMEM((1, n_rows), jnp.int32),
            pltpu.VMEM((1, n_rows), jnp.int32),
            pltpu.VMEM((1, n_cols), jnp.int32),
            pltpu.VMEM((1, n_cols), jnp.int32),
            pltpu.SemaphoreType.DMA((5,)),
        ],
        flops=0,
        moved=0,
    )(*(in_hbm(x) for x in (section, row_shift, row_frac, col_shift, col_frac)))
    first = lax.ppermute(send_first, ("parts", "gz", "ty"), halo_table(n_parts, n_gz, n_ty, False))

    edge_shape = shape((MARGIN, MARGIN + half), bf16)
    mid, more_tables, first_table, second_table = call(
        middle_kernel,
        (shape((n_mid, n_cols), bf16), shape((n_blocks - early, window, BLOCK), bf16), edge_shape, edge_shape),
        [vmem] * 4,
        [vmem] * 4,
        [pltpu.VMEM((n_mid, n_cols + 2 * LANES), bf16)],
    )(held, row_pos, col_pos, tables)
    old_mid = lax.ppermute(mid, "gz", to_next)
    turned_mid = call(
        turn_middle_kernel,
        shape((3 * n_patches, MARGIN, LANES), bf16),
        [smem, vmem],
        vmem,
        flops=1_000_000_000,
        moved=3_000_000,
    )(peak_shift, mid)

    send_second = call(send_kernel, shape((MARGIN, n_cols), bf16), [vmem, unread], vmem, flops=4_000_000_000)(
        held, turned_mid
    )
    second = lax.ppermute(send_second, ("parts", "gz", "ty"), halo_table(n_parts, n_gz, n_ty, True))
    def render_edges(which, parts, *args):
        return call(
            functools.partial(edges_kernel, which, parts),
            [shape((MARGIN, n_cols // parts), bf16)] * parts,
            [vmem] * 5 + [unread] * (len(args) - 5),
            [vmem] * parts,
            [pltpu.VMEM((MARGIN, n_cols + 2 * LANES), bf16)],
        )(*args)

    turned_shape = shape((3 * patch_cols, MARGIN, LANES), bf16)
    (first_edge,) = render_edges(False, 1, first, held, first_table, tables, more_tables, send_second)
    old_first = lax.ppermute(first_edge, "gz", to_next)
    turned_first = call(
        functools.partial(turn_first_kernel, patch_rows),
        turned_shape,
        [smem, vmem],
        vmem,
        flops=500_000_000,
        moved=1_000_000,
    )(peak_shift, first_edge)
    second_edges = render_edges(True, EDGE_PARTS, second, held, second_table, tables, more_tables, turned_first)
    part_cols = patch_cols // EDGE_PARTS
    old_seconds = [lax.ppermute(e, "gz", to_next) for e in second_edges]
    smooth = jnp.asarray(column_smoother(patch_cols))
    acc = pltpu.VMEM((9 * patch_cols * 8, LANES), f32)
    terms = (len(swaps) + 1) * 2 * patch_rows
    rendered, turned_second, bands, peak, row_weights, payload = call(
        functools.partial(waiting_kernel, n_ty, tuple(swaps)),
        (
            shape((n_rows, n_cols), bf16),
            turned_shape,
            shape((n_patches, PATCH // 8, LANES), f32),
            shape((2, n_patches, LANES), f32),
            shape((terms, 8, LANES), f32),
            shape((8, LANES), f32),
        ),
        [smem] + [vmem] * (4 + EDGE_PARTS) + [hbm, vmem, unread],
        [hbm] + [vmem] * 5,
        [acc, pltpu.VMEM((n_rows, n_cols), bf16), pltpu.SemaphoreType.DMA((3 + EDGE_PARTS,))],
        flops=1_000_000_000,
        moved=3_000_000,
    )(peak_shift, mid, first_edge, *second_edges, turned_mid, turned_first, in_hbm(boundary), smooth, old_mid)
    windows = [(True, range(patch_cols), turned_second, old_first)]
    for k, old in enumerate(old_seconds):
        windows.append((False, range(k * part_cols, (k + 1) * part_cols), turned_first, old))
    for which, cols, turned, old in windows:
        payload = call(
            functools.partial(window_kernel, which, cols), shape((8, LANES), f32), [vmem] * 8, vmem, [acc]
        )(turned_mid, turned, bands, peak, old_mid, old, smooth, payload)
    blocks = [payload] + [lax.ppermute(payload, ("gz", "ty"), route) for route in routes]
    flow = call(
        rows_kernel, shape((2, 1, patch_rows, patch_cols), f32), [vmem] * (1 + len(blocks)), vmem
    )(row_weights, *blocks)
    return rendered[None], flow


def solution(mesh):
    in_specs = (
        P(("parts", "gz"), "ty", None),
        P(("parts", "ty"), None),
        P(("parts", "gz"), "ty"),
        P(("parts", "gz"), "ty"),
        P(("parts", "gz"), None),
        P(("parts", "gz"), None),
        P(None, ("parts", "gz"), "ty", None),
    )
    out_specs = (P(("parts", "gz"), "ty", None), P(None, ("parts", "gz"), "ty", None))
    return jax.shard_map(local, mesh=mesh, in_specs=in_specs, out_specs=out_specs, check_vma=False)
```

```python
import functools

import jax
import jax.numpy as jnp
import numpy as np
from jax import lax
from jax.experimental import pallas as pl
from jax.experimental.pallas import tpu as pltpu
from jax.sharding import PartitionSpec as P

PATCH = 128
MARGIN = 64
SMOOTH_PASSES = 2
BLOCK = 256
LANES = 128
TAPS = (0.0625, 0.25, 0.375, 0.25, 0.0625)
FAR = 1 << 20
VMEM_LIMIT = 16 * 1024 * 1024
TURN_UNROLL = 16
PLAN_UNROLL = 8
EARLY_BLOCKS = 6 / 8
EDGE_PARTS = 2

f32 = jnp.float32
bf16 = jnp.bfloat16


def swap_table(n_gz, n_ty, steps):
    table = []
    for z in range(n_gz):
        d, second = steps[z // 2 % 2]
        for t in range(n_ty):
            partner = t + d if ((t // d) % 2 == 0) != second else t - d
            if 0 <= partner < n_ty:
                table.append((z * n_ty + t, z * n_ty + partner))
            elif (z ^ 1) < n_gz:
                table.append((z * n_ty + t, (z ^ 1) * n_ty + t))
    return tuple(table)


def halo_table(n_parts, n_gz, n_ty, second):
    table = []
    for p in range(n_parts):
        for z in range(n_gz):
            for t in range(n_ty):
                partner = t + 1 if (t % 2 == 0) != (second != (z % 2 == 1)) else t - 1
                if 0 <= partner < n_ty:
                    there = (p, z, partner)
                elif (p ^ 1) < n_parts:
                    there = (p ^ 1, z, t)
                else:
                    continue
                table.append(tuple((a * n_gz + b) * n_ty + c for a, b, c in ((p, z, t), there)))
    return tuple(table)


def next_chip_table(n_parts, n_gz):
    table = []
    for p in range(n_parts):
        for z in range(n_gz):
            partner = z + 1 if z % 2 else z - 1
            if 0 <= partner < n_gz:
                there = (p, partner)
            elif (p ^ 1) < n_parts:
                there = (p ^ 1, z)
            else:
                continue
            table.append((p * n_gz + z, there[0] * n_gz + there[1]))
    return tuple(table)


def partner_of(tile, d, second):
    up = (tile // d) % 2 == int(second)
    return tile + jnp.where(up, d, -d)


def has_partners(n_ty, d, second):
    return any(((t // d) % 2 == 0) != second and t + d < n_ty for t in range(n_ty))


def takes_bottom(second):
    return (lax.axis_index("ty") + lax.axis_index("gz")) % 2 == int(second)


def hat(coord, position):
    return jnp.maximum(1.0 - jnp.abs(coord - position), 0.0)


def source_positions(ids, shift, frac, limit, base):
    source = jnp.clip(ids + shift, 0, limit) - base
    return source.astype(f32) + frac.astype(f32) * (1.0 / 256.0)


def times(left, right):
    return jnp.dot(left, right, preferred_element_type=f32).astype(bf16)


def build_tables(col_pos, first, tables):
    reach = BLOCK + LANES
    whole = (reach, BLOCK)
    slot = lax.broadcasted_iota(jnp.int16, whole, 0)
    edge = jnp.zeros((LANES // 2, BLOCK), bf16)

    @pl.loop(0, tables.shape[0])
    def _(k):
        at = pl.multiple_of((first + k) * BLOCK, BLOCK)
        pos = col_pos[:, pl.ds(at, BLOCK)] - at.astype(f32) + float(LANES // 2)
        low = pos.astype(jnp.int32)
        part = pos - low.astype(f32)
        near = jnp.broadcast_to(low, whole).astype(jnp.int16)
        left = jnp.broadcast_to(1.0 - part, whole).astype(bf16)
        right = jnp.broadcast_to(part, whole).astype(bf16)
        weight = jnp.where(slot == near, left, jnp.where(slot == near + 1, right, jnp.zeros((), bf16)))
        tables[k, 0 : LANES // 2, :] = edge
        tables[k, LANES // 2 : LANES // 2 + reach, :] = weight
        tables[k, LANES // 2 + reach :, :] = edge


def fetch_kernel(all_rows, section, row_shift, row_frac, col_shift, col_frac, *rest):
    send_first, row_pos, col_pos, tables = rest[:4]
    row_shift_v, row_frac_v, col_shift_v, col_frac_v, sems = rest[4:]
    n_rows, n_cols = section.shape
    base = lax.axis_index("ty") * n_rows
    at = pl.multiple_of(jnp.where(takes_bottom(False), n_rows - MARGIN, 0), MARGIN)
    copies = [
        pltpu.make_async_copy(source, target, sems.at[k])
        for k, (source, target) in enumerate(
            (
                (col_shift, col_shift_v),
                (col_frac, col_frac_v),
                (row_shift, row_shift_v),
                (row_frac, row_frac_v),
                (section.at[pl.ds(at, MARGIN), :], send_first),
            )
        )
    ]
    for copy in copies:
        copy.start()
    for copy in copies[:4]:
        copy.wait()
    ids = lax.broadcasted_iota(jnp.int32, (1, n_cols), 1)
    col_pos[...] = source_positions(ids, col_shift_v[...], col_frac_v[...], n_cols - 2, 0)
    ids = lax.broadcasted_iota(jnp.int32, (1, n_rows), 1) + base
    row_pos[...] = source_positions(ids, row_shift_v[...], row_frac_v[...], all_rows - 2, base)
    build_tables(col_pos, 0, tables)
    for copy in copies[4:]:
        copy.wait()


def columns_of(mix, tables, *out_refs):
    j = 0
    wide = out_refs[0].shape[1] // BLOCK
    for table in tables:
        for k in range(table.shape[0]):
            at = j % wide
            out_refs[j // wide][:, at * BLOCK : (at + 1) * BLOCK] = times(
                mix[:, j * BLOCK : (j + 1) * BLOCK + 2 * LANES], table[k]
            )
            j += 1


def clear_sides(mix):
    edge = jnp.zeros((mix.shape[0], LANES), bf16)
    mix[:, 0:LANES] = edge
    mix[:, mix.shape[1] - LANES :] = edge


def edge_table(second, row_pos, table):
    n_rows = row_pos.shape[1]
    half = n_rows // 2
    slot = lax.broadcasted_iota(jnp.int32, (MARGIN + half, MARGIN), 0)
    bottom = takes_bottom(second)
    start = jnp.where(
        slot < MARGIN, jnp.where(bottom, n_rows, -MARGIN), jnp.where(bottom, half - MARGIN, -MARGIN)
    )
    here = jnp.where(bottom, row_pos[:, n_rows - MARGIN :], row_pos[:, :MARGIN])
    table[...] = hat((slot + start).astype(f32), here).T.astype(bf16)


def middle_kernel(held, row_pos, col_pos, tables, mid_ref, more_tables, first_table, second_table, mix):
    n_rows, n_cols = held.shape
    build_tables(col_pos, tables.shape[0], more_tables)
    edge_table(False, row_pos, first_table)
    edge_table(True, row_pos, second_table)
    coord = lax.broadcasted_iota(jnp.int32, (n_rows, n_rows - 2 * MARGIN), 0).astype(f32)
    mid_table = hat(coord, row_pos[:, MARGIN : n_rows - MARGIN]).T.astype(bf16)
    clear_sides(mix)
    for j in range(n_cols // BLOCK):
        mix[:, LANES + j * BLOCK : LANES + (j + 1) * BLOCK] = times(
            mid_table, held[:, j * BLOCK : (j + 1) * BLOCK]
        )
    columns_of(mix, (tables, more_tables), mid_ref)


def send_kernel(held, _, send_second):
    n_rows = held.shape[0]
    at = pl.multiple_of(jnp.where(takes_bottom(True), n_rows - MARGIN, 0), MARGIN)
    send_second[...] = held[pl.ds(at, MARGIN), :]


def edges_kernel(second, parts, halo, held, table, tables, more_tables, *rest):
    edge_refs, mix = rest[-1 - parts : -1], rest[-1]
    n_rows, n_cols = held.shape
    half = n_rows // 2
    own = pl.ds(pl.multiple_of(jnp.where(takes_bottom(second), half, 0), half), half)
    clear_sides(mix)
    for j in range(n_cols // BLOCK):
        here = slice(j * BLOCK, (j + 1) * BLOCK)
        stack = jnp.concatenate([halo[:, here], held[own, here]], axis=0)
        mix[:, LANES + j * BLOCK : LANES + (j + 1) * BLOCK] = times(table[...], stack)
    columns_of(mix, (tables, more_tables), *edge_refs)


def turn_patches(peaks, i, rows, source, turned, first):
    patch_cols = source.shape[1] // PATCH
    n_turned = turned.shape[0] // 3
    first_col = first % peaks.shape[3]

    @pl.loop(0, patch_cols, unroll=min(TURN_UNROLL, patch_cols))
    def _(j):
        block = source[rows, pl.ds(pl.multiple_of(j * PATCH, PATCH), PATCH)]
        for dx in range(3):
            turned[dx * n_turned + first + j] = pltpu.roll(block, (peaks[1, 0, i, first_col + j] + (dx - 1)) % PATCH, 1)


def plan_windows(peaks, bands, peak):
    lane = lax.broadcasted_iota(jnp.int32, (PATCH // 8, LANES), 1)
    offset = lane - 8 * lax.broadcasted_iota(jnp.int32, (PATCH // 8, LANES), 0) + 1
    patch_rows, patch_cols = peaks.shape[2:]
    for i in range(patch_rows):

        @pl.loop(0, patch_cols, unroll=PLAN_UNROLL)
        def _(j):
            p = i * patch_cols + j
            bands[p] = jnp.where(((offset - peaks[0, 0, i, j]) & (PATCH - 1)) <= 9, 1.0, 0.0)
            for c in range(2):
                peak[c, pl.ds(p, 1), :] = jnp.full((1, LANES), peaks[c, 0, i, j], jnp.int32).astype(f32)


def turn_middle_kernel(peaks, mid, turned):
    for i in range(mid.shape[0] // MARGIN):
        turn_patches(peaks, i, slice(i * MARGIN, (i + 1) * MARGIN), mid, turned, i * (mid.shape[1] // PATCH))


def edge_patch_row(second, patch_rows):
    return jnp.where(takes_bottom(second), patch_rows - 1, 0)


def patch_row_flow(i, cols, turned_edge, turned_mid, bands, peak, smooth, old_of, acc):
    patch_cols = turned_edge.shape[0] // 3
    n_patches = bands.shape[0]
    lane = lax.broadcasted_iota(jnp.int32, (8, LANES), 1) - lax.broadcasted_iota(jnp.int32, (8, LANES), 0)
    n_here = len(cols)
    for at_j, j in enumerate(cols):
        p = i * patch_cols + j
        left = []
        for dx in range(3):
            left += [turned_edge[dx * patch_cols + j], turned_mid[dx * n_patches + p]]
        products = lax.dot_general(
            jnp.concatenate(left, axis=0), old_of(j), (((1,), (1,)), ((), ())), preferred_element_type=f32
        )
        band = bands[p]
        place = (lane - peak[0, pl.ds(p, 1), :].astype(jnp.int32)) & 15
        for dx in range(3):
            lines = [
                products[dx * PATCH + 8 * r : dx * PATCH + 8 * r + 8, :] * band[r : r + 1, :]
                for r in range(PATCH // 8)
            ]
            even, odd = sum(lines[2::2], lines[0]), sum(lines[3::2], lines[1])
            for dy in range(3):
                at = ((dy * 3 + dx) * n_here + at_j) * 8
                acc[at : at + 8, :] = jnp.where(place == (dy - 1) % 16, even, 0.0) + jnp.where(
                    place == (dy + 7) % 16, odd, 0.0
                )
    total = acc[pl.ds(0, 9 * n_here, stride=8), :]
    for s in range(1, 8):
        total = total + acc[pl.ds(s, 9 * n_here, stride=8), :]
    weights = jnp.maximum(jnp.sum(total, axis=1, keepdims=True) * (1.0 / PATCH), 0.0)
    w = [weights[k * n_here : (k + 1) * n_here] for k in range(9)]
    scale = 1.0 / jnp.maximum(sum(w), 1.0)
    moves = (
        (w[6] + w[7] + w[8] - w[0] - w[1] - w[2]) * scale,
        (w[2] + w[5] + w[8] - w[0] - w[3] - w[6]) * scale,
    )
    here = pl.ds(pl.multiple_of(i * patch_cols + cols[0], 8), n_here)
    share = smooth[cols[0] : cols[0] + n_here, :]
    return [jnp.sum((moves[c] + peak[c, here, :]) * share, axis=0, keepdims=True) for c in range(2)]


def put_lines(lines, i, patch_rows):
    at = lax.broadcasted_iota(jnp.int32, (8, LANES), 0)
    return sum(jnp.where(at == c * patch_rows + i, line, 0.0) for c, line in enumerate(lines))


def boundary_flow(i, patch_rows, turned_edge, turned_mid, bands, peak, whole, smooth, acc):
    at_edge = pl.multiple_of(i * PATCH + jnp.where(i == 0, 0, PATCH - MARGIN), MARGIN)
    at_mid = pl.multiple_of(i * PATCH + jnp.where(i == 0, MARGIN, 0), MARGIN)

    def old_of(j):
        here = slice(j * PATCH, (j + 1) * PATCH)
        return jnp.concatenate([whole[pl.ds(at_edge, MARGIN), here], whole[pl.ds(at_mid, MARGIN), here]], axis=0)

    cols = range(whole.shape[1] // PATCH)
    return put_lines(
        patch_row_flow(i, cols, turned_edge, turned_mid, bands, peak, smooth, old_of, acc), i, patch_rows
    )


def first_waiting_kernel(n_ty, swaps, peaks, edge, turned_mid, boundary, smooth, *rest):
    turned, bands, peak, row_weights, flow, whole, acc, sem = rest
    patch_rows = boundary.shape[0] // PATCH
    i = edge_patch_row(False, patch_rows)
    fetch = pltpu.make_async_copy(boundary, whole, sem)
    has_boundary = lax.axis_index("gz") == 0

    @pl.when(has_boundary)
    def _():
        fetch.start()

    flow[...] = jnp.zeros_like(flow)
    turn_patches(peaks, i, slice(None), edge, turned, 0)
    plan_windows(peaks, bands, peak)
    fill_row_weights(n_ty, swaps, patch_rows, row_weights)

    @pl.when(has_boundary)
    def _():
        fetch.wait()
        flow[...] = boundary_flow(i, patch_rows, turned, turned_mid, bands, peak, whole, smooth, acc)


def waiting_kernel(peaks, mid, first, *rest):
    seconds, rest = rest[:EDGE_PARTS], rest[EDGE_PARTS:]
    turned_mid, bands, peak, whole, smooth, before, _ = rest[:7]
    rendered, turned, flow, acc, sems = rest[7:]
    n_rows, n_cols = whole.shape
    patch_rows = n_rows // PATCH
    moves = [(mid, pl.ds(MARGIN, mid.shape[0]), pl.ds(0, n_cols))]
    wide = n_cols // EDGE_PARTS
    for edge, which, start in [(first, False, 0)] + [(e, True, k * wide) for k, e in enumerate(seconds)]:
        at = pl.multiple_of(jnp.where(takes_bottom(which), n_rows - MARGIN, 0), MARGIN)
        moves.append((edge, pl.ds(at, MARGIN), pl.ds(start, edge.shape[1])))
    copies = [pltpu.make_async_copy(a, rendered.at[b, c], sems.at[k]) for k, (a, b, c) in enumerate(moves)]
    i = edge_patch_row(True, patch_rows)
    has_boundary = lax.axis_index("gz") == 0
    for copy in copies:
        copy.start()
    flow[...] = before[...]
    for k, edge in enumerate(seconds):
        turn_patches(peaks, i, slice(None), edge, turned, k * (wide // PATCH))

    @pl.when(has_boundary)
    def _():
        flow[...] = before[...] + boundary_flow(
            i, patch_rows, turned, turned_mid, bands, peak, whole, smooth, acc
        )

    for copy in copies:
        copy.wait()


def window_kernel(second, cols, turned_mid, turned_edge, bands, peak, old_mid, smooth, before, *rest):
    old_edges, (out_ref, acc) = rest[:-2], rest[-2:]
    patch_rows = old_mid.shape[0] // MARGIN
    out_ref[...] = before[...]
    odd = lax.axis_index("gz") % 2 == 1

    @pl.when(lax.axis_index("gz") != 0)
    def _():
        i = edge_patch_row(second, patch_rows)
        at_mid = pl.multiple_of(i * MARGIN, MARGIN)

        def old_of(j):
            here = slice((j - cols[0]) * PATCH, (j - cols[0] + 1) * PATCH)
            there = slice(j * PATCH, (j + 1) * PATCH)
            old_edge = old_edges[0][:, here]
            for other in old_edges[1:]:
                old_edge = jnp.where(odd, other[:, here], old_edge)
            return jnp.concatenate([old_edge, old_mid[pl.ds(at_mid, MARGIN), there]], axis=0)

        lines = patch_row_flow(i, cols, turned_edge, turned_mid, bands, peak, smooth, old_of, acc)
        out_ref[...] = before[...] + put_lines(lines, i, patch_rows)


def fill_row_weights(n_ty, swaps, patch_rows, out_ref):
    all_rows = n_ty * patch_rows
    tile = lax.axis_index("ty")
    held = 2 * patch_rows
    depth = LANES
    at = lax.broadcasted_iota(jnp.int32, (8, depth), 0)
    slot = lax.broadcasted_iota(jnp.int32, (8, depth), 1)
    holder = jnp.full((8, depth), tile, jnp.int32)
    even_chip = (lax.axis_index("gz") // 2) % 2 == 0
    for k, (step, other) in enumerate(swaps):
        partner = jnp.where(even_chip, partner_of(tile, *step), partner_of(tile, *other))
        holder = jnp.where((slot >> 3) == k + 1, partner, holder)
    inner = slot & 7
    c_out = (at >= patch_rows).astype(jnp.int32)
    c_in = (inner >= patch_rows).astype(jnp.int32)
    row = tile * patch_rows + at - c_out * patch_rows
    source = holder * patch_rows + inner - c_in * patch_rows

    def inside(r):
        return (r >= 0) & (r < all_rows)

    def tap(delta):
        size = jnp.abs(delta)
        return jnp.where(
            size == 0, TAPS[2], jnp.where(size == 1, TAPS[1], jnp.where(size == 2, TAPS[0], 0.0))
        )

    def norm(r):
        return sum(jnp.where(inside(r + o), TAPS[o + 2], 0.0) for o in range(-2, 3))

    weight = jnp.zeros((8, depth), f32)
    for o in range(-2, 3):
        weight = weight + jnp.where(inside(row + o), TAPS[o + 2] * tap(source - row - o) / norm(row + o), 0.0)
    used = (inner < held) & (at < held) & (c_in == c_out) & inside(source)
    weight = jnp.where(used, weight / norm(row), 0.0)
    for k in range(len(swaps) + 1):
        for b in range(held):
            out_ref[k * held + b] = jnp.broadcast_to(weight[:, 8 * k + b : 8 * k + b + 1], (8, LANES))


def rows_kernel(row_weights, *refs):
    blocks, out_ref = refs[:-1], refs[-1]
    patch_rows, patch_cols = out_ref.shape[2], out_ref.shape[3]
    held = 2 * patch_rows
    result = None
    for k, block in enumerate(blocks):
        for b in range(held):
            term = row_weights[k * held + b] * block[b : b + 1, :]
            result = term if result is None else result + term
    for c in range(2):
        out_ref[c, 0] = result[c * patch_rows : (c + 1) * patch_rows, :patch_cols]


def column_smoother(n):
    kernel = np.zeros((n, n))
    for i in range(n):
        for o in range(-2, 3):
            if 0 <= i + o < n:
                kernel[i, i + o] = TAPS[o + 2]
    kernel = kernel / kernel.sum(1, keepdims=True)
    table = np.zeros((n, LANES), np.float32)
    table[:, :n] = np.linalg.matrix_power(kernel, SMOOTH_PASSES).T
    return table


def call(body, out_shape, in_specs, out_specs, scratch=(), flops=0, moved=0):
    return pl.pallas_call(
        body,
        out_shape=out_shape,
        in_specs=in_specs,
        out_specs=out_specs,
        scratch_shapes=scratch,
        compiler_params=pltpu.CompilerParams(vmem_limit_bytes=VMEM_LIMIT),
        cost_estimate=pl.CostEstimate(flops=flops, bytes_accessed=moved, transcendentals=0),
    )


def in_hbm(x):
    return pltpu.with_memory_space_constraint(x, pltpu.HBM)


def local(sections, boundary, row_shift, row_frac, col_shift, col_frac, peak_shift):
    section = sections[0]
    n_rows, n_cols = section.shape
    n_ty, n_gz, n_parts = lax.axis_size("ty"), lax.axis_size("gz"), lax.axis_size("parts")
    patch_rows, patch_cols = n_rows // PATCH, n_cols // PATCH
    n_patches = patch_rows * patch_cols
    all_rows = n_rows * n_ty
    n_mid, half = n_rows - 2 * MARGIN, n_rows // 2
    n_blocks = n_cols // BLOCK
    vmem = pl.BlockSpec(memory_space=pltpu.VMEM)
    smem = pl.BlockSpec(memory_space=pltpu.SMEM)
    hbm = pl.BlockSpec(memory_space=pltpu.HBM)
    unread = pl.BlockSpec(memory_space=pl.ANY)
    shape = jax.ShapeDtypeStruct
    to_next = [(i, (i + 1) % n_gz) for i in range(n_gz)]

    reach = -(-2 * SMOOTH_PASSES // patch_rows)
    far = [(d, other) for d in range(reach, 1, -1) for other in (False, True)]
    swaps = list(zip([(1, False), *far, (1, True)], [(1, True), *far, (1, False)]))
    swaps = [steps for steps in swaps if any(has_partners(n_ty, *step) for step in steps)]
    routes = [swap_table(n_gz, n_ty, steps) for steps in swaps]

    early = max(1, min(n_blocks - 1, int(n_blocks * EARLY_BLOCKS)))
    window = BLOCK + 2 * LANES
    held = section
    send_first, row_pos, col_pos, tables = call(
        functools.partial(fetch_kernel, all_rows),
        (
            shape((MARGIN, n_cols), bf16),
            shape((1, n_rows), f32),
            shape((1, n_cols), f32),
            shape((early, window, BLOCK), bf16),
        ),
        [hbm] * 5,
        [vmem] * 4,
        [
            pltpu.VMEM((1, n_rows), jnp.int32),
            pltpu.VMEM((1, n_rows), jnp.int32),
            pltpu.VMEM((1, n_cols), jnp.int32),
            pltpu.VMEM((1, n_cols), jnp.int32),
            pltpu.SemaphoreType.DMA((5,)),
        ],
        flops=0,
        moved=0,
    )(*(in_hbm(x) for x in (section, row_shift, row_frac, col_shift, col_frac)))
    first = lax.ppermute(send_first, ("parts", "gz", "ty"), halo_table(n_parts, n_gz, n_ty, False))

    edge_shape = shape((MARGIN, MARGIN + half), bf16)
    mid, more_tables, first_table, second_table = call(
        middle_kernel,
        (shape((n_mid, n_cols), bf16), shape((n_blocks - early, window, BLOCK), bf16), edge_shape, edge_shape),
        [vmem] * 4,
        [vmem] * 4,
        [pltpu.VMEM((n_mid, n_cols + 2 * LANES), bf16)],
    )(held, row_pos, col_pos, tables)
    old_mid = lax.ppermute(mid, "gz", to_next)
    turned_mid = call(
        turn_middle_kernel,
        shape((3 * n_patches, MARGIN, LANES), bf16),
        [smem, vmem],
        vmem,
        flops=1_000_000_000,
        moved=3_000_000,
    )(peak_shift, mid)

    send_second = call(send_kernel, shape((MARGIN, n_cols), bf16), [vmem, unread], vmem, flops=4_000_000_000)(
        held, turned_mid
    )
    second = lax.ppermute(send_second, ("parts", "gz", "ty"), halo_table(n_parts, n_gz, n_ty, True))
    def render_edges(which, parts, *args):
        return call(
            functools.partial(edges_kernel, which, parts),
            [shape((MARGIN, n_cols // parts), bf16)] * parts,
            [vmem] * 5 + [unread] * (len(args) - 5),
            [vmem] * parts,
            [pltpu.VMEM((MARGIN, n_cols + 2 * LANES), bf16)],
        )(*args)

    turned_shape = shape((3 * patch_cols, MARGIN, LANES), bf16)
    (first_edge,) = render_edges(False, 1, first, held, first_table, tables, more_tables, send_second)
    old_first = lax.ppermute(first_edge, "gz", to_next)
    smooth = jnp.asarray(column_smoother(patch_cols))
    acc = pltpu.VMEM((9 * patch_cols * 8, LANES), f32)
    line_shape = shape((8, LANES), f32)
    turned_first, bands, peak, row_weights, payload, old_boundary = call(
        functools.partial(first_waiting_kernel, n_ty, tuple(swaps)),
        (
            turned_shape,
            shape((n_patches, PATCH // 8, LANES), f32),
            shape((2, n_patches, LANES), f32),
            shape(((len(swaps) + 1) * 2 * patch_rows, 8, LANES), f32),
            line_shape,
            shape((n_rows, n_cols), bf16),
        ),
        [smem, vmem, vmem, hbm, vmem],
        [vmem] * 6,
        [acc, pltpu.SemaphoreType.DMA],
        flops=500_000_000,
        moved=1_000_000,
    )(peak_shift, first_edge, turned_mid, in_hbm(boundary), smooth)
    second_edges = render_edges(True, EDGE_PARTS, second, held, second_table, tables, more_tables, turned_first)
    part_cols = patch_cols // EDGE_PARTS
    old_seconds = [[lax.ppermute(e, "gz", to_next)] for e in second_edges[:-1]]
    in_chip = [(z, z ^ 1) for z in range(n_gz) if (z ^ 1) < n_gz]
    old_seconds.append(
        [
            lax.ppermute(second_edges[-1], ("parts", "gz"), next_chip_table(n_parts, n_gz)),
            lax.ppermute(second_edges[-1], "gz", in_chip),
        ]
    )
    rendered, turned_second, payload = call(
        waiting_kernel,
        (shape((n_rows, n_cols), bf16), turned_shape, line_shape),
        [smem] + [vmem] * (8 + EDGE_PARTS) + [unread],
        [hbm] + [vmem] * 2,
        [acc, pltpu.SemaphoreType.DMA((2 + EDGE_PARTS,))],
        flops=1_000_000_000,
        moved=3_000_000,
    )(
        peak_shift,
        mid,
        first_edge,
        *second_edges,
        turned_mid,
        bands,
        peak,
        old_boundary,
        smooth,
        payload,
        old_mid,
    )
    windows = [(True, range(patch_cols), turned_second, [old_first])]
    for k, old in enumerate(old_seconds):
        windows.append((False, range(k * part_cols, (k + 1) * part_cols), turned_first, old))
    for which, cols, turned, old in windows:
        payload = call(
            functools.partial(window_kernel, which, cols), line_shape, [vmem] * (7 + len(old)), vmem, [acc]
        )(turned_mid, turned, bands, peak, old_mid, smooth, payload, *old)
    blocks = [payload] + [lax.ppermute(payload, ("gz", "ty"), route) for route in routes]
    flow = call(
        rows_kernel, shape((2, 1, patch_rows, patch_cols), f32), [vmem] * (1 + len(blocks)), vmem
    )(row_weights, *blocks)
    return rendered[None], flow


def solution(mesh):
    in_specs = (
        P(("parts", "gz"), "ty", None),
        P(("parts", "ty"), None),
        P(("parts", "gz"), "ty"),
        P(("parts", "gz"), "ty"),
        P(("parts", "gz"), None),
        P(("parts", "gz"), None),
        P(None, ("parts", "gz"), "ty", None),
    )
    out_specs = (P(("parts", "gz"), "ty", None), P(None, ("parts", "gz"), "ty", None))
    return jax.shard_map(local, mesh=mesh, in_specs=in_specs, out_specs=out_specs, check_vma=False)
```

```python
import functools

import jax
import jax.numpy as jnp
import numpy as np
from jax import lax
from jax.experimental import pallas as pl
from jax.experimental.pallas import tpu as pltpu
from jax.sharding import PartitionSpec as P

PATCH = 128
MARGIN = 64
SMOOTH_PASSES = 2
BLOCK = 256
LANES = 128
TAPS = (0.0625, 0.25, 0.375, 0.25, 0.0625)
FAR = 1 << 20
VMEM_LIMIT = 16 * 1024 * 1024
TURN_UNROLL = 8
PLAN_UNROLL = 8
EARLY_BLOCKS = 6 / 8
EDGE_PARTS = 2

f32 = jnp.float32
bf16 = jnp.bfloat16


def swap_table(n_gz, n_ty, steps):
    table = []
    for z in range(n_gz):
        d, second = steps[z // 2 % 2]
        for t in range(n_ty):
            partner = t + d if ((t // d) % 2 == 0) != second else t - d
            if 0 <= partner < n_ty:
                table.append((z * n_ty + t, z * n_ty + partner))
            elif (z ^ 1) < n_gz:
                table.append((z * n_ty + t, (z ^ 1) * n_ty + t))
    return tuple(table)


def halo_table(n_parts, n_gz, n_ty, second):
    table = []
    for p in range(n_parts):
        for z in range(n_gz):
            for t in range(n_ty):
                partner = t + 1 if (t % 2 == 0) != (second != (z % 2 == 1)) else t - 1
                if 0 <= partner < n_ty:
                    there = (p, z, partner)
                elif (p ^ 1) < n_parts:
                    there = (p ^ 1, z, t)
                else:
                    continue
                table.append(tuple((a * n_gz + b) * n_ty + c for a, b, c in ((p, z, t), there)))
    return tuple(table)


def next_chip_table(n_parts, n_gz):
    table = []
    for p in range(n_parts):
        for z in range(n_gz):
            partner = z + 1 if z % 2 else z - 1
            if 0 <= partner < n_gz:
                there = (p, partner)
            elif (p ^ 1) < n_parts:
                there = (p ^ 1, z)
            else:
                continue
            table.append((p * n_gz + z, there[0] * n_gz + there[1]))
    return tuple(table)


def partner_of(tile, d, second):
    up = (tile // d) % 2 == int(second)
    return tile + jnp.where(up, d, -d)


def has_partners(n_ty, d, second):
    return any(((t // d) % 2 == 0) != second and t + d < n_ty for t in range(n_ty))


def takes_bottom(second):
    return (lax.axis_index("ty") + lax.axis_index("gz")) % 2 == int(second)


def hat(coord, position):
    return jnp.maximum(1.0 - jnp.abs(coord - position), 0.0)


def source_positions(ids, shift, frac, limit, base):
    source = jnp.clip(ids + shift, 0, limit) - base
    return source.astype(f32) + frac.astype(f32) * (1.0 / 256.0)


def times(left, right):
    return jnp.dot(left, right, preferred_element_type=f32).astype(bf16)


def build_tables(col_pos, first, tables):
    reach = BLOCK + LANES
    whole = (reach, BLOCK)
    slot = lax.broadcasted_iota(jnp.int16, whole, 0)
    edge = jnp.zeros((LANES // 2, BLOCK), bf16)

    @pl.loop(0, tables.shape[0])
    def _(k):
        at = pl.multiple_of((first + k) * BLOCK, BLOCK)
        pos = col_pos[:, pl.ds(at, BLOCK)] - at.astype(f32) + float(LANES // 2)
        low = pos.astype(jnp.int32)
        part = pos - low.astype(f32)
        near = jnp.broadcast_to(low, whole).astype(jnp.int16)
        left = jnp.broadcast_to(1.0 - part, whole).astype(bf16)
        right = jnp.broadcast_to(part, whole).astype(bf16)
        weight = jnp.where(slot == near, left, jnp.where(slot == near + 1, right, jnp.zeros((), bf16)))
        tables[k, 0 : LANES // 2, :] = edge
        tables[k, LANES // 2 : LANES // 2 + reach, :] = weight
        tables[k, LANES // 2 + reach :, :] = edge


def fetch_kernel(all_rows, section, row_shift, row_frac, col_shift, col_frac, *rest):
    send_first, row_pos, col_pos, tables = rest[:4]
    row_shift_v, row_frac_v, col_shift_v, col_frac_v, sems = rest[4:]
    n_rows, n_cols = section.shape
    base = lax.axis_index("ty") * n_rows
    at = pl.multiple_of(jnp.where(takes_bottom(False), n_rows - MARGIN, 0), MARGIN)
    copies = [
        pltpu.make_async_copy(source, target, sems.at[k])
        for k, (source, target) in enumerate(
            (
                (col_shift, col_shift_v),
                (col_frac, col_frac_v),
                (row_shift, row_shift_v),
                (row_frac, row_frac_v),
                (section.at[pl.ds(at, MARGIN), :], send_first),
            )
        )
    ]
    for copy in copies:
        copy.start()
    for copy in copies[:4]:
        copy.wait()
    ids = lax.broadcasted_iota(jnp.int32, (1, n_cols), 1)
    col_pos[...] = source_positions(ids, col_shift_v[...], col_frac_v[...], n_cols - 2, 0)
    ids = lax.broadcasted_iota(jnp.int32, (1, n_rows), 1) + base
    row_pos[...] = source_positions(ids, row_shift_v[...], row_frac_v[...], all_rows - 2, base)
    build_tables(col_pos, 0, tables)
    for copy in copies[4:]:
        copy.wait()


def columns_of(mix, tables, *out_refs):
    j = 0
    wide = out_refs[0].shape[1] // BLOCK
    for table in tables:
        for k in range(table.shape[0]):
            at = j % wide
            out_refs[j // wide][:, at * BLOCK : (at + 1) * BLOCK] = times(
                mix[:, j * BLOCK : (j + 1) * BLOCK + 2 * LANES], table[k]
            )
            j += 1


def clear_sides(mix):
    edge = jnp.zeros((mix.shape[0], LANES), bf16)
    mix[:, 0:LANES] = edge
    mix[:, mix.shape[1] - LANES :] = edge


def edge_table(second, row_pos, table):
    n_rows = row_pos.shape[1]
    half = n_rows // 2
    slot = lax.broadcasted_iota(jnp.int32, (MARGIN + half, MARGIN), 0)
    bottom = takes_bottom(second)
    start = jnp.where(
        slot < MARGIN, jnp.where(bottom, n_rows, -MARGIN), jnp.where(bottom, half - MARGIN, -MARGIN)
    )
    here = jnp.where(bottom, row_pos[:, n_rows - MARGIN :], row_pos[:, :MARGIN])
    table[...] = hat((slot + start).astype(f32), here).T.astype(bf16)


def middle_kernel(held, row_pos, col_pos, tables, mid_ref, more_tables, first_table, second_table, mix):
    n_rows, n_cols = held.shape
    build_tables(col_pos, tables.shape[0], more_tables)
    edge_table(False, row_pos, first_table)
    edge_table(True, row_pos, second_table)
    coord = lax.broadcasted_iota(jnp.int32, (n_rows, n_rows - 2 * MARGIN), 0).astype(f32)
    mid_table = hat(coord, row_pos[:, MARGIN : n_rows - MARGIN]).T.astype(bf16)
    clear_sides(mix)
    for j in range(n_cols // BLOCK):
        mix[:, LANES + j * BLOCK : LANES + (j + 1) * BLOCK] = times(
            mid_table, held[:, j * BLOCK : (j + 1) * BLOCK]
        )
    columns_of(mix, (tables, more_tables), mid_ref)


def send_kernel(held, _, send_second):
    n_rows = held.shape[0]
    at = pl.multiple_of(jnp.where(takes_bottom(True), n_rows - MARGIN, 0), MARGIN)
    send_second[...] = held[pl.ds(at, MARGIN), :]


def edges_kernel(second, parts, halo, held, table, tables, more_tables, *rest):
    edge_refs, mix = rest[-1 - parts : -1], rest[-1]
    n_rows, n_cols = held.shape
    half = n_rows // 2
    own = pl.ds(pl.multiple_of(jnp.where(takes_bottom(second), half, 0), half), half)
    clear_sides(mix)
    for j in range(n_cols // BLOCK):
        here = slice(j * BLOCK, (j + 1) * BLOCK)
        stack = jnp.concatenate([halo[:, here], held[own, here]], axis=0)
        mix[:, LANES + j * BLOCK : LANES + (j + 1) * BLOCK] = times(table[...], stack)
    columns_of(mix, (tables, more_tables), *edge_refs)


def turn_patches(peaks, i, rows, source, turned, first):
    patch_cols = source.shape[1] // PATCH
    n_turned = turned.shape[0] // 3
    first_col = first % peaks.shape[3]

    @pl.loop(0, patch_cols, unroll=min(TURN_UNROLL, patch_cols))
    def _(j):
        block = source[rows, pl.ds(pl.multiple_of(j * PATCH, PATCH), PATCH)]
        for dx in range(3):
            turned[dx * n_turned + first + j] = pltpu.roll(block, (peaks[1, 0, i, first_col + j] + (dx - 1)) % PATCH, 1)


def plan_windows(peaks, bands, peak):
    lane = lax.broadcasted_iota(jnp.int32, (PATCH // 8, LANES), 1)
    offset = lane - 8 * lax.broadcasted_iota(jnp.int32, (PATCH // 8, LANES), 0) + 1
    patch_rows, patch_cols = peaks.shape[2:]
    for i in range(patch_rows):

        @pl.loop(0, patch_cols, unroll=PLAN_UNROLL)
        def _(j):
            p = i * patch_cols + j
            bands[p] = jnp.where(((offset - peaks[0, 0, i, j]) & (PATCH - 1)) <= 9, 1.0, 0.0)
            for c in range(2):
                peak[c, pl.ds(p, 1), :] = jnp.full((1, LANES), peaks[c, 0, i, j], jnp.int32).astype(f32)


def turn_middle_kernel(peaks, mid, turned):
    for i in range(mid.shape[0] // MARGIN):
        turn_patches(peaks, i, slice(i * MARGIN, (i + 1) * MARGIN), mid, turned, i * (mid.shape[1] // PATCH))


def edge_patch_row(second, patch_rows):
    return jnp.where(takes_bottom(second), patch_rows - 1, 0)


def patch_row_flow(i, cols, turned_edge, turned_mid, bands, peak, smooth, old_of, acc):
    patch_cols = turned_edge.shape[0] // 3
    n_patches = bands.shape[0]
    lane = lax.broadcasted_iota(jnp.int32, (8, LANES), 1) - lax.broadcasted_iota(jnp.int32, (8, LANES), 0)
    n_here = len(cols)
    for at_j, j in enumerate(cols):
        p = i * patch_cols + j
        left = []
        for dx in range(3):
            left += [turned_edge[dx * patch_cols + j], turned_mid[dx * n_patches + p]]
        products = lax.dot_general(
            jnp.concatenate(left, axis=0), old_of(j), (((1,), (1,)), ((), ())), preferred_element_type=f32
        )
        band = bands[p]
        place = (lane - peak[0, pl.ds(p, 1), :].astype(jnp.int32)) & 15
        for dx in range(3):
            lines = [
                products[dx * PATCH + 8 * r : dx * PATCH + 8 * r + 8, :] * band[r : r + 1, :]
                for r in range(PATCH // 8)
            ]
            even, odd = sum(lines[2::2], lines[0]), sum(lines[3::2], lines[1])
            for dy in range(3):
                at = ((dy * 3 + dx) * n_here + at_j) * 8
                acc[at : at + 8, :] = jnp.where(place == (dy - 1) % 16, even, 0.0) + jnp.where(
                    place == (dy + 7) % 16, odd, 0.0
                )
    total = acc[pl.ds(0, 9 * n_here, stride=8), :]
    for s in range(1, 8):
        total = total + acc[pl.ds(s, 9 * n_here, stride=8), :]
    weights = jnp.maximum(jnp.sum(total, axis=1, keepdims=True) * (1.0 / PATCH), 0.0)
    w = [weights[k * n_here : (k + 1) * n_here] for k in range(9)]
    scale = 1.0 / jnp.maximum(sum(w), 1.0)
    moves = (
        (w[6] + w[7] + w[8] - w[0] - w[1] - w[2]) * scale,
        (w[2] + w[5] + w[8] - w[0] - w[3] - w[6]) * scale,
    )
    here = pl.ds(pl.multiple_of(i * patch_cols + cols[0], 8), n_here)
    share = smooth[cols[0] : cols[0] + n_here, :]
    return [jnp.sum((moves[c] + peak[c, here, :]) * share, axis=0, keepdims=True) for c in range(2)]


def put_lines(lines, i, patch_rows):
    at = lax.broadcasted_iota(jnp.int32, (8, LANES), 0)
    return sum(jnp.where(at == c * patch_rows + i, line, 0.0) for c, line in enumerate(lines))


def boundary_flow(i, patch_rows, turned_edge, turned_mid, bands, peak, whole, smooth, acc):
    at_edge = pl.multiple_of(i * PATCH + jnp.where(i == 0, 0, PATCH - MARGIN), MARGIN)
    at_mid = pl.multiple_of(i * PATCH + jnp.where(i == 0, MARGIN, 0), MARGIN)

    def old_of(j):
        here = slice(j * PATCH, (j + 1) * PATCH)
        return jnp.concatenate([whole[pl.ds(at_edge, MARGIN), here], whole[pl.ds(at_mid, MARGIN), here]], axis=0)

    cols = range(whole.shape[1] // PATCH)
    return put_lines(
        patch_row_flow(i, cols, turned_edge, turned_mid, bands, peak, smooth, old_of, acc), i, patch_rows
    )


def first_waiting_kernel(n_ty, swaps, peaks, edge, turned_mid, boundary, smooth, *rest):
    turned, bands, peak, row_weights, flow, whole, acc, sem = rest
    patch_rows = boundary.shape[0] // PATCH
    i = edge_patch_row(False, patch_rows)
    fetch = pltpu.make_async_copy(boundary, whole, sem)
    has_boundary = lax.axis_index("gz") == 0

    @pl.when(has_boundary)
    def _():
        fetch.start()

    flow[...] = jnp.zeros_like(flow)
    turn_patches(peaks, i, slice(None), edge, turned, 0)
    plan_windows(peaks, bands, peak)
    fill_row_weights(n_ty, swaps, patch_rows, row_weights)

    @pl.when(has_boundary)
    def _():
        fetch.wait()
        flow[...] = boundary_flow(i, patch_rows, turned, turned_mid, bands, peak, whole, smooth, acc)


def waiting_kernel(peaks, mid, first, *rest):
    seconds, rest = rest[:EDGE_PARTS], rest[EDGE_PARTS:]
    turned_mid, bands, peak, whole, smooth, before, _ = rest[:7]
    rendered, turned, flow, acc, sems = rest[7:]
    n_rows, n_cols = whole.shape
    patch_rows = n_rows // PATCH
    moves = [(mid, pl.ds(MARGIN, mid.shape[0]), pl.ds(0, n_cols))]
    wide = n_cols // EDGE_PARTS
    for edge, which, start in [(first, False, 0)] + [(e, True, k * wide) for k, e in enumerate(seconds)]:
        at = pl.multiple_of(jnp.where(takes_bottom(which), n_rows - MARGIN, 0), MARGIN)
        moves.append((edge, pl.ds(at, MARGIN), pl.ds(start, edge.shape[1])))
    copies = [pltpu.make_async_copy(a, rendered.at[b, c], sems.at[k]) for k, (a, b, c) in enumerate(moves)]
    i = edge_patch_row(True, patch_rows)
    has_boundary = lax.axis_index("gz") == 0
    for copy in copies:
        copy.start()
    flow[...] = before[...]
    for k, edge in enumerate(seconds):
        turn_patches(peaks, i, slice(None), edge, turned, k * (wide // PATCH))

    @pl.when(has_boundary)
    def _():
        flow[...] = before[...] + boundary_flow(
            i, patch_rows, turned, turned_mid, bands, peak, whole, smooth, acc
        )

    for copy in copies:
        copy.wait()


def window_kernel(second, cols, turned_mid, turned_edge, bands, peak, old_mid, smooth, before, *rest):
    old_edges, (out_ref, acc) = rest[:-2], rest[-2:]
    patch_rows = old_mid.shape[0] // MARGIN
    out_ref[...] = before[...]
    odd = lax.axis_index("gz") % 2 == 1

    @pl.when(lax.axis_index("gz") != 0)
    def _():
        i = edge_patch_row(second, patch_rows)
        at_mid = pl.multiple_of(i * MARGIN, MARGIN)

        def old_of(j):
            here = slice((j - cols[0]) * PATCH, (j - cols[0] + 1) * PATCH)
            there = slice(j * PATCH, (j + 1) * PATCH)
            old_edge = old_edges[0][:, here]
            for other in old_edges[1:]:
                old_edge = jnp.where(odd, other[:, here], old_edge)
            return jnp.concatenate([old_edge, old_mid[pl.ds(at_mid, MARGIN), there]], axis=0)

        lines = patch_row_flow(i, cols, turned_edge, turned_mid, bands, peak, smooth, old_of, acc)
        out_ref[...] = before[...] + put_lines(lines, i, patch_rows)


def fill_row_weights(n_ty, swaps, patch_rows, out_ref):
    all_rows = n_ty * patch_rows
    tile = lax.axis_index("ty")
    held = 2 * patch_rows
    depth = LANES
    at = lax.broadcasted_iota(jnp.int32, (8, depth), 0)
    slot = lax.broadcasted_iota(jnp.int32, (8, depth), 1)
    holder = jnp.full((8, depth), tile, jnp.int32)
    even_chip = (lax.axis_index("gz") // 2) % 2 == 0
    for k, (step, other) in enumerate(swaps):
        partner = jnp.where(even_chip, partner_of(tile, *step), partner_of(tile, *other))
        holder = jnp.where((slot >> 3) == k + 1, partner, holder)
    inner = slot & 7
    c_out = (at >= patch_rows).astype(jnp.int32)
    c_in = (inner >= patch_rows).astype(jnp.int32)
    row = tile * patch_rows + at - c_out * patch_rows
    source = holder * patch_rows + inner - c_in * patch_rows

    def inside(r):
        return (r >= 0) & (r < all_rows)

    def tap(delta):
        size = jnp.abs(delta)
        return jnp.where(
            size == 0, TAPS[2], jnp.where(size == 1, TAPS[1], jnp.where(size == 2, TAPS[0], 0.0))
        )

    def norm(r):
        return sum(jnp.where(inside(r + o), TAPS[o + 2], 0.0) for o in range(-2, 3))

    weight = jnp.zeros((8, depth), f32)
    for o in range(-2, 3):
        weight = weight + jnp.where(inside(row + o), TAPS[o + 2] * tap(source - row - o) / norm(row + o), 0.0)
    used = (inner < held) & (at < held) & (c_in == c_out) & inside(source)
    weight = jnp.where(used, weight / norm(row), 0.0)
    for k in range(len(swaps) + 1):
        for b in range(held):
            out_ref[k * held + b] = jnp.broadcast_to(weight[:, 8 * k + b : 8 * k + b + 1], (8, LANES))


def rows_kernel(row_weights, *refs):
    blocks, out_ref = refs[:-1], refs[-1]
    patch_rows, patch_cols = out_ref.shape[2], out_ref.shape[3]
    held = 2 * patch_rows
    result = None
    for k, block in enumerate(blocks):
        for b in range(held):
            term = row_weights[k * held + b] * block[b : b + 1, :]
            result = term if result is None else result + term
    for c in range(2):
        out_ref[c, 0] = result[c * patch_rows : (c + 1) * patch_rows, :patch_cols]


def column_smoother(n):
    kernel = np.zeros((n, n))
    for i in range(n):
        for o in range(-2, 3):
            if 0 <= i + o < n:
                kernel[i, i + o] = TAPS[o + 2]
    kernel = kernel / kernel.sum(1, keepdims=True)
    table = np.zeros((n, LANES), np.float32)
    table[:, :n] = np.linalg.matrix_power(kernel, SMOOTH_PASSES).T
    return table


def call(body, out_shape, in_specs, out_specs, scratch=(), flops=0, moved=0):
    return pl.pallas_call(
        body,
        out_shape=out_shape,
        in_specs=in_specs,
        out_specs=out_specs,
        scratch_shapes=scratch,
        compiler_params=pltpu.CompilerParams(vmem_limit_bytes=VMEM_LIMIT),
        cost_estimate=pl.CostEstimate(flops=flops, bytes_accessed=moved, transcendentals=0),
    )


def in_hbm(x):
    return pltpu.with_memory_space_constraint(x, pltpu.HBM)


def local(sections, boundary, row_shift, row_frac, col_shift, col_frac, peak_shift):
    section = sections[0]
    n_rows, n_cols = section.shape
    n_ty, n_gz, n_parts = lax.axis_size("ty"), lax.axis_size("gz"), lax.axis_size("parts")
    patch_rows, patch_cols = n_rows // PATCH, n_cols // PATCH
    n_patches = patch_rows * patch_cols
    all_rows = n_rows * n_ty
    n_mid, half = n_rows - 2 * MARGIN, n_rows // 2
    n_blocks = n_cols // BLOCK
    vmem = pl.BlockSpec(memory_space=pltpu.VMEM)
    smem = pl.BlockSpec(memory_space=pltpu.SMEM)
    hbm = pl.BlockSpec(memory_space=pltpu.HBM)
    unread = pl.BlockSpec(memory_space=pl.ANY)
    shape = jax.ShapeDtypeStruct
    to_next = [(i, (i + 1) % n_gz) for i in range(n_gz)]

    reach = -(-2 * SMOOTH_PASSES // patch_rows)
    far = [(d, other) for d in range(reach, 1, -1) for other in (False, True)]
    swaps = list(zip([(1, False), *far, (1, True)], [(1, True), *far, (1, False)]))
    swaps = [steps for steps in swaps if any(has_partners(n_ty, *step) for step in steps)]
    routes = [swap_table(n_gz, n_ty, steps) for steps in swaps]

    early = max(1, min(n_blocks - 1, int(n_blocks * EARLY_BLOCKS)))
    window = BLOCK + 2 * LANES
    held = section
    send_first, row_pos, col_pos, tables = call(
        functools.partial(fetch_kernel, all_rows),
        (
            shape((MARGIN, n_cols), bf16),
            shape((1, n_rows), f32),
            shape((1, n_cols), f32),
            shape((early, window, BLOCK), bf16),
        ),
        [hbm] * 5,
        [vmem] * 4,
        [
            pltpu.VMEM((1, n_rows), jnp.int32),
            pltpu.VMEM((1, n_rows), jnp.int32),
            pltpu.VMEM((1, n_cols), jnp.int32),
            pltpu.VMEM((1, n_cols), jnp.int32),
            pltpu.SemaphoreType.DMA((5,)),
        ],
        flops=0,
        moved=0,
    )(*(in_hbm(x) for x in (section, row_shift, row_frac, col_shift, col_frac)))
    first = lax.ppermute(send_first, ("parts", "gz", "ty"), halo_table(n_parts, n_gz, n_ty, False))

    edge_shape = shape((MARGIN, MARGIN + half), bf16)
    mid, more_tables, first_table, second_table = call(
        middle_kernel,
        (shape((n_mid, n_cols), bf16), shape((n_blocks - early, window, BLOCK), bf16), edge_shape, edge_shape),
        [vmem] * 4,
        [vmem] * 4,
        [pltpu.VMEM((n_mid, n_cols + 2 * LANES), bf16)],
    )(held, row_pos, col_pos, tables)
    old_mid = lax.ppermute(mid, "gz", to_next)
    turned_mid = call(
        turn_middle_kernel,
        shape((3 * n_patches, MARGIN, LANES), bf16),
        [smem, vmem],
        vmem,
        flops=1_000_000_000,
        moved=3_000_000,
    )(peak_shift, mid)

    send_second = call(send_kernel, shape((MARGIN, n_cols), bf16), [vmem, unread], vmem, flops=4_000_000_000)(
        held, turned_mid
    )
    second = lax.ppermute(send_second, ("parts", "gz", "ty"), halo_table(n_parts, n_gz, n_ty, True))
    def render_edges(which, parts, *args):
        return call(
            functools.partial(edges_kernel, which, parts),
            [shape((MARGIN, n_cols // parts), bf16)] * parts,
            [vmem] * 5 + [unread] * (len(args) - 5),
            [vmem] * parts,
            [pltpu.VMEM((MARGIN, n_cols + 2 * LANES), bf16)],
        )(*args)

    turned_shape = shape((3 * patch_cols, MARGIN, LANES), bf16)
    (first_edge,) = render_edges(False, 1, first, held, first_table, tables, more_tables, send_second)
    old_first = lax.ppermute(first_edge, "gz", to_next)
    smooth = jnp.asarray(column_smoother(patch_cols))
    acc = pltpu.VMEM((9 * patch_cols * 8, LANES), f32)
    line_shape = shape((8, LANES), f32)
    turned_first, bands, peak, row_weights, payload, old_boundary = call(
        functools.partial(first_waiting_kernel, n_ty, tuple(swaps)),
        (
            turned_shape,
            shape((n_patches, PATCH // 8, LANES), f32),
            shape((2, n_patches, LANES), f32),
            shape(((len(swaps) + 1) * 2 * patch_rows, 8, LANES), f32),
            line_shape,
            shape((n_rows, n_cols), bf16),
        ),
        [smem, vmem, vmem, hbm, vmem],
        [vmem] * 6,
        [acc, pltpu.SemaphoreType.DMA],
        flops=500_000_000,
        moved=1_000_000,
    )(peak_shift, first_edge, turned_mid, in_hbm(boundary), smooth)
    second_edges = render_edges(True, EDGE_PARTS, second, held, second_table, tables, more_tables, turned_first)
    part_cols = patch_cols // EDGE_PARTS
    old_seconds = [[lax.ppermute(e, "gz", to_next)] for e in second_edges[:-1]]
    in_chip = [(z, z ^ 1) for z in range(n_gz) if (z ^ 1) < n_gz]
    old_seconds.append(
        [
            lax.ppermute(second_edges[-1], ("parts", "gz"), next_chip_table(n_parts, n_gz)),
            lax.ppermute(second_edges[-1], "gz", in_chip),
        ]
    )
    rendered, turned_second, payload = call(
        waiting_kernel,
        (shape((n_rows, n_cols), bf16), turned_shape, line_shape),
        [smem] + [vmem] * (8 + EDGE_PARTS) + [unread],
        [hbm] + [vmem] * 2,
        [acc, pltpu.SemaphoreType.DMA((2 + EDGE_PARTS,))],
        flops=1_000_000_000,
        moved=3_000_000,
    )(
        peak_shift,
        mid,
        first_edge,
        *second_edges,
        turned_mid,
        bands,
        peak,
        old_boundary,
        smooth,
        payload,
        old_mid,
    )
    windows = [(True, range(patch_cols), turned_second, [old_first])]
    for k, old in enumerate(old_seconds):
        windows.append((False, range(k * part_cols, (k + 1) * part_cols), turned_first, old))
    for which, cols, turned, old in windows:
        payload = call(
            functools.partial(window_kernel, which, cols), line_shape, [vmem] * (7 + len(old)), vmem, [acc]
        )(turned_mid, turned, bands, peak, old_mid, smooth, payload, *old)
    blocks = [payload] + [lax.ppermute(payload, ("gz", "ty"), route) for route in routes]
    flow = call(
        rows_kernel, shape((2, 1, patch_rows, patch_cols), f32), [vmem] * (1 + len(blocks)), vmem
    )(row_weights, *blocks)
    return rendered[None], flow


def solution(mesh):
    in_specs = (
        P(("parts", "gz"), "ty", None),
        P(("parts", "ty"), None),
        P(("parts", "gz"), "ty"),
        P(("parts", "gz"), "ty"),
        P(("parts", "gz"), None),
        P(("parts", "gz"), None),
        P(None, ("parts", "gz"), "ty", None),
    )
    out_specs = (P(("parts", "gz"), "ty", None), P(None, ("parts", "gz"), "ty", None))
    return jax.shard_map(local, mesh=mesh, in_specs=in_specs, out_specs=out_specs, check_vma=False)
```
